32 devices in a mesh: fsdp: 8 (over y, x, core), dp: 4 (over z).
Axes of the slice: x: 2, y: 2, z: 4, core: 2. Of those that a mesh axis runs over, the one named last changes fastest.
Arguments:
- target: bfloat16 [32, 1024, 768], P(('fsdp', 'dp')), may hold values from -6 to 6
- memory: bfloat16 [32, 1024, 768], P(('fsdp', 'dp')), may hold values from -6 to 6
- target_lengths: int32 [32], P(('fsdp', 'dp')), may hold values from 256 to 1024, as said below
- memory_lengths: int32 [32], P(('fsdp', 'dp')), may hold values from 256 to 1024, as said below
- self_qkv: bfloat16 [3, 768, 768], P(None, 'fsdp'), may hold values from -0.21875 to 0.21875
- self_bias: bfloat16 [3, 768], P(None, 'fsdp'), may hold values from -3 to 3
- self_out: bfloat16 [768, 768], P('fsdp'), may hold values from -0.875 to 0.875
- cross_qkv: bfloat16 [3, 768, 768], P(None, 'fsdp'), may hold values from -0.21875 to 0.21875
- cross_bias: bfloat16 [3, 768], P(None, 'fsdp'), may hold values from -3 to 3
- cross_out: bfloat16 [768, 768], P('fsdp'), may hold values from -0.875 to 0.875
- ffn_in: bfloat16 [768, 3072], P('fsdp'), may hold values from -0.21875 to 0.21875
- ffn_in_bias: bfloat16 [3072], P('fsdp'), may hold values from -3 to 3
- ffn_out: bfloat16 [3072, 768], P('fsdp'), may hold values from -0.109375 to 0.109375
- ffn_out_bias: bfloat16 [768], P('fsdp'), may hold values from -3 to 3
- norm_gain: bfloat16 [3, 768], P(None, 'fsdp'), may hold values from 0.5 to 1.5
- norm_bias: bfloat16 [3, 768], P(None, 'fsdp'), may hold values from -3 to 3
- cotangent: bfloat16 [32, 1024, 768], P(('fsdp', 'dp')), may hold values from -6 to 6
Outputs:
- mixed: bfloat16 [32, 1024, 768], P(('fsdp', 'dp'))
- target_grad: float32 [32, 1024, 768], P(('fsdp', 'dp'))
- memory_grad: float32 [32, 1024, 768], P(('fsdp', 'dp'))
- self_qkv_grad: float32 [3, 768, 768], P(None, 'fsdp')
- self_bias_grad: float32 [3, 768], P(None, 'fsdp')
- self_out_grad: float32 [768, 768], P('fsdp')
- cross_qkv_grad: float32 [3, 768, 768], P(None, 'fsdp')
- cross_bias_grad: float32 [3, 768], P(None, 'fsdp')
- cross_out_grad: float32 [768, 768], P('fsdp')
- ffn_in_grad: float32 [768, 3072], P('fsdp')
- ffn_in_bias_grad: float32 [3072], P('fsdp')
- ffn_out_grad: float32 [3072, 768], P('fsdp')
- ffn_out_bias_grad: float32 [768], P('fsdp')
- norm_gain_grad: float32 [3, 768], P(None, 'fsdp')
- norm_bias_grad: float32 [3, 768], P(None, 'fsdp')
The draws below stay inside these ranges and needn't reach their ends.
Inputs may be any that keep to these rules, and one draw needn't show every extreme that they name: `target_lengths`: real target tokens of each row; some row has all 1024. Queries past a row's length still produce outputs. `memory_lengths`: real memory tokens of each row; some row has all 1024.
All inputs are finite; a program needn't handle non-finite values.
Results may differ from the reference program's by a relative error of at most 0.025.
Values may be sent and summed in bfloat16 or wider, within the bound.
No kernel may reach another device: no remote copies, remote signals or barrier semaphores. Data moves between devices by JAX's collectives and lax.ppermute only.
A program may use at most 448 MiB of HBM per device.

```python
import jax
import jax.numpy as jnp
from jax import lax

D = 768
HEADS = 12
HDIM = 64
FF = 3072
LEN = 1024
MLEN = 1024
ROWS = 32


def draw_target_lengths(key, part):
    key = jax.random.fold_in(key, 11)
    key_len, key_top = jax.random.split(key)
    lengths = jax.random.randint(key_len, (ROWS,), LEN // 4, LEN + 1, dtype=jnp.int32)
    longest = jax.random.randint(key_top, (), 0, ROWS, dtype=jnp.int32)
    return jnp.where(jnp.arange(ROWS, dtype=jnp.int32) == longest, LEN, lengths).astype(jnp.int32)


def draw_memory_lengths(key, part):
    key = jax.random.fold_in(key, 23)
    key_len, key_top = jax.random.split(key)
    lengths = jax.random.randint(key_len, (ROWS,), MLEN // 4, MLEN + 1, dtype=jnp.int32)
    longest = jax.random.randint(key_top, (), 0, ROWS, dtype=jnp.int32)
    return jnp.where(jnp.arange(ROWS, dtype=jnp.int32) == longest, MLEN, lengths).astype(jnp.int32)


def spiked(entries, stream_key, source, target, blocks, factor):
    def block_of(dim):
        return (jnp.arange(entries.shape[dim]) // (entries.shape[dim] // blocks)).reshape((-1,) + (1,) * (entries.ndim - 1 - dim))

    one_side = jax.random.permutation(stream_key, blocks)[block_of(target)]
    second = (block_of(target) + blocks // 2) % blocks
    return jnp.where((block_of(source) == one_side) | (block_of(source) == second), factor * entries, entries)


def level_of(key, dims, cuts, smallest, high):
    level = 1.0
    for dim, shards_of in cuts:
        heights = jax.random.uniform(jax.random.fold_in(jax.random.fold_in(key, 6), dim), (shards_of,), jnp.float32, smallest / len(cuts), high / len(cuts))
        level = level * jnp.repeat(jnp.exp(heights), dims[dim] // shards_of).reshape((-1,) + (1,) * (len(dims) - 1 - dim))
    return level


def bell_draw(key, extent, deviation, limit, pieces=(), held_as=jnp.bfloat16):
    result = deviation * jax.random.normal(key, extent, jnp.float32)
    if pieces:
        result = result * level_of(key, extent, pieces, -0.22, 0.18)
    return jnp.clip(result, -limit, limit).astype(held_as)


def gaussian_with(key, dims, width, limit, pieces, heavy, kind=jnp.bfloat16):
    array = width * jax.random.normal(key, dims, jnp.float32)
    if pieces:
        array = array * level_of(key, dims, pieces, -0.22, 0.18)
    return jnp.clip(spiked(array, jax.random.fold_in(key, 3), *heavy), -limit, limit).astype(kind)


def setup_inputs(seed: int = 0) -> dict:
    key_of = jax.random.split(jax.random.key(seed), 18)
    return {
        "target": bell_draw(key_of[0], (ROWS, LEN, D), 1.0, 6.0, ((0, 32),)),
        "memory": bell_draw(key_of[1], (ROWS, MLEN, D), 1.0, 6.0, ((0, 32),)),
        "target_lengths": draw_target_lengths(jax.random.fold_in(key_of[17], 71), 0),
        "memory_lengths": draw_memory_lengths(jax.random.fold_in(key_of[17], 71), 0),
        "self_qkv": bell_draw(key_of[4], (3, D, D), D ** -0.5, 0.21875, ((1, 8),)),
        "self_bias": bell_draw(key_of[5], (3, D), 0.5, 3.0, ((1, 8),)),
        "self_out": bell_draw(key_of[6], (D, D), (D // 16) ** -0.5, 0.875, ((0, 8),)),
        "cross_qkv": bell_draw(key_of[7], (3, D, D), D ** -0.5, 0.21875, ((1, 8),)),
        "cross_bias": bell_draw(key_of[8], (3, D), 0.5, 3.0, ((1, 8),)),
        "cross_out": bell_draw(key_of[9], (D, D), (D // 16) ** -0.5, 0.875, ((0, 8),)),
        "ffn_in": bell_draw(key_of[10], (D, FF), D ** -0.5, 0.21875, ((0, 8),)),
        "ffn_in_bias": bell_draw(key_of[11], (FF,), 0.5, 3.0, ((0, 8),)),
        "ffn_out": bell_draw(key_of[12], (FF, D), FF ** -0.5, 0.109375, ((0, 8),)),
        "ffn_out_bias": bell_draw(key_of[13], (D,), 0.5, 3.0, ((0, 8),)),
        "norm_gain": jnp.clip(1.0 + 0.1 * jax.random.normal(key_of[14], (3, D), jnp.float32), 0.5, 1.5).astype(jnp.bfloat16),
        "norm_bias": bell_draw(key_of[15], (3, D), 0.5, 3.0, ((1, 8),)),
        "cotangent": gaussian_with(key_of[16], (ROWS, LEN, D), 1.0, 6.0, ((0, 32),), (0, 2, 32, 2.75)),
    }


@jax.custom_vjp
def low(v):
    return lax.optimization_barrier(v.astype(jnp.bfloat16)).astype(jnp.float32)

@jax.custom_vjp
def low_back(v):
    return v

def low_keep(v):
    return (low(v), None)

def low_pass(kept, grad):
    return (grad,)

def back_keep(v):
    return (v, None)

def back_low(kept, grad):
    return (low(grad),)
low.defvjp(low_keep, low_pass)
low_back.defvjp(back_keep, back_low)

def product(left, right):
    return jnp.dot(left, right, precision=lax.Precision.HIGHEST)

def layer_norm(summed, gain, shift):
    centred = summed - lax.optimization_barrier(jnp.mean(summed, axis=-1, keepdims=True))
    inverse = lax.rsqrt(lax.optimization_barrier(jnp.mean(centred * centred, axis=-1, keepdims=True)) + 1e-05)
    return centred * inverse * gain + shift

def split_heads(values):
    return values.reshape(values.shape[0], HEADS, HDIM).transpose(1, 0, 2)

def attend(query_in, source, weights, biases, out_weight, allowed):
    query_count = query_in.shape[0]
    factor = HDIM ** (-0.5)
    queries = low_back(low((product(query_in, weights[0]) + biases[0]) * factor))
    keys_all = low_back(low(product(source, weights[1])))
    values_all = low_back(low(product(source, weights[2]) + biases[1]))
    scores = jnp.einsum('hqd,hkd->hqk', split_heads(queries), split_heads(keys_all), precision=lax.Precision.HIGHEST)
    scores = low_back(jnp.where(allowed[None], scores, -1000000000.0))
    highest = lax.optimization_barrier(jnp.max(scores, axis=-1, keepdims=True))
    expo = jnp.exp(scores - highest)
    probs = low(expo / lax.optimization_barrier(jnp.sum(expo, axis=-1, keepdims=True)))
    mixed = jnp.einsum('hqk,hkd->hqd', probs, split_heads(values_all), precision=lax.Precision.HIGHEST)
    mixed = low_back(low(mixed.transpose(1, 0, 2).reshape(query_count, HEADS * HDIM)))
    return low_back(product(mixed, out_weight) + biases[2])

def layer_row(params, target_row, memory_row, target_len, memory_len):
    self_qkv, self_bias, self_out, cross_qkv, cross_bias, cross_out, ffn_in, ffn_in_bias, ffn_out, ffn_out_bias, norm_gain, norm_bias = params
    positions = jnp.arange(target_row.shape[0], dtype=jnp.int32)
    sources = jnp.arange(memory_row.shape[0], dtype=jnp.int32)
    self_allowed = (positions[None, :] <= positions[:, None]) & (positions[None, :] < target_len)
    cross_allowed = jnp.broadcast_to(sources[None, :] < memory_len, (positions.shape[0], sources.shape[0]))
    hidden_one = layer_norm(target_row + attend(target_row, target_row, self_qkv, self_bias, self_out, self_allowed), norm_gain[0], norm_bias[0])
    hidden_two = layer_norm(hidden_one + attend(low(hidden_one), memory_row, cross_qkv, cross_bias, cross_out, cross_allowed), norm_gain[1], norm_bias[1])
    pre_act = low_back(product(low(hidden_two), ffn_in) + ffn_in_bias)
    activ = low(jax.nn.gelu(pre_act, approximate=False))
    branch = low_back(product(activ, ffn_out) + ffn_out_bias)
    return layer_norm(hidden_two + branch, norm_gain[2], norm_bias[2])

def reference(target, memory, target_lengths, memory_lengths, self_qkv, self_bias, self_out, cross_qkv, cross_bias, cross_out, ffn_in, ffn_in_bias, ffn_out, ffn_out_bias, norm_gain, norm_bias, cotangent):
    params = tuple((member.astype(jnp.float32) for member in (self_qkv, self_bias, self_out, cross_qkv, cross_bias, cross_out, ffn_in, ffn_in_bias, ffn_out, ffn_out_bias, norm_gain, norm_bias)))

    def forward(weights, target_f, memory_f):

        def one_row(packed):
            return layer_row(weights, packed[0], packed[1], packed[2], packed[3])
        return lax.map(jax.checkpoint(one_row), (target_f, memory_f, target_lengths, memory_lengths))
    output, pullback = jax.vjp(forward, params, target.astype(jnp.float32), memory.astype(jnp.float32))
    grad_params, grad_target, grad_memory = pullback(cotangent.astype(jnp.float32))
    return (output.astype(jnp.bfloat16), grad_target, grad_memory, grad_params[0], grad_params[1], grad_params[2], grad_params[3], grad_params[4], grad_params[5], grad_params[6], grad_params[7], grad_params[8], grad_params[9], grad_params[10], grad_params[11])
```

```python
import jax
import jax.numpy as jnp
from jax import lax
from jax.experimental import pallas as pl
from jax.experimental.pallas import tpu as pltpu
from jax.sharding import PartitionSpec as P

HDIM = 64
PAIR = 2 * HDIM
BLOCK = 256
ROWS = 256
MASKED = -1e30
FACTOR = HDIM ** (-0.5)
BF = jnp.bfloat16
F32 = jnp.float32


def dot_nn(a, b):
    return lax.dot_general(a, b, (((1,), (0,)), ((), ())), preferred_element_type=F32)


def dot_nt(a, b):
    return lax.dot_general(a, b, (((1,), (1,)), ((), ())), preferred_element_type=F32)


def dot_tn(a, b):
    return lax.dot_general(a, b, (((0,), (0,)), ((), ())), preferred_element_type=F32)


def column_sum(values):
    return jnp.sum(values.astype(F32), axis=0, keepdims=True)


def head_lanes(head):
    lane = lax.broadcasted_iota(jnp.int32, (1, PAIR), 1)
    return (lane // HDIM) == head, lane == (HDIM if head == 0 else 0)


def pick(mask, yes, no, shape):
    return jnp.where(jnp.broadcast_to(mask, shape), yes, no)


def length_bias(count, limit):
    positions = lax.broadcasted_iota(jnp.int32, (count, PAIR), 0)
    return jnp.where(positions < limit, 0.0, MASKED).astype(F32)


def causal_edge(values, fill):
    key_at = lax.broadcasted_iota(jnp.int32, values.shape, 0)
    query_at = lax.broadcasted_iota(jnp.int32, values.shape, 1)
    return jnp.where(key_at <= query_at, values, fill)


def attend_forward_kernel(causal, limit_ref, q_ref, k_ref, v_ref, o_ref, lse_ref):
    count, sources = q_ref.shape[0], k_ref.shape[0]
    k_all, v_all = k_ref[...].astype(F32), v_ref[...].astype(F32)
    bias = length_bias(sources, limit_ref[0])
    keys, values = [], []
    for head in range(2):
        own, spare = head_lanes(head)
        keys.append(pick(spare, bias, k_all, k_all.shape).astype(BF))
        ones = pick(spare, 1.0, 0.0, v_all.shape)
        values.append(pick(own, v_all, ones, v_all.shape).T.astype(BF))

    def scores_of(unit):
        block, head = unit
        rows = slice(block * BLOCK, (block + 1) * BLOCK)
        extent = (block + 1) * BLOCK if causal else sources
        own, spare = head_lanes(head)
        q_block = q_ref[rows, :].astype(F32)
        ones = pick(spare, 1.0, 0.0, q_block.shape)
        scores = dot_nt(keys[head][:extent], pick(own, q_block, ones, q_block.shape).astype(BF))
        if causal:
            edge = causal_edge(scores[extent - BLOCK:], MASKED)
            scores = edge if extent == BLOCK else jnp.concatenate([scores[: extent - BLOCK], edge], axis=0)
        return scores

    parts = {}

    def finish(unit, expo, highest):
        block, head = unit
        rows = slice(block * BLOCK, (block + 1) * BLOCK)
        mixed = dot_nn(values[head][:, : expo.shape[0]], expo)
        at = HDIM if head == 0 else 0
        total = mixed[at:at + 1]
        lse_ref[0, head:head + 1, rows] = highest + jnp.log(total)
        parts[unit] = mixed[head * HDIM:(head + 1) * HDIM] * (1.0 / total)
        if head == 1:
            o_ref[rows, :] = jnp.concatenate([parts[(block, 0)], parts[unit]], axis=0).T.astype(BF)

    units = [(block, head) for block in range(count // BLOCK) for head in range(2)]
    ahead = [scores_of(unit) for unit in units[:2]]
    before = None
    for at, unit in enumerate(units):
        if at + 2 < len(units):
            ahead.append(scores_of(units[at + 2]))
        highest = jnp.max(ahead[at], axis=0, keepdims=True)
        expo = jnp.exp(ahead[at] - highest).astype(BF)
        if before is not None:
            finish(*before)
        before = (unit, expo, highest)
    finish(*before)


def attend_backward_kernel(
    causal, limit_ref, q_ref, k_ref, v_ref, o_ref, do_ref, lse_ref, dq_ref, dk_ref, dv_ref, sums_ref, dq_acc
):
    count, sources = q_ref.shape[0], k_ref.shape[0]
    q_all, k_all = q_ref[...].astype(F32), k_ref[...].astype(F32)
    do_all = do_ref[...].astype(F32)
    bias = length_bias(sources, limit_ref[0])
    product = (do_all * o_ref[...].astype(F32)).T
    q_aug, q_own, k_aug, kt_own, do_own, delta, lse = [], [], [], [], [], [], []
    for head in range(2):
        own, spare = head_lanes(head)
        q_aug.append(pick(own, q_all, pick(spare, 1.0, 0.0, q_all.shape), q_all.shape).astype(BF))
        q_own.append(pick(own, q_all, 0.0, q_all.shape).astype(BF))
        k_aug.append(pick(spare, bias, k_all, k_all.shape).astype(BF))
        kt_own.append(pick(own, k_all, 0.0, k_all.shape).T.astype(BF))
        do_own.append(pick(own, do_all, 0.0, do_all.shape).astype(BF))
        delta.append(jnp.sum(product[head * HDIM:(head + 1) * HDIM], axis=0, keepdims=True))
        lse.append(lse_ref[0, head:head + 1, :])

    def products(unit):
        block, head = unit
        rows = slice(block * BLOCK, (block + 1) * BLOCK)
        first = block * BLOCK if causal else 0
        return (
            dot_nt(k_aug[head][rows], q_aug[head][first:]),
            dot_nt(v_ref[rows, :], do_own[head][first:]),
        )

    def gradients(unit, scores, d_probs):
        block, head = unit
        first = block * BLOCK if causal else 0
        probs = jnp.exp(scores - lse[head][:, first:])
        if causal:
            edge = causal_edge(probs[:, :BLOCK], 0.0)
            probs = edge if first + BLOCK == count else jnp.concatenate([edge, probs[:, BLOCK:]], axis=1)
        d_scores = (probs * (d_probs - delta[head][:, first:])).astype(BF)
        return probs.astype(BF), d_scores

    held = {}

    def finish(unit, probs, d_scores):
        block, head = unit
        rows = slice(block * BLOCK, (block + 1) * BLOCK)
        first = block * BLOCK if causal else 0
        dv = dot_nn(probs, do_own[head][first:])
        dk = dot_nn(d_scores, q_own[head][first:])
        dq = dot_nn(kt_own[head][:, rows], d_scores)
        if head == 0:
            held[block] = (dv, dk, dq)
            return
        dv = (held[block][0] + dv).astype(BF)
        dv_ref[rows, :] = dv
        held["dv"] = held.get("dv", 0.0) + column_sum(dv)
        dk_ref[rows, :] = (held[block][1] + dk).astype(BF)
        if block == 0:
            dq_acc[...] = held[block][2] + dq
        else:
            dq_acc[:, first:] += held[block][2] + dq

    units = [(block, head) for block in range(sources // BLOCK) for head in range(2)]
    ahead = [products(units[0])]
    before = None
    for at, unit in enumerate(units):
        if at + 1 < len(units):
            ahead.append(products(units[at + 1]))
        current = (unit,) + gradients(unit, *ahead[at])
        if before is not None:
            finish(*before)
        before = current
    finish(*before)
    dq = dq_acc[...].T.astype(BF)
    dq_ref[...] = dq
    sums_ref[...] = jnp.concatenate([column_sum(dq) * FACTOR, held["dv"], jnp.zeros((6, PAIR), F32)], axis=0)


def attend_forward(q, k, v, limit, causal):
    count, width = q.shape
    sources = k.shape[0]
    pairs = width // PAIR
    of_q = pl.BlockSpec((count, PAIR), lambda i: (0, i))
    of_k = pl.BlockSpec((sources, PAIR), lambda i: (0, i))
    work = 16 * count * sources * width * (5 if causal else 8) // 8
    return pl.pallas_call(
        lambda *refs: attend_forward_kernel(causal, *refs),
        grid=(pairs,),
        in_specs=[pl.BlockSpec(memory_space=pltpu.SMEM), of_q, of_k, of_k],
        out_specs=[of_q, pl.BlockSpec((1, 2, count), lambda i: (i, 0, 0))],
        out_shape=[
            jax.ShapeDtypeStruct((count, width), BF),
            jax.ShapeDtypeStruct((pairs, 2, count), F32),
        ],
        compiler_params=pltpu.CompilerParams(vmem_limit_bytes=40 << 20),
        cost_estimate=pl.CostEstimate(flops=work, bytes_accessed=8 * count * width, transcendentals=0),
        name="attend_forward",
    )(limit, q, k, v)


def attend_backward(q, k, v, o, do, lse, limit, causal):
    count, width = q.shape
    sources = k.shape[0]
    pairs = width // PAIR
    of_q = pl.BlockSpec((count, PAIR), lambda i: (0, i))
    of_k = pl.BlockSpec((sources, PAIR), lambda i: (0, i))
    work = 40 * count * sources * width * (5 if causal else 8) // 8
    return pl.pallas_call(
        lambda *refs: attend_backward_kernel(causal, *refs),
        grid=(pairs,),
        in_specs=[
            pl.BlockSpec(memory_space=pltpu.SMEM),
            of_q,
            of_k,
            of_k,
            of_q,
            of_q,
            pl.BlockSpec((1, 2, count), lambda i: (i, 0, 0)),
        ],
        out_specs=[of_q, of_k, of_k, pl.BlockSpec((8, PAIR), lambda i: (0, i))],
        out_shape=[
            jax.ShapeDtypeStruct((count, width), BF),
            jax.ShapeDtypeStruct((sources, width), BF),
            jax.ShapeDtypeStruct((sources, width), BF),
            jax.ShapeDtypeStruct((8, width), F32),
        ],
        scratch_shapes=[pltpu.VMEM((PAIR, count), F32)],
        compiler_params=pltpu.CompilerParams(vmem_limit_bytes=40 << 20),
        cost_estimate=pl.CostEstimate(flops=work, bytes_accessed=16 * count * width, transcendentals=0),
        name="attend_backward",
    )(limit, q, k, v, o, do, lse)


WHOLE = pl.BlockSpec(memory_space=pltpu.VMEM)
ANYWHERE = pl.BlockSpec(memory_space=pl.ANY)
SCALAR = pl.BlockSpec(memory_space=pltpu.SMEM)
SLAB = 16


def params(limit=48):
    return pltpu.CompilerParams(vmem_limit_bytes=limit << 20)


def cost(flops, *arrays):
    size = sum(a.size * a.dtype.itemsize for a in arrays)
    return pl.CostEstimate(flops=flops, bytes_accessed=size, transcendentals=0)


def of(*shape, dtype=BF):
    return jax.ShapeDtypeStruct(shape, dtype)


def matrix(bundle, index):
    owners, width = bundle.shape[0], bundle.shape[2]
    part = width // owners
    return bundle[:, index * part:(index + 1) * part, :].reshape(width, width)


def fetch(me, pieces, bundle, sem, first):
    copies = []
    for at, ((relative, offset, rows), piece) in enumerate(pieces):
        owner = jnp.bitwise_xor(me, relative)
        if len(bundle.shape) == 3:
            target = bundle.at[owner, pl.ds(offset, rows)]
        else:
            target = bundle.at[pl.ds(pl.multiple_of(owner * rows, 16), rows)]
        copies.append(pltpu.make_async_copy(piece, target, sem.at[first + at]))
        copies[-1].start()
    return copies


def wait_all(copies):
    for copy in copies:
        copy.wait()


def at_first(action):
    pl.when(pl.program_id(0) == 0)(action)


def normalise(summed):
    centred = summed - jnp.mean(summed, axis=-1, keepdims=True)
    inverse = lax.rsqrt(jnp.mean(centred * centred, axis=-1, keepdims=True) + 1e-05)
    return centred * inverse, inverse


def norm_backward(d_out, normed, inverse, gain):
    d_normed = d_out * gain
    return inverse * (
        d_normed
        - jnp.mean(d_normed, axis=-1, keepdims=True)
        - normed * jnp.mean(d_normed * normed, axis=-1, keepdims=True)
    )


def gelu_parts(a):
    bell = jnp.exp(-0.5 * a * a)
    t = 1.0 / (1.0 + 0.23164189 * jnp.abs(a))
    tail = t * (0.127414796 + t * (-0.142248368 + t * (0.7107068705 + t * (-0.7265760135 + t * 0.5307027145)))) * bell
    phi = jnp.where(a >= 0.0, 1.0 - tail, tail)
    return a * phi, phi + a * bell * 0.3989422804014327


def add_rows(ref, rows):
    block = jnp.concatenate(rows + [jnp.zeros((ref.shape[0] - len(rows), ref.shape[1]), F32)], axis=0)

    @pl.when(pl.program_id(0) == 0)
    def _():
        ref[...] = block

    @pl.when(pl.program_id(0) > 0)
    def _():
        ref[...] += block


def pack_kernel(counts, *refs):
    matrices, vectors, out, hold = refs[:counts], refs[counts:-2], refs[-2], refs[-1]
    at = 0
    for ref in matrices:
        out[at:at + ref.shape[0], :] = ref[...]
        at += ref.shape[0]
    hold[...] = jnp.zeros(hold.shape, F32)
    row = 0
    for ref in vectors:
        hold[row:row + ref.shape[0], : ref.shape[1]] = ref[...].astype(F32)
        row += ref.shape[0]
    out[at:, :] = hold[...].astype(BF)


def pack(matrices, vectors, name):
    width = matrices[0].shape[1]
    rows = sum(m.shape[0] for m in matrices) + SLAB
    return pl.pallas_call(
        lambda *refs: pack_kernel(len(matrices), *refs),
        in_specs=[WHOLE] * (len(matrices) + len(vectors)),
        out_specs=WHOLE,
        out_shape=of(rows, width),
        scratch_shapes=[pltpu.VMEM((SLAB, width), F32)],
        compiler_params=params(),
        name=name,
    )(*matrices, *vectors)


def project_kernel(layout, me_ref, x, *refs):
    pieces, (w, vec, q_ref, k_ref, v_ref, sem) = refs[: len(layout)], refs[len(layout):]
    owners, width = w.shape[0], w.shape[2]
    part = width // owners

    @at_first
    def _():
        wait_all(fetch(me_ref[0], list(zip(layout, pieces)), w, sem, 0))
        vec[...] = jnp.zeros(vec.shape, F32)
        for owner in range(owners):
            slab = w[owner, 3 * part:, :].astype(F32)
            vec[:12, owner * part:(owner + 1) * part] = slab[:12, :part]
            for row in range(4):
                at = (owner * 4 + row) * part
                vec[12 + at // width:13 + at // width, at % width:at % width + part] = slab[12 + row:13 + row, :part]

    values = x[...]
    q_ref[...] = ((dot_nn(values, matrix(w, 0)) + vec[0:1, :]) * FACTOR).astype(BF)
    k_ref[...] = dot_nn(values, matrix(w, 1)).astype(BF)
    v_ref[...] = (dot_nn(values, matrix(w, 2)) + vec[1:2, :]).astype(BF)


def project(me, x, pieces, owners):
    count, width = x.shape
    rows = pl.BlockSpec((ROWS, width), lambda i: (i, 0))
    layout = [key for key, _ in pieces]
    return pl.pallas_call(
        lambda *refs: project_kernel(layout, *refs),
        grid=(count // ROWS,),
        in_specs=[SCALAR, rows] + [ANYWHERE] * len(pieces),
        out_specs=[WHOLE, WHOLE, rows, rows, rows],
        out_shape=[of(owners, 3 * width // owners + SLAB, width), of(16, width, dtype=F32)] + [of(count, width)] * 3,
        scratch_shapes=[pltpu.SemaphoreType.DMA((len(pieces),))],
        compiler_params=params(),
        cost_estimate=cost(6 * count * width * width, x, x, x, x, x),
        name="self_project",
    )(me, x, *[piece for _, piece in pieces])


def between_kernel(layouts, me_ref, vec, o, x, mem, *refs):
    count = len(layouts[0])
    ones, twos = refs[:count], refs[count:count + len(layouts[1])]
    w, wo, z_ref, r_ref, h_ref, q_ref, k_ref, v_ref, sem = refs[count + len(layouts[1]):]

    @at_first
    def _():
        copies = fetch(me_ref[0], list(zip(layouts[0], ones)), w, sem, 0)
        copies += fetch(me_ref[0], list(zip(layouts[1], twos)), wo, sem, count)
        wait_all(copies)

    summed = x[...].astype(F32) + dot_nn(o[...], matrix(wo, 0)) + vec[2:3, :]
    source = mem[...]
    k_ref[...] = dot_nn(source, matrix(w, 1)).astype(BF)
    v_ref[...] = (dot_nn(source, matrix(w, 2)) + vec[4:5, :]).astype(BF)
    z, r = normalise(summed)
    z_ref[...] = z
    r_ref[...] = r
    hidden = (z * vec[6:7, :] + vec[9:10, :]).astype(BF)
    h_ref[...] = hidden
    q_ref[...] = ((dot_nn(hidden, matrix(w, 0)) + vec[3:4, :]) * FACTOR).astype(BF)


def between(me, vec, o, x, mem, ones, twos, owners):
    count, width = x.shape
    part = width // owners
    rows = pl.BlockSpec((ROWS, width), lambda i: (i, 0))
    layouts = [key for key, _ in ones], [key for key, _ in twos]
    return pl.pallas_call(
        lambda *refs: between_kernel(layouts, *refs),
        grid=(count // ROWS,),
        in_specs=[SCALAR, WHOLE, rows, rows, rows] + [ANYWHERE] * (len(ones) + len(twos)),
        out_specs=[WHOLE, WHOLE, rows, pl.BlockSpec((ROWS, 1), lambda i: (i, 0))] + [rows] * 4,
        out_shape=[
            of(owners, 3 * part, width), of(owners, 2 * part + SLAB, width), of(count, width, dtype=F32),
            of(count, 1, dtype=F32),
        ] + [of(count, width)] * 4,
        scratch_shapes=[pltpu.SemaphoreType.DMA((len(ones) + len(twos),))],
        compiler_params=params(),
        cost_estimate=cost(8 * count * width * width, x, x, x, x, x, x, x, x, x),
        name="self_out_cross_project",
    )(me, vec, o, x, mem, *[piece for _, piece in ones + twos])


def ffn_kernel(layouts, me_ref, vec, o, z_in, cot, wo, *refs):
    count = len(layouts[0])
    ins, outs = refs[:count], refs[count:count + len(layouts[1])]
    (mixed, act_ref, da_ref, df_ref, h_ref, dy_ref, db_ref, do_ref, sums_ref, w_in, w_out, slope, b_out, sem) = (
        refs[count + len(layouts[1]):]
    )
    width = o.shape[1]
    chunks = w_in.shape[1] // width
    owners = wo.shape[0]
    part = width // owners
    in_copies = list(zip(layouts[0], ins)), list(zip(layouts[1], outs))

    @at_first
    def _():
        copies = fetch(me_ref[0], in_copies[0], w_in, sem, 0) + fetch(me_ref[0], in_copies[1], w_out, sem, count)
        for owner in range(owners):
            b_out[0:1, owner * part:(owner + 1) * part] = wo[owner, 2 * part:, :].astype(F32)[0:1, :part]
        wait_all(copies)

    gains = [vec[6 + i:7 + i, :] for i in range(3)]
    shifts = [vec[9 + i:10 + i, :] for i in range(3)]
    first = z_in[...] * gains[0] + shifts[0]
    z_two, r_two = normalise(first + dot_nn(o[...], matrix(wo, 1)) + vec[5:6, :])
    second = z_two * gains[1] + shifts[1]
    hidden = second.astype(BF)
    h_ref[...] = hidden

    def columns(c):
        return slice(c * width, (c + 1) * width)

    total = second + b_out[0:1, :]
    ahead = dot_nn(hidden, w_in[:, columns(0)])
    before = None
    for c in range(chunks):
        pre = ahead + vec[12 + c:13 + c, :]
        if c + 1 < chunks:
            ahead = dot_nn(hidden, w_in[:, columns(c + 1)])
        act, grad = gelu_parts(pre)
        act = act.astype(BF)
        act_ref[:, columns(c)] = act
        slope[:, columns(c)] = grad
        if before is not None:
            total = total + dot_nn(before, w_out[columns(c - 1), :])
        before = act
    total = total + dot_nn(before, w_out[columns(chunks - 1), :])
    z, r = normalise(total)
    mixed[...] = (z * gains[2] + shifts[2]).astype(BF)
    incoming = cot[...].astype(F32)
    dy_three = norm_backward(incoming, z, r, gains[2])
    df = dy_three.astype(BF)
    df_ref[...] = df
    rows = [column_sum(df), column_sum(incoming * z), column_sum(incoming)]

    da_sums = []
    d_two = dy_three
    ahead = dot_nt(df, w_out[columns(0), :])
    before = None
    for c in range(chunks):
        d_act = ahead
        if c + 1 < chunks:
            ahead = dot_nt(df, w_out[columns(c + 1), :])
        da = (d_act * slope[:, columns(c)]).astype(BF)
        da_ref[:, columns(c)] = da
        da_sums.append(column_sum(da))
        if before is not None:
            d_two = d_two + dot_nt(before, w_in[:, columns(c - 1)])
        before = da
    d_two = d_two + dot_nt(before, w_in[:, columns(chunks - 1)])
    dy_two = norm_backward(d_two, z_two, r_two, gains[1])
    dy_ref[...] = dy_two
    db = dy_two.astype(BF)
    db_ref[...] = db
    do_ref[...] = dot_nt(db, matrix(wo, 1)).astype(BF)
    rows += [column_sum(d_two * z_two), column_sum(d_two), column_sum(db)]
    add_rows(sums_ref, rows + da_sums)


def ffn(me, vec, o, z, cot, wo, ins, outs, hidden):
    count, width = o.shape
    rows = pl.BlockSpec((ROWS, width), lambda i: (i, 0))
    wide = pl.BlockSpec((ROWS, hidden), lambda i: (i, 0))
    layouts = [key for key, _ in ins], [key for key, _ in outs]
    return pl.pallas_call(
        lambda *refs: ffn_kernel(layouts, *refs),
        grid=(count // ROWS,),
        in_specs=[SCALAR, WHOLE, rows, rows, rows, WHOLE] + [ANYWHERE] * (len(ins) + len(outs)),
        out_specs=[rows, wide, wide, rows, rows, rows, rows, rows, pl.BlockSpec((16, width), lambda i: (0, 0))],
        out_shape=[
            of(count, width), of(count, hidden), of(count, hidden), of(count, width), of(count, width),
            of(count, width, dtype=F32), of(count, width), of(count, width), of(16, width, dtype=F32),
        ],
        scratch_shapes=[
            pltpu.VMEM((width, hidden), BF),
            pltpu.VMEM((hidden, width), BF),
            pltpu.VMEM((ROWS, hidden), F32),
            pltpu.VMEM((8, width), F32),
            pltpu.SemaphoreType.DMA((len(ins) + len(outs),)),
        ],
        compiler_params=params(56),
        cost_estimate=cost(8 * count * width * hidden + 4 * count * width * width, o, z, z, cot, o, o, o, o),
        name="ffn",
    )(me, vec, o, z, cot, wo, *[piece for _, piece in ins + outs])


def cross_back_kernel(vec, dq, dy, z, r, w, wo, dy_ref, db_ref, do_ref, sums_ref):
    d_one = dy[...] + dot_nt(dq[...], matrix(w, 0)) * FACTOR
    normed = z[...]
    dy_one = norm_backward(d_one, normed, r[...], vec[6:7, :])
    dy_ref[...] = dy_one
    db = dy_one.astype(BF)
    db_ref[...] = db
    do_ref[...] = dot_nt(db, matrix(wo, 0)).astype(BF)
    add_rows(sums_ref, [column_sum(d_one * normed), column_sum(d_one), column_sum(db)])


def cross_back(vec, dq, dy, z, r, w, wo):
    count, width = dq.shape
    rows = pl.BlockSpec((ROWS, width), lambda i: (i, 0))
    return pl.pallas_call(
        cross_back_kernel,
        grid=(count // ROWS,),
        in_specs=[WHOLE] + [rows] * 3 + [pl.BlockSpec((ROWS, 1), lambda i: (i, 0)), WHOLE, WHOLE],
        out_specs=[rows] * 3 + [pl.BlockSpec((8, width), lambda i: (0, 0))],
        out_shape=[of(count, width, dtype=F32), of(count, width), of(count, width), of(8, width, dtype=F32)],
        compiler_params=params(),
        cost_estimate=cost(4 * count * width * width, dq, dy, z, dy, dq, dq, w, wo),
        name="cross_query_back",
    )(vec, dq, dy, z, r, w, wo)


def memory_back_kernel(dk, dv, w, out):
    out[...] = dot_nt(dk[...], matrix(w, 1)) + dot_nt(dv[...], matrix(w, 2))


def memory_back(dk, dv, w):
    count, width = dk.shape
    rows = pl.BlockSpec((ROWS, width), lambda i: (i, 0))
    return pl.pallas_call(
        memory_back_kernel,
        grid=(count // ROWS,),
        in_specs=[rows, rows, WHOLE],
        out_specs=rows,
        out_shape=of(count, width, dtype=F32),
        compiler_params=params(),
        cost_estimate=cost(4 * count * width * width, dk, dv, dk, dk, w),
        name="memory_back",
    )(dk, dv, w)


def self_back_kernel(dq, dk, dv, dy, w, out):
    total = dy[...] + dot_nt(dq[...], matrix(w, 0)) * FACTOR
    out[...] = total + dot_nt(dk[...], matrix(w, 1)) + dot_nt(dv[...], matrix(w, 2))


def self_back(dq, dk, dv, dy, w):
    count, width = dq.shape
    rows = pl.BlockSpec((ROWS, width), lambda i: (i, 0))
    return pl.pallas_call(
        self_back_kernel,
        grid=(count // ROWS,),
        in_specs=[rows] * 4 + [WHOLE],
        out_specs=rows,
        out_shape=of(count, width, dtype=F32),
        compiler_params=params(),
        cost_estimate=cost(6 * count * width * width, dq, dk, dv, dy, dy, w),
        name="self_project_back",
    )(dq, dk, dv, dy, w)


def weight_grad_kernel(items, slabs, me_ref, *refs):
    ins, (keep, send, hold, extra) = refs[:-4], refs[-4:]
    me = me_ref[0]
    width = hold.shape[2]
    part = width // 8
    for at, (left, right, left_chunk, right_chunk, scale) in enumerate(items):
        a = ins[left][:, left_chunk * width:(left_chunk + 1) * width]
        b = ins[right][:, right_chunk * width:(right_chunk + 1) * width]
        product = dot_tn(a, b)
        hold[at % 2] = product if scale == 1.0 else product * scale
        for relative in range(8):
            owner = jnp.bitwise_xor(me, relative)
            block = hold[at % 2, pl.ds(pl.multiple_of(owner * part, part), part), :].astype(BF)
            (send if relative % 2 else keep)[relative // 2, at * part:(at + 1) * part, :] = block
    if slabs:
        row = 0
        extra[...] = jnp.zeros(extra.shape, F32)
        for ref in ins[len(ins) - slabs:]:
            extra[row:row + ref.shape[0], :] = ref[...]
            row += ref.shape[0]
        block = extra[...].astype(BF)
        for relative in range(8):
            (send if relative % 2 else keep)[relative // 2, part * len(items):, :] = block


def weight_grad(me, operands, items, name, slabs=(), slab_rows=0):
    width = operands[0].shape[1]
    part = width // 8
    shape = of(4, part * len(items) + slab_rows, width)
    return pl.pallas_call(
        lambda *refs: weight_grad_kernel(items, len(slabs), *refs),
        in_specs=[SCALAR] + [WHOLE] * (len(operands) + len(slabs)),
        out_specs=[WHOLE, WHOLE],
        out_shape=[shape, shape],
        scratch_shapes=[pltpu.VMEM((2, width, width), F32), pltpu.VMEM((max(slab_rows, 8), width), F32)],
        compiler_params=params(54),
        cost_estimate=cost(2 * operands[0].shape[0] * width * width * len(items), *operands),
        name=name,
    )(me, *operands, *slabs)


def tall_grad_kernel(me_ref, left, right, keep, send, hold):
    me = me_ref[0]
    width = right.shape[1]
    part = left.shape[1] // 8
    for c in range(left.shape[1] // width):
        hold[c * width:(c + 1) * width, :] = dot_tn(left[:, c * width:(c + 1) * width], right[...]).astype(BF)
    for relative in range(8):
        owner = jnp.bitwise_xor(me, relative)
        block = hold[pl.ds(pl.multiple_of(owner * part, part), part), :]
        (send if relative % 2 else keep)[relative // 2] = block


def tall_grad(me, left, right, name):
    tall, width = left.shape[1], right.shape[1]
    shape = of(4, tall // 8, width)
    return pl.pallas_call(
        tall_grad_kernel,
        in_specs=[SCALAR, WHOLE, WHOLE],
        out_specs=[WHOLE, WHOLE],
        out_shape=[shape, shape],
        scratch_shapes=[pltpu.VMEM((tall, width), BF)],
        compiler_params=params(54),
        cost_estimate=cost(2 * left.shape[0] * tall * width, left, left, right),
        name=name,
    )(me, left, right)


def swap(value, bit, axis="fsdp", size=8):
    return lax.ppermute(value, axis, [(i, i ^ bit) for i in range(size)])


def tie(*values):
    return lax.optimization_barrier(values)


def local(kernel, name, out_shape, *args, scratch=(), scalars=0):
    return pl.pallas_call(
        kernel,
        in_specs=[SCALAR] * scalars + [WHOLE] * (len(args) - scalars),
        out_specs=[WHOLE] * len(out_shape),
        out_shape=out_shape,
        scratch_shapes=scratch,
        compiler_params=params(),
        cost_estimate=cost(0, *args, *out_shape),
        name=name,
    )(*args)


def split_kernel(keep, came, own, to_x, to_y, to_far):
    own[...] = keep[0].astype(F32) + came[0].astype(F32)
    for index, ref in enumerate((to_x, to_y, to_far)):
        ref[...] = (keep[index + 1].astype(F32) + came[index + 1].astype(F32)).astype(BF)


def reduce_core(keep, send):
    return [keep, swap(send, 1)]


def reduce_plane(state):
    keep, came = state
    rows, width = keep.shape[1:]
    own, to_x, to_y, to_far = local(
        split_kernel, "grad_split", [of(rows, width, dtype=F32)] + [of(rows, width)] * 3, keep, came
    )
    return [own, swap(to_far, 6), swap(to_x, 2), swap(to_y, 4)]


def quarter_kernel(at_ref, own, far, from_x, from_y, mine, one, two, three):
    at = at_ref[0]
    rows = mine.shape[0]
    for index, ref in enumerate((mine, one, two, three)):
        place = pl.ds(pl.multiple_of(jnp.bitwise_xor(at, index) * rows, rows), rows)
        total = own[place, :] + far[place, :].astype(F32) + from_x[place, :].astype(F32) + from_y[place, :].astype(F32)
        ref[...] = total.astype(ref.dtype)


def depth_index():
    return lax.axis_index("dp").astype(jnp.int32).reshape(1)


def reduce_quarters(state):
    rows, width = state[0].shape
    shapes = [of(rows // 4, width, dtype=F32)] + [of(rows // 4, width)] * 3
    mine, one, two, three = local(quarter_kernel, "grad_quarters", shapes, depth_index(), *state, scalars=1)
    return [mine, swap(three, 3, "dp", 4), swap(two, 2, "dp", 4), swap(one, 1, "dp", 4)]


def add_kernel(mine, three, two, one, out):
    out[...] = (mine[...] + three[...].astype(F32) + two[...].astype(F32) + one[...].astype(F32)).astype(BF)


def reduce_return(state):
    (mine,) = local(add_kernel, "grad_add", [of(*state[0].shape)], *state)
    return [mine, swap(mine, 3, "dp", 4), swap(mine, 2, "dp", 4), swap(mine, 1, "dp", 4)]


def place_kernel(spans, at_ref, mine, three, two, one, *refs):
    outs, hold = refs[:-1], refs[-1]
    at = at_ref[0]
    rows = mine.shape[0]
    for relative, ref in enumerate((mine, one, two, three)):
        hold[pl.ds(pl.multiple_of(jnp.bitwise_xor(at, relative) * rows, rows), rows), :] = ref[...].astype(F32)
    for (first, count, columns), out in zip(spans, outs):
        if len(out.shape) == 3:
            for index in range(out.shape[0]):
                out[index] = hold[first + index * out.shape[1]:first + (index + 1) * out.shape[1], :]
        else:
            for column in range(columns):
                begin = first + column * count
                out[:, column * hold.shape[1]:(column + 1) * hold.shape[1]] = hold[begin:begin + count, :]


def reduce_end(state, spans, shapes):
    rows, width = state[0].shape
    return local(
        lambda *refs: place_kernel(spans, *refs), "grad_place", shapes, depth_index(), *state,
        scratch=[pltpu.VMEM((4 * rows, width), F32)], scalars=1,
    )


def small_kernel(me_ref, early, late, self_b, cross_b, gain, shift, b_in, b_out):
    me = me_ref[0]
    width, part = early.shape[1], self_b.shape[1]
    turn = lax.rem(width - me * part, width)

    def own(ref, row):
        return pltpu.roll(ref[row // 8 * 8:row // 8 * 8 + 8, :], turn, 1)[row % 8:row % 8 + 1, :part]

    for ref, rows in ((gain, (16, 3, 1)), (shift, (17, 4, 2))):
        for index, row in enumerate(rows):
            ref[index:index + 1, :] = own(early, row)
    b_out[...] = own(early, 0)
    cross_b[0:1, :] = own(early, 24)
    cross_b[1:2, :] = own(early, 25)
    cross_b[2:3, :] = own(early, 5)
    self_b[0:1, :] = own(late, 0)
    self_b[1:2, :] = own(late, 1)
    self_b[2:3, :] = own(early, 18)
    wide = b_in.shape[1]
    row = early[pl.ds(6 + me * wide // width, 1), :]
    b_in[...] = jnp.where(lax.rem(me, 2) == 0, row[:, :wide], row[:, wide:])


def reduce_plain(sizes, blocks):
    value = lax.psum_scatter(blocks.astype(F32), "fsdp", scatter_dimension=0, tiled=False)
    return lax.psum(value.astype(BF), "dp").astype(F32)


def first_hops(shard):
    return swap(shard, 2), swap(shard, 4)


def pieces_of(shard, x, y, far, offsets=(0,)):
    rows = shard.shape[0]
    found = [((0, 0, rows), shard), ((1, 0, rows), swap(shard, 1)), ((2, 0, rows), x), ((4, 0, rows), y)]
    found += [((3, 0, rows), swap(x, 1)), ((5, 0, rows), swap(y, 1))]
    for offset, piece in zip(offsets, far):
        found += [((6, offset, piece.shape[0]), piece), ((7, offset, piece.shape[0]), swap(piece, 1))]
    return found


def shards(sizes, target, memory, target_lengths, memory_lengths, self_qkv, self_bias, self_out, cross_qkv, cross_bias,
           cross_out, ffn_in, ffn_in_bias, ffn_out, ffn_out_bias, norm_gain, norm_bias, cotangent):
    n = sizes[0]
    fast = n == 8 and sizes[1] == 4
    width, hidden = target.shape[-1], ffn_in.shape[1]
    part, wide = width // n, hidden // n
    ratio = hidden // width
    x, mem, cot = target[0], memory[0], cotangent[0]
    place = lax.axis_index("fsdp").astype(jnp.int32)
    me = place.reshape(1)
    vectors = [self_bias, cross_bias, norm_gain, norm_bias, ffn_in_bias.reshape(ratio, part)]

    if fast:
        owners = 8
        own = pack([self_qkv.reshape(3 * part, width)], vectors, "pack_self")
        half = own.shape[0] // 32 * 16
        s_x, s_y = first_hops(own)
        s_low, s_high = swap(s_y[:half], 2), swap(s_x[half:], 4)
        c_one = cross_qkv.reshape(3 * part, width)
        c_two = pack([self_out, cross_out], [ffn_out_bias.reshape(1, part)], "pack_out")
        _, _, c_one, c_two = tie(s_x, s_y, c_one, c_two)
        c_one_x, c_one_y = first_hops(c_one)
        c_two_x, c_two_y = first_hops(c_two)
        self_pieces = pieces_of(own, s_x, s_y, (s_low, s_high), (0, half))
    else:
        owners, me = 1, jnp.zeros((1,), jnp.int32)

        def gathered(member, axis):
            return lax.all_gather(member, "fsdp", axis=axis, tiled=True)

        def single(value):
            return [((0, 0, value.shape[0]), value)]

        fulls = [gathered(member, 1) for member in vectors[:4]] + [gathered(ffn_in_bias, 0).reshape(ratio, width)]
        last = jnp.pad(gathered(ffn_out_bias, 0).reshape(1, width), ((0, SLAB - 1), (0, 0)))
        self_pieces = single(jnp.concatenate([gathered(self_qkv, 1).reshape(3 * width, width)] + fulls))
        ones = single(gathered(cross_qkv, 1).reshape(3 * width, width))
        twos = single(jnp.concatenate([gathered(self_out, 0), gathered(cross_out, 0), last]))
        in_pieces, out_pieces = single(gathered(ffn_in, 0)), single(gathered(ffn_out, 0))

    self_w, vec, q, k, v = project(me, x, self_pieces, owners)
    if fast:
        q, c_one_x, c_one_y, c_two_x, c_two_y, f_in, f_out = tie(q, c_one_x, c_one_y, c_two_x, c_two_y, ffn_in, ffn_out)
        c_one_far, c_two_far = swap(c_one_y, 2), swap(c_two_x, 4)
        f_in_x, f_in_y = first_hops(f_in)
        f_out_x, f_out_y = first_hops(f_out)
    o, lse = attend_forward(q, k, v, target_lengths, True)
    if fast:
        o, c_one_far, c_two_far = tie(o, c_one_far, c_two_far)
        ones = pieces_of(c_one, c_one_x, c_one_y, (c_one_far,))
        twos = pieces_of(c_two, c_two_x, c_two_y, (c_two_far,))
    cross_w, out_w, z_one, r_one, h_one, q2, k2, v2 = between(me, vec, o, x, mem, ones, twos, owners)
    if fast:
        q2, f_in_x, f_in_y, f_out_x, f_out_y = tie(q2, f_in_x, f_in_y, f_out_x, f_out_y)
        f_in_far, f_out_far = swap(f_in_y, 2), swap(f_out_x, 4)
    o2, lse2 = attend_forward(q2, k2, v2, memory_lengths, False)
    if fast:
        o2, f_in_far, f_out_far = tie(o2, f_in_far, f_out_far)
        in_pieces = pieces_of(f_in, f_in_x, f_in_y, (f_in_far,))
        out_pieces = pieces_of(f_out, f_out_x, f_out_y, (f_out_far,))
    mixed, act, da, df, h_two, dy, db2, do2, ffn_sums = ffn(
        me, vec, o2, z_one, cot, out_w, in_pieces, out_pieces, hidden
    )
    if fast:
        out_state = reduce_core(*tall_grad(me, act, df, "ffn_out_grad"))
        h_two, out_state[0] = tie(h_two, out_state[0])
        items = [(0, 1, 0, c, 1.0) for c in range(ratio)]
        in_state = reduce_core(*weight_grad(me, [h_two, da], items, "ffn_in_grad"))
        do2, *out_state = tie(do2, *out_state)
        out_state = reduce_plane(out_state)
        do2, in_state[0], out_state[0] = tie(do2, in_state[0], out_state[0])
    dq2, dk2, dv2, cross_sums = attend_backward(q2, k2, v2, o2, do2, lse2, memory_lengths, False)
    if fast:
        dq2, *states = tie(dq2, *out_state, *in_state)
        out_state, in_state = reduce_quarters(states[:4]), reduce_plane(states[4:])
        dq2, out_state[0], in_state[0] = tie(dq2, out_state[0], in_state[0])
    dy_one, db, do, back_sums = cross_back(vec, dq2, dy, z_one, r_one, cross_w, out_w)
    if fast:
        db, *states = tie(db, *out_state)
        out_state = reduce_return(states)
        operands = [h_one, dq2, mem, dk2, dv2, o2, db2, o, db]
        items = [(0, 1, 0, 0, FACTOR), (2, 3, 0, 0, 1.0), (2, 4, 0, 0, 1.0), (5, 6, 0, 0, 1.0), (7, 8, 0, 0, 1.0)]
        cross_state = reduce_core(
            *weight_grad(me, operands, items, "cross_grad", (ffn_sums, back_sums, cross_sums), 2 * SLAB)
        )
        do, *states = tie(do, *in_state, cross_state[0], out_state[0])
        in_state = reduce_quarters(states[:4])
        do, in_state[0] = tie(do, in_state[0])
    dq, dk, dv, self_sums = attend_backward(q, k, v, o, do, lse, target_lengths, True)
    if fast:
        dq, *states = tie(dq, *in_state, *cross_state)
        in_state, cross_state = reduce_return(states[:4]), reduce_plane(states[4:])
        items = [(0, 1, 0, 0, FACTOR), (0, 2, 0, 0, 1.0), (0, 3, 0, 0, 1.0)]
        self_state = reduce_core(*weight_grad(me, [x, dq, dk, dv], items, "self_grad", (self_sums,), 2 * SLAB))
        dq, dk2, self_state[0], cross_state[0] = tie(dq, dk2, self_state[0], cross_state[0])
    d_target = self_back(dq, dk, dv, dy_one, self_w)
    if fast:
        d_target, dk2, *self_state = tie(d_target, dk2, *self_state)
        self_state = reduce_plane(self_state)
    d_memory = memory_back(dk2, dv2, cross_w)

    if fast:
        f32 = dict(dtype=F32)
        (out_sum,) = reduce_end(out_state, [(0, wide, 1)], [of(wide, width, **f32)])
        (in_sum,) = reduce_end(in_state, [(0, part, ratio)], [of(part, hidden, **f32)])
        cross_state = reduce_quarters(cross_state)
        self_state = reduce_quarters(self_state)
        cross_w_sum, cross_o_sum, self_o_sum, early = reduce_end(
            reduce_return(cross_state),
            [(0, 0, 0), (3 * part, part, 1), (4 * part, part, 1), (5 * part, 2 * SLAB, 1)],
            [of(3, part, width, **f32), of(part, width, **f32), of(part, width, **f32), of(2 * SLAB, width, **f32)],
        )
        self_w_sum, late = reduce_end(
            reduce_return(self_state), [(0, 0, 0), (3 * part, 2 * SLAB, 1)],
            [of(3, part, width, **f32), of(2 * SLAB, width, **f32)],
        )
        shapes = [of(3, part, **f32)] * 4 + [of(1, wide, **f32), of(1, part, **f32)]
        self_b, cross_b, gain, shift, b_in, b_out = local(small_kernel, "small_grads", shapes, me, early, late, scalars=1)
        b_in, b_out = b_in[0], b_out[0]
    else:
        def whole(left, right, scale=1.0):
            return reduce_plain(sizes, (dot_tn(left, right) * scale).reshape(n, left.shape[1] // n, right.shape[1]))

        def mine(rows, size):
            rows = rows.reshape(-1, n * size)
            return lax.dynamic_slice(rows, (0, place * size), (rows.shape[0], size))

        self_w_sum = jnp.stack([whole(x, dq, FACTOR), whole(x, dk), whole(x, dv)])
        cross_w_sum = jnp.stack([whole(h_one, dq2, FACTOR), whole(mem, dk2), whole(mem, dv2)])
        cross_o_sum, self_o_sum = whole(o2, db2), whole(o, db)
        in_sum, out_sum = whole(h_two, da), whole(act, df)
        sums = lax.psum(jnp.concatenate([ffn_sums, back_sums, cross_sums, self_sums]), ("fsdp", "dp"))
        narrow = mine(sums, part)
        self_b = jnp.stack([narrow[32], narrow[33], narrow[18]])
        cross_b = jnp.stack([narrow[24], narrow[25], narrow[5]])
        gain = jnp.stack([narrow[16], narrow[3], narrow[1]])
        shift = jnp.stack([narrow[17], narrow[4], narrow[2]])
        b_in, b_out = mine(sums[6:10], wide)[0], narrow[0]
    return (
        mixed[None], d_target[None], d_memory[None], self_w_sum, self_b, self_o_sum, cross_w_sum, cross_b, cross_o_sum,
        in_sum, b_in, out_sum, b_out, gain, shift,
    )


def solution(mesh):
    rows = P(("fsdp", "dp"), None, None)
    row = P(("fsdp", "dp"))
    stacked, vectors, matrix, vector = P(None, "fsdp", None), P(None, "fsdp"), P("fsdp", None), P("fsdp")
    weights = (stacked, vectors, matrix, stacked, vectors, matrix, matrix, vector, matrix, vector, vectors, vectors)
    sizes = (mesh.shape["fsdp"], mesh.shape["dp"])
    return jax.shard_map(
        lambda *args: shards(sizes, *args),
        mesh=mesh,
        in_specs=(rows, rows, row, row) + weights + (rows,),
        out_specs=(rows, rows, rows) + weights,
        check_vma=False,
    )
```

```python
import jax
import jax.numpy as jnp
from jax import lax
from jax.experimental import pallas as pl
from jax.experimental.pallas import tpu as pltpu
from jax.sharding import PartitionSpec as P

HDIM = 64
PAIR = 2 * HDIM
BLOCK = 256
ROWS = 256
ATTEND_VMEM = 20
MASKED = -1e30
FACTOR = HDIM ** (-0.5)
BF = jnp.bfloat16
F32 = jnp.float32


def dot_nn(a, b):
    return lax.dot_general(a, b, (((1,), (0,)), ((), ())), preferred_element_type=F32)


def dot_nt(a, b):
    return lax.dot_general(a, b, (((1,), (1,)), ((), ())), preferred_element_type=F32)


def dot_tn(a, b):
    return lax.dot_general(a, b, (((0,), (0,)), ((), ())), preferred_element_type=F32)


def column_sum(values):
    return jnp.sum(values.astype(F32), axis=0, keepdims=True)


def head_lanes(head):
    lane = lax.broadcasted_iota(jnp.int32, (1, PAIR), 1)
    return (lane // HDIM) == head, lane == (HDIM if head == 0 else 0)


def pick(mask, yes, no, shape):
    return jnp.where(jnp.broadcast_to(mask, shape), yes, no)


def length_bias(count, limit):
    positions = lax.broadcasted_iota(jnp.int32, (count, PAIR), 0)
    return jnp.where(positions < limit, 0.0, MASKED).astype(F32)


def causal_edge(values, fill):
    key_at = lax.broadcasted_iota(jnp.int32, values.shape, 0)
    query_at = lax.broadcasted_iota(jnp.int32, values.shape, 1)
    return jnp.where(key_at <= query_at, values, fill)


def attend_forward_kernel(causal, limit_ref, q_ref, k_ref, v_ref, o_ref, lse_ref):
    count, sources = q_ref.shape[0], k_ref.shape[0]
    k_all, v_all = k_ref[...].astype(F32), v_ref[...].astype(F32)
    bias = length_bias(sources, limit_ref[0])
    keys, values = [], []
    for head in range(2):
        own, spare = head_lanes(head)
        keys.append(pick(spare, bias, k_all, k_all.shape).astype(BF))
        ones = pick(spare, 1.0, 0.0, v_all.shape)
        values.append(pick(own, v_all, ones, v_all.shape).T.astype(BF))

    def scores_of(unit):
        block, head = unit
        rows = slice(block * BLOCK, (block + 1) * BLOCK)
        extent = (block + 1) * BLOCK if causal else sources
        own, spare = head_lanes(head)
        q_block = q_ref[rows, :].astype(F32)
        ones = pick(spare, 1.0, 0.0, q_block.shape)
        scores = dot_nt(keys[head][:extent], pick(own, q_block, ones, q_block.shape).astype(BF))
        if causal:
            edge = causal_edge(scores[extent - BLOCK:], MASKED)
            scores = edge if extent == BLOCK else jnp.concatenate([scores[: extent - BLOCK], edge], axis=0)
        return scores

    parts = {}

    def finish(unit, expo, highest):
        block, head = unit
        rows = slice(block * BLOCK, (block + 1) * BLOCK)
        mixed = dot_nn(values[head][:, : expo.shape[0]], expo)
        at = HDIM if head == 0 else 0
        total = mixed[at:at + 1]
        lse_ref[0, head:head + 1, rows] = highest + jnp.log(total)
        parts[unit] = mixed[head * HDIM:(head + 1) * HDIM] * (1.0 / total)
        if head == 1:
            o_ref[rows, :] = jnp.concatenate([parts[(block, 0)], parts[unit]], axis=0).T.astype(BF)

    units = [(block, head) for block in range(count // BLOCK) for head in range(2)]
    ahead = [scores_of(unit) for unit in units[:2]]
    before = None
    for at, unit in enumerate(units):
        if at + 2 < len(units):
            ahead.append(scores_of(units[at + 2]))
        highest = jnp.max(ahead[at], axis=0, keepdims=True)
        expo = jnp.exp(ahead[at] - highest).astype(BF)
        if before is not None:
            finish(*before)
        before = (unit, expo, highest)
    finish(*before)


def attend_backward_kernel(
    causal, limit_ref, q_ref, k_ref, v_ref, o_ref, do_ref, lse_ref, dq_ref, dk_ref, dv_ref, sums_ref, dq_acc
):
    count, sources = q_ref.shape[0], k_ref.shape[0]
    q_all, k_all = q_ref[...].astype(F32), k_ref[...].astype(F32)
    do_all = do_ref[...].astype(F32)
    bias = length_bias(sources, limit_ref[0])
    product = (do_all * o_ref[...].astype(F32)).T
    q_aug, q_own, k_aug, kt_own, do_own, delta, lse = [], [], [], [], [], [], []
    for head in range(2):
        own, spare = head_lanes(head)
        q_aug.append(pick(own, q_all, pick(spare, 1.0, 0.0, q_all.shape), q_all.shape).astype(BF))
        q_own.append(pick(own, q_all, 0.0, q_all.shape).astype(BF))
        k_aug.append(pick(spare, bias, k_all, k_all.shape).astype(BF))
        kt_own.append(pick(own, k_all, 0.0, k_all.shape).T.astype(BF))
        do_own.append(pick(own, do_all, 0.0, do_all.shape).astype(BF))
        delta.append(jnp.sum(product[head * HDIM:(head + 1) * HDIM], axis=0, keepdims=True))
        lse.append(lse_ref[0, head:head + 1, :])

    def products(unit):
        block, head = unit
        rows = slice(block * BLOCK, (block + 1) * BLOCK)
        first = block * BLOCK if causal else 0
        return (
            dot_nt(k_aug[head][rows], q_aug[head][first:]),
            dot_nt(v_ref[rows, :], do_own[head][first:]),
        )

    def gradients(unit, scores, d_probs):
        block, head = unit
        first = block * BLOCK if causal else 0
        probs = jnp.exp(scores - lse[head][:, first:])
        if causal:
            edge = causal_edge(probs[:, :BLOCK], 0.0)
            probs = edge if first + BLOCK == count else jnp.concatenate([edge, probs[:, BLOCK:]], axis=1)
        d_scores = (probs * (d_probs - delta[head][:, first:])).astype(BF)
        return probs.astype(BF), d_scores

    held = {}

    def finish(unit, probs, d_scores):
        block, head = unit
        rows = slice(block * BLOCK, (block + 1) * BLOCK)
        first = block * BLOCK if causal else 0
        dv = dot_nn(probs, do_own[head][first:])
        dk = dot_nn(d_scores, q_own[head][first:])
        dq = dot_nn(kt_own[head][:, rows], d_scores)
        if head == 0:
            held[block] = (dv, dk, dq)
            return
        dv = (held[block][0] + dv).astype(BF)
        dv_ref[rows, :] = dv
        held["dv"] = held.get("dv", 0.0) + column_sum(dv)
        dk_ref[rows, :] = (held[block][1] + dk).astype(BF)
        if block == 0:
            dq_acc[...] = held[block][2] + dq
        else:
            dq_acc[:, first:] += held[block][2] + dq

    units = [(block, head) for block in range(sources // BLOCK) for head in range(2)]
    ahead = [products(units[0])]
    before = None
    for at, unit in enumerate(units):
        if at + 1 < len(units):
            ahead.append(products(units[at + 1]))
        current = (unit,) + gradients(unit, *ahead[at])
        if before is not None:
            finish(*before)
        before = current
    finish(*before)
    dq = dq_acc[...].T.astype(BF)
    dq_ref[...] = dq
    sums_ref[...] = jnp.concatenate([column_sum(dq) * FACTOR, held["dv"], jnp.zeros((6, PAIR), F32)], axis=0)


def attend_call(kernel, name, causal, work, specs, arrays, out_specs, outs, scratch, limit, pairs, held):
    first, last = pairs
    held = list(held)

    def shifted(spec):
        if spec is None:
            return pl.BlockSpec(memory_space=pltpu.SMEM)
        shape, index = spec
        return pl.BlockSpec(shape, lambda i: index(i + first))

    def body(*refs):
        kernel(causal, *refs[: len(specs)], *refs[len(specs) + len(held):])

    return pl.pallas_call(
        body,
        grid=(last - first,),
        in_specs=[shifted(spec) for spec in specs] + [pl.BlockSpec(memory_space=pl.ANY)] * len(held),
        out_specs=[shifted(spec) for spec in out_specs],
        out_shape=outs,
        scratch_shapes=scratch,
        input_output_aliases={len(specs) + at: at for at in range(len(held))},
        compiler_params=pltpu.CompilerParams(vmem_limit_bytes=limit << 20),
        cost_estimate=pl.CostEstimate(flops=8 * work * (last - first) * PAIR, bytes_accessed=1 << 20, transcendentals=0),
        name=name,
    )(*arrays, *held)


def attend_forward(q, k, v, limit, causal, pairs=None, held=()):
    count, width = q.shape
    sources = k.shape[0]
    total = width // PAIR
    of_q = ((count, PAIR), lambda i: (0, i))
    of_k = ((sources, PAIR), lambda i: (0, i))
    stats = ((1, 2, count), lambda i: (i, 0, 0))
    outs = [jax.ShapeDtypeStruct((count, width), BF), jax.ShapeDtypeStruct((total, 2, count), F32)]
    return attend_call(
        attend_forward_kernel, "attend_forward", causal, 16 * count * sources * (5 if causal else 8) // 8,
        [None, of_q, of_k, of_k], [limit, q, k, v], [of_q, stats], outs, [], ATTEND_VMEM, pairs or (0, total), held,
    )


def attend_backward(q, k, v, o, do, lse, limit, causal, pairs=None, held=()):
    count, width = q.shape
    sources = k.shape[0]
    total = width // PAIR
    of_q = ((count, PAIR), lambda i: (0, i))
    of_k = ((sources, PAIR), lambda i: (0, i))
    stats = ((1, 2, count), lambda i: (i, 0, 0))
    outs = [
        jax.ShapeDtypeStruct((count, width), BF),
        jax.ShapeDtypeStruct((sources, width), BF),
        jax.ShapeDtypeStruct((sources, width), BF),
        jax.ShapeDtypeStruct((8, width), F32),
    ]
    return attend_call(
        attend_backward_kernel, "attend_backward", causal, 40 * count * sources * (5 if causal else 8) // 8,
        [None, of_q, of_k, of_k, of_q, of_q, stats], [limit, q, k, v, o, do, lse],
        [of_q, of_k, of_k, ((8, PAIR), lambda i: (0, i))], outs, [pltpu.VMEM((PAIR, count), F32)], ATTEND_VMEM,
        pairs or (0, total), held,
    )


WHOLE = pl.BlockSpec(memory_space=pltpu.VMEM)
DENSE_VMEM = 32
FFN_VMEM = 48
GRAD_VMEM = 56
SMALL_VMEM = 16
ANYWHERE = pl.BlockSpec(memory_space=pl.ANY)
SCALAR = pl.BlockSpec(memory_space=pltpu.SMEM)
SLAB = 32


def params(limit):
    return pltpu.CompilerParams(vmem_limit_bytes=limit << 20)


def full(value):
    shape = tuple(value.shape)
    return pl.BlockSpec(shape, lambda *_: (0,) * len(shape), pipeline_mode=pl.Buffered(1))


def cost(flops, *arrays):
    size = sum(a.size * a.dtype.itemsize for a in arrays)
    return pl.CostEstimate(flops=8 * flops, bytes_accessed=size, transcendentals=0)


def of(*shape, dtype=BF):
    return jax.ShapeDtypeStruct(shape, dtype)


def matrix(bundle, index):
    owners, width = bundle.shape[0], bundle.shape[2]
    part = width // owners
    return bundle[:, index * part:(index + 1) * part, :].reshape(width, width)


def bring(refs, holds, sem):
    copies = [pltpu.make_async_copy(ref, hold, sem.at[at]) for at, (ref, hold) in enumerate(zip(refs, holds))]
    for copy in copies:
        copy.start()
    return copies


def fetch(me, pieces, bundle, sem, first):
    copies = []
    shard = max(offset + rows for (_, offset, rows), _ in pieces)
    for at, ((relative, offset, rows), piece) in enumerate(pieces):
        owner = jnp.bitwise_xor(me, relative)
        if len(bundle.shape) == 3:
            target = bundle.at[owner, pl.ds(offset, rows)]
        else:
            target = bundle.at[pl.ds(pl.multiple_of(owner * shard + offset, 16), rows)]
        copies.append(pltpu.make_async_copy(piece, target, sem.at[first + at]))
        copies[-1].start()
    return copies


def wait_all(copies):
    for copy in copies:
        copy.wait()


def leave(inside, outside, sem, at):
    return pltpu.make_async_copy(inside, outside, sem.at[at])


def at_first(action):
    pl.when(pl.program_id(0) == 0)(action)


def at_last(action):
    pl.when(pl.program_id(0) == pl.num_programs(0) - 1)(action)


def normalise(summed):
    centred = summed - jnp.mean(summed, axis=-1, keepdims=True)
    inverse = lax.rsqrt(jnp.mean(centred * centred, axis=-1, keepdims=True) + 1e-05)
    return centred * inverse, inverse


def norm_backward(d_out, normed, inverse, gain):
    d_normed = d_out * gain
    return inverse * (
        d_normed
        - jnp.mean(d_normed, axis=-1, keepdims=True)
        - normed * jnp.mean(d_normed * normed, axis=-1, keepdims=True)
    )


def gelu_parts(a):
    bell = jnp.exp(-0.5 * a * a)
    t = 1.0 / (1.0 + 0.23164189 * jnp.abs(a))
    tail = t * (0.127414796 + t * (-0.142248368 + t * (0.7107068705 + t * (-0.7265760135 + t * 0.5307027145)))) * bell
    phi = jnp.where(a >= 0.0, 1.0 - tail, tail)
    return a * phi, phi + a * bell * 0.3989422804014327


def add_rows(ref, rows):
    block = jnp.concatenate(rows + [jnp.zeros((ref.shape[0] - len(rows), ref.shape[1]), F32)], axis=0)

    @pl.when(pl.program_id(0) == 0)
    def _():
        ref[...] = block

    @pl.when(pl.program_id(0) > 0)
    def _():
        ref[...] += block


def pack_kernel(*refs):
    count = (len(refs) - 3) // 2
    vectors, out, holds, slab, sem = refs[:count], refs[count], refs[count + 1:-2], refs[-2], refs[-1]
    copies = bring(vectors, holds, sem)
    slab[...] = jnp.zeros(slab.shape, F32)
    row = 0
    for copy, hold in zip(copies, holds):
        copy.wait()
        slab[row:row + hold.shape[0], : hold.shape[1]] = hold[...].astype(F32)
        row += hold.shape[0]
    for owner in range(out.shape[0]):
        out[owner] = slab[...].astype(BF)


def pack(vectors, owners, width):
    return pl.pallas_call(
        pack_kernel,
        grid=(1,),
        in_specs=[ANYWHERE] * len(vectors),
        out_specs=full(of(owners, SLAB, width)),
        out_shape=of(owners, SLAB, width),
        scratch_shapes=[pltpu.VMEM(vector.shape, BF) for vector in vectors] + [
            pltpu.VMEM((SLAB, width), F32), pltpu.SemaphoreType.DMA((len(vectors),)),
        ],
        compiler_params=params(SMALL_VMEM),
        name="pack_small",
    )(*vectors)


def project_kernel(layout, me_ref, x, slabs, *refs):
    pieces, (w_out, vec, q_ref, k_ref, v_ref, w, sem) = refs[: len(layout)], refs[len(layout):]
    owners, width = w.shape[0], w.shape[2]
    part = width // owners

    @at_first
    def _():
        copies = fetch(me_ref[0], list(zip(layout, pieces)), w, sem, 0)
        vec[...] = jnp.zeros(vec.shape, F32)
        for owner in range(owners):
            slab = slabs[owner].astype(F32)
            vec[:12, owner * part:(owner + 1) * part] = slab[:12, :part]
            vec[16:17, owner * part:(owner + 1) * part] = slab[16:17, :part]
            for row in range(4):
                at = (owner * 4 + row) * part
                vec[12 + at // width:13 + at // width, at % width:at % width + part] = slab[12 + row:13 + row, :part]
        wait_all(copies)
        leave(w, w_out, sem, len(layout)).start()

    values = x[...]
    q_ref[...] = ((dot_nn(values, matrix(w, 0)) + vec[0:1, :]) * FACTOR).astype(BF)
    k_ref[...] = dot_nn(values, matrix(w, 1)).astype(BF)
    v_ref[...] = (dot_nn(values, matrix(w, 2)) + vec[1:2, :]).astype(BF)
    at_last(lambda: leave(w, w_out, sem, len(layout)).wait())


def project(me, x, slabs, pieces, owners):
    count, width = x.shape
    rows = pl.BlockSpec((ROWS, width), lambda i: (i, 0))
    layout = [key for key, _ in pieces]
    return pl.pallas_call(
        lambda *refs: project_kernel(layout, *refs),
        grid=(count // ROWS,),
        in_specs=[SCALAR, rows, full(slabs)] + [ANYWHERE] * len(pieces),
        out_specs=[ANYWHERE, full(of(24, width)), rows, rows, rows],
        out_shape=[of(owners, 3 * width // owners, width), of(24, width, dtype=F32)] + [of(count, width)] * 3,
        scratch_shapes=[
            pltpu.VMEM((owners, 3 * width // owners, width), BF),
            pltpu.SemaphoreType.DMA((len(pieces) + 1,)),
        ],
        compiler_params=params(DENSE_VMEM),
        cost_estimate=cost(6 * count * width * width, x, x, x, x, x),
        name="self_project",
    )(me, x, slabs, *[piece for _, piece in pieces])


def between_kernel(layouts, me_ref, vec, o, x, mem, *refs):
    count = len(layouts[0])
    ones, twos = refs[:count], refs[count:count + len(layouts[1])]
    w_out, wo_out, z_ref, r_ref, h_ref, q_ref, k_ref, v_ref, w, wo, sem = refs[count + len(layouts[1]):]
    leaving = leave(w, w_out, sem, sem.shape[0] - 2), leave(wo, wo_out, sem, sem.shape[0] - 1)

    @at_first
    def _():
        copies = fetch(me_ref[0], list(zip(layouts[0], ones)), w, sem, 0)
        copies += fetch(me_ref[0], list(zip(layouts[1], twos)), wo, sem, count)
        wait_all(copies)
        for copy in leaving:
            copy.start()

    summed = x[...].astype(F32) + dot_nn(o[...], matrix(wo, 0)) + vec[2:3, :]
    source = mem[...]
    k_ref[...] = dot_nn(source, matrix(w, 1)).astype(BF)
    v_ref[...] = (dot_nn(source, matrix(w, 2)) + vec[4:5, :]).astype(BF)
    z, r = normalise(summed)
    z_ref[...] = z
    r_ref[...] = jnp.broadcast_to(r, r_ref.shape)
    hidden = (z * vec[6:7, :] + vec[9:10, :]).astype(BF)
    h_ref[...] = hidden
    q_ref[...] = ((dot_nn(hidden, matrix(w, 0)) + vec[3:4, :]) * FACTOR).astype(BF)
    at_last(lambda: wait_all(leaving))


def between(me, vec, o, x, mem, ones, twos, owners):
    count, width = x.shape
    part = width // owners
    rows = pl.BlockSpec((ROWS, width), lambda i: (i, 0))
    layouts = [key for key, _ in ones], [key for key, _ in twos]
    return pl.pallas_call(
        lambda *refs: between_kernel(layouts, *refs),
        grid=(count // ROWS,),
        in_specs=[SCALAR, full(vec), rows, rows, rows] + [ANYWHERE] * (len(ones) + len(twos)),
        out_specs=[ANYWHERE, ANYWHERE, rows, pl.BlockSpec((ROWS, 128), lambda i: (i, 0))] + [rows] * 4,
        out_shape=[
            of(owners, 3 * part, width), of(owners, 2 * part, width), of(count, width, dtype=F32),
            of(count, 128, dtype=F32),
        ] + [of(count, width)] * 4,
        scratch_shapes=[
            pltpu.VMEM((owners, 3 * part, width), BF),
            pltpu.VMEM((owners, 2 * part, width), BF),
            pltpu.SemaphoreType.DMA((len(ones) + len(twos) + 2,)),
        ],
        compiler_params=params(DENSE_VMEM),
        cost_estimate=cost(8 * count * width * width, x, x, x, x, x, x, x, x, x),
        name="self_out_cross_project",
    )(me, vec, o, x, mem, *[piece for _, piece in ones + twos])


def ffn_kernel(layouts, me_ref, vec, o, z_in, cot, wo, *refs):
    count = len(layouts[0])
    ins, outs = refs[:count], refs[count:count + len(layouts[1])]
    (mixed, act_ref, da_ref, df_ref, h_ref, dy_ref, db_ref, do_ref, sums_ref, w_in, w_out, slope, sem) = (
        refs[count + len(layouts[1]):]
    )
    width = o.shape[1]
    chunks = w_in.shape[1] // width
    in_copies = list(zip(layouts[0], ins)), list(zip(layouts[1], outs))

    @at_first
    def _():
        copies = fetch(me_ref[0], in_copies[0], w_in, sem, 0) + fetch(me_ref[0], in_copies[1], w_out, sem, count)
        wait_all(copies)

    gains = [vec[6 + i:7 + i, :] for i in range(3)]
    shifts = [vec[9 + i:10 + i, :] for i in range(3)]
    first = z_in[...] * gains[0] + shifts[0]
    z_two, r_two = normalise(first + dot_nn(o[...], matrix(wo, 1)) + vec[5:6, :])
    second = z_two * gains[1] + shifts[1]
    hidden = second.astype(BF)
    h_ref[...] = hidden

    def columns(c):
        return slice(c * width, (c + 1) * width)

    total = second + vec[16:17, :]
    ahead = dot_nn(hidden, w_in[:, columns(0)])
    before = None
    for c in range(chunks):
        pre = ahead + vec[12 + c:13 + c, :]
        if c + 1 < chunks:
            ahead = dot_nn(hidden, w_in[:, columns(c + 1)])
        act, grad = gelu_parts(pre)
        act = act.astype(BF)
        act_ref[:, columns(c)] = act
        slope[:, columns(c)] = grad
        if before is not None:
            total = total + dot_nn(before, w_out[columns(c - 1), :])
        before = act
    total = total + dot_nn(before, w_out[columns(chunks - 1), :])
    z, r = normalise(total)
    mixed[...] = (z * gains[2] + shifts[2]).astype(BF)
    incoming = cot[...].astype(F32)
    dy_three = norm_backward(incoming, z, r, gains[2])
    df = dy_three.astype(BF)
    df_ref[...] = df
    rows = [column_sum(df), column_sum(incoming * z), column_sum(incoming)]

    da_sums = []
    d_two = dy_three
    ahead = dot_nt(df, w_out[columns(0), :])
    before = None
    for c in range(chunks):
        d_act = ahead
        if c + 1 < chunks:
            ahead = dot_nt(df, w_out[columns(c + 1), :])
        da = (d_act * slope[:, columns(c)]).astype(BF)
        da_ref[:, columns(c)] = da
        da_sums.append(column_sum(da))
        if before is not None:
            d_two = d_two + dot_nt(before, w_in[:, columns(c - 1)])
        before = da
    d_two = d_two + dot_nt(before, w_in[:, columns(chunks - 1)])
    dy_two = norm_backward(d_two, z_two, r_two, gains[1])
    dy_ref[...] = dy_two
    db = dy_two.astype(BF)
    db_ref[...] = db
    do_ref[...] = dot_nt(db, matrix(wo, 1)).astype(BF)
    rows += [column_sum(d_two * z_two), column_sum(d_two), column_sum(db)]
    add_rows(sums_ref, rows + da_sums)


def ffn(me, vec, o, z, cot, wo, ins, outs, hidden):
    count, width = o.shape
    rows = pl.BlockSpec((ROWS, width), lambda i: (i, 0))
    wide = pl.BlockSpec((ROWS, hidden), lambda i: (i, 0))
    layouts = [key for key, _ in ins], [key for key, _ in outs]
    return pl.pallas_call(
        lambda *refs: ffn_kernel(layouts, *refs),
        grid=(count // ROWS,),
        in_specs=[SCALAR, full(vec), rows, rows, rows, full(wo)] + [ANYWHERE] * (len(ins) + len(outs)),
        out_specs=[rows, wide, wide, rows, rows, rows, rows, rows, pl.BlockSpec((16, width), lambda i: (0, 0))],
        out_shape=[
            of(count, width), of(count, hidden), of(count, hidden), of(count, width), of(count, width),
            of(count, width, dtype=F32), of(count, width), of(count, width), of(16, width, dtype=F32),
        ],
        scratch_shapes=[
            pltpu.VMEM((width, hidden), BF),
            pltpu.VMEM((hidden, width), BF),
            pltpu.VMEM((ROWS, hidden), F32),
            pltpu.SemaphoreType.DMA((len(ins) + len(outs),)),
        ],
        compiler_params=params(FFN_VMEM),
        cost_estimate=cost(8 * count * width * hidden + 4 * count * width * width, o, z, z, cot, o, o, o, o),
        name="ffn",
    )(me, vec, o, z, cot, wo, *[piece for _, piece in ins + outs])


def cross_back_kernel(vec, dq, dy, z, r, w, wo, dy_ref, db_ref, do_ref, sums_ref):
    d_one = dy[...] + dot_nt(dq[...], matrix(w, 0)) * FACTOR
    normed = z[...]
    dy_one = norm_backward(d_one, normed, r[:, :1], vec[6:7, :])
    dy_ref[...] = dy_one
    db = dy_one.astype(BF)
    db_ref[...] = db
    do_ref[...] = dot_nt(db, matrix(wo, 0)).astype(BF)
    add_rows(sums_ref, [column_sum(d_one * normed), column_sum(d_one), column_sum(db)])


def cross_back(vec, dq, dy, z, r, w, wo):
    count, width = dq.shape
    rows = pl.BlockSpec((ROWS, width), lambda i: (i, 0))
    return pl.pallas_call(
        cross_back_kernel,
        grid=(count // ROWS,),
        in_specs=[full(vec)] + [rows] * 3 + [pl.BlockSpec((ROWS, 128), lambda i: (i, 0)), full(w), full(wo)],
        out_specs=[rows] * 3 + [pl.BlockSpec((8, width), lambda i: (0, 0))],
        out_shape=[of(count, width, dtype=F32), of(count, width), of(count, width), of(8, width, dtype=F32)],
        compiler_params=params(DENSE_VMEM),
        cost_estimate=cost(4 * count * width * width, dq, dy, z, dy, dq, dq, w, wo),
        name="cross_query_back",
    )(vec, dq, dy, z, r, w, wo)


def memory_back_kernel(dk, dv, w, out):
    out[...] = dot_nt(dk[...], matrix(w, 1)) + dot_nt(dv[...], matrix(w, 2))


def memory_back(dk, dv, w):
    count, width = dk.shape
    rows = pl.BlockSpec((ROWS, width), lambda i: (i, 0))
    return pl.pallas_call(
        memory_back_kernel,
        grid=(count // ROWS,),
        in_specs=[rows, rows, full(w)],
        out_specs=rows,
        out_shape=of(count, width, dtype=F32),
        compiler_params=params(DENSE_VMEM),
        cost_estimate=cost(4 * count * width * width, dk, dv, dk, dk, w),
        name="memory_back",
    )(dk, dv, w)


def self_back_kernel(dq, dk, dv, dy, w, out):
    total = dy[...] + dot_nt(dq[...], matrix(w, 0)) * FACTOR
    out[...] = total + dot_nt(dk[...], matrix(w, 1)) + dot_nt(dv[...], matrix(w, 2))


def self_back(dq, dk, dv, dy, w):
    count, width = dq.shape
    rows = pl.BlockSpec((ROWS, width), lambda i: (i, 0))
    return pl.pallas_call(
        self_back_kernel,
        grid=(count // ROWS,),
        in_specs=[rows] * 4 + [full(w)],
        out_specs=rows,
        out_shape=of(count, width, dtype=F32),
        compiler_params=params(DENSE_VMEM),
        cost_estimate=cost(6 * count * width * width, dq, dk, dv, dy, dy, w),
        name="self_project_back",
    )(dq, dk, dv, dy, w)


def hand_out(me, hold, keep, send, sem, rows, first):
    copies = []
    for relative in range(8):
        source = hold.at[jnp.bitwise_xor(me, relative), rows]
        target = (send if relative % 2 else keep).at[relative // 2, rows]
        copies.append(pltpu.make_async_copy(source, target, sem.at[first + relative]))
        copies[-1].start()
    return copies


def weight_grad_kernel(items, parts, count, me_ref, *refs):
    held = len(parts)
    outside, slabs = refs[:count], refs[count:-(held + 5)]
    keep, send = refs[-(held + 5):-(held + 3)]
    holds, hold, extra, sem = refs[-(held + 3):-3], refs[-3], refs[-2], refs[-1]
    width = hold.shape[2]
    part = width // 8
    coming = bring([outside[at].at[:, pl.ds(chunk * width, width)] for at, chunk in parts], holds, sem)
    waited = set()
    leaving, done = [], 0
    for at, (left, right, scale) in enumerate(items):
        for index in (left, right):
            if index not in waited:
                coming[index].wait()
                waited.add(index)
        product = dot_tn(holds[left][...], holds[right][...])
        product = product if scale == 1.0 else product * scale
        hold[:, at * part:(at + 1) * part, :] = product.astype(BF).reshape(8, part, width)
        if at == len(items) - 2:
            done = (at + 1) * part
            leaving += hand_out(me_ref[0], hold, keep, send, sem, pl.ds(0, done), held)
    if slabs:
        row = 0
        extra[...] = jnp.zeros(extra.shape, F32)
        for ref in slabs:
            extra[row:row + ref.shape[0], :] = ref[...]
            row += ref.shape[0]
        block = extra[...].astype(BF)
        for owner in range(8):
            hold[owner, part * len(items):, :] = block
    leaving += hand_out(me_ref[0], hold, keep, send, sem, pl.ds(done, hold.shape[1] - done), held + 8)
    wait_all(leaving)


def weight_grad(me, operands, parts, items, name, slabs=(), slab_rows=0):
    count, width = operands[0].shape
    rows = width // 8 * len(items) + slab_rows
    return pl.pallas_call(
        lambda *refs: weight_grad_kernel(items, parts, len(operands), *refs),
        grid=(1,),
        in_specs=[SCALAR] + [ANYWHERE] * len(operands) + [full(slab) for slab in slabs],
        out_specs=[ANYWHERE, ANYWHERE],
        out_shape=[of(4, rows, width)] * 2,
        scratch_shapes=[pltpu.VMEM((count, width), BF) for _ in parts] + [
            pltpu.VMEM((8, rows, width), BF),
            pltpu.VMEM((max(slab_rows, 8), width), F32),
            pltpu.SemaphoreType.DMA((len(parts) + 16,)),
        ],
        compiler_params=params(GRAD_VMEM),
        cost_estimate=cost(2 * count * width * width * len(items), *operands),
        name=name,
    )(me, *operands, *slabs)


def tall_grad_kernel(me_ref, left, right, keep, send, left_hold, right_hold, hold, sem):
    width = right.shape[1]
    chunks = left.shape[1] // width
    chip, core = me_ref[0] // 2, lax.rem(me_ref[0], 2)
    coming = [pltpu.make_async_copy(right, right_hold, sem.at[0])]
    for c in range(chunks):
        span = pl.ds(pl.multiple_of(jnp.bitwise_xor(chip, c) * width, width), width)
        coming.append(pltpu.make_async_copy(left.at[:, span], left_hold.at[c], sem.at[1 + c]))
    for copy in coming:
        copy.start()
    coming[0].wait()
    leaving = []
    for c in range(chunks):
        coming[1 + c].wait()
        product = dot_tn(left_hold[c], right_hold[...])
        hold[c] = product.astype(BF).reshape(hold.shape[1:])
        for at, (index, out) in enumerate(((core, keep), (1 - core, send))):
            leaving.append(pltpu.make_async_copy(hold.at[c, index], out.at[c], sem.at[1 + chunks + 2 * c + at]))
            leaving[-1].start()
    wait_all(leaving)


def tall_grad(me, left, right, name):
    (count, tall), width = left.shape, right.shape[1]
    chunks = tall // width
    return pl.pallas_call(
        tall_grad_kernel,
        grid=(1,),
        in_specs=[SCALAR, ANYWHERE, ANYWHERE],
        out_specs=[ANYWHERE, ANYWHERE],
        out_shape=[of(4, tall // 8, width)] * 2,
        scratch_shapes=[
            pltpu.VMEM((chunks, count, width), BF),
            pltpu.VMEM(right.shape, BF),
            pltpu.VMEM((chunks, 2, tall // 8, width), BF),
            pltpu.SemaphoreType.DMA((1 + 3 * chunks,)),
        ],
        compiler_params=params(GRAD_VMEM),
        cost_estimate=cost(2 * count * tall * width, left, left, right),
        name=name,
    )(me, left, right)


def swap(value, bit, axis="fsdp", size=8):
    return lax.ppermute(value, axis, [(i, i ^ bit) for i in range(size)])


def tie(*values):
    return lax.optimization_barrier(values)


def local(kernel, name, out_shape, *args, scratch=(), scalars=0):
    return pl.pallas_call(
        kernel,
        in_specs=[SCALAR] * scalars + [WHOLE] * (len(args) - scalars),
        out_specs=[WHOLE] * len(out_shape),
        out_shape=out_shape,
        scratch_shapes=scratch,
        compiler_params=params(SMALL_VMEM),
        cost_estimate=cost(0, *args, *out_shape),
        name=name,
    )(*args)


def halves(rows):
    return rows // 32 * 16


def split_kernel(keep, came, own, to_x, to_y, rest_y, rest_x):
    half = rest_y.shape[0]

    def total(index, rows):
        return keep[index, rows, :].astype(F32) + came[index, rows, :].astype(F32)

    low, high = slice(None, half), slice(half, None)
    own[...] = total(0, slice(None))
    to_x[0], to_x[1] = total(1, low).astype(BF), total(3, low).astype(BF)
    to_y[0], to_y[1] = total(2, high).astype(BF), total(3, high).astype(BF)
    rest_y[...] = total(2, low).astype(BF)
    rest_x[...] = total(1, high).astype(BF)


def reduce_core(keep, send):
    return [keep, swap(send, 1)]


def reduce_first(state):
    keep, came = state
    rows, width = keep.shape[1:]
    low, high = halves(rows), rows - halves(rows)
    shapes = [of(rows, width, dtype=F32), of(2, low, width), of(2, high, width), of(low, width), of(high, width)]
    own, to_x, to_y, rest_y, rest_x = local(split_kernel, "grad_split", shapes, keep, came)
    return [own, rest_y, rest_x, swap(to_x, 2), swap(to_y, 4)]


def second_kernel(own, rest_y, rest_x, from_x, from_y, out, last_y, last_x):
    half = rest_y.shape[0]
    out[:half, :] = own[:half, :] + from_x[0].astype(F32)
    out[half:, :] = own[half:, :] + from_y[0].astype(F32)
    last_y[...] = (rest_y[...].astype(F32) + from_x[1].astype(F32)).astype(BF)
    last_x[...] = (rest_x[...].astype(F32) + from_y[1].astype(F32)).astype(BF)


def reduce_second(state):
    own, rest_y, rest_x = state[:3]
    shapes = [of(*own.shape, dtype=F32), of(*rest_y.shape), of(*rest_x.shape)]
    out, last_y, last_x = local(second_kernel, "grad_second", shapes, *state)
    return [out, swap(last_y, 4), swap(last_x, 2)]


def joined_kernel(own, got_y, got_x, *outs):
    half = got_y.shape[0]
    at = 0
    for out in outs:
        rows = out.shape[-2] * (out.shape[0] if len(out.shape) == 3 else 1)
        value = own[at:at + rows, :]
        parts = []
        if at < half:
            parts.append(got_y[at:min(half, at + rows), :].astype(F32))
        if at + rows > half:
            parts.append(got_x[max(at, half) - half:at + rows - half, :].astype(F32))
        value = value + (parts[0] if len(parts) == 1 else jnp.concatenate(parts, axis=0))
        out[...] = value.astype(BF).reshape(out.shape)
        at += rows


def inward(value):
    return [value, lax.ppermute(value, "dp", [(0, 1), (3, 2)])]


def reduce_inward(state, chunks=1):
    rows, width = state[0].shape
    step = rows // chunks // 16 * 16
    sizes = [step] * (chunks - 1) + [rows - step * (chunks - 1)]
    values = local(joined_kernel, "grad_join", [of(size, width) for size in sizes], *state)
    return [inward(value) for value in values]


def pair_kernel(one, two, out):
    out[...] = (one[...].astype(F32) + two[...].astype(F32)).astype(BF)


def reduce_across(state):
    (side,) = local(pair_kernel, "grad_add", [of(*state[0].shape)], *state)
    return [side, lax.ppermute(side, "dp", [(1, 2), (2, 1)])]


def reduce_outward(state):
    (total,) = local(pair_kernel, "grad_add", [of(*state[0].shape)], *state)
    return [total, lax.ppermute(total, "dp", [(1, 0), (2, 3)])]


def exchange(value):
    return lax.all_to_all(value, "dp", 0, 0)


def reduce_quarters(state):
    rows, width = state[0].shape
    (value,) = local(joined_kernel, "grad_join", [of(4, rows // 4, width)], *state)
    return exchange(value)


def four_kernel(parts, out):
    total = parts[0].astype(F32) + parts[1].astype(F32) + parts[2].astype(F32) + parts[3].astype(F32)
    for index in range(4):
        out[index] = total.astype(BF)


def reduce_return(parts):
    (value,) = local(four_kernel, "grad_add", [of(*parts.shape)], parts)
    return exchange(value)


def place_kernel(spans, at_ref, *refs):
    count = len(refs) - 1 - len(spans)
    ins, outs, hold = refs[:count], refs[count:-1], refs[-1]
    at = at_ref[0]
    middle = (at == 1) | (at == 2)
    if count == 1:
        rows = ins[0].shape[1]
        for index in range(4):
            hold[index * rows:(index + 1) * rows, :] = ins[0][index].astype(F32)
    else:
        row = 0
        for total, came in zip(ins[::2], ins[1::2]):
            rows = total.shape[0]
            hold[row:row + rows, :] = jnp.where(middle, total[...].astype(F32), came[...].astype(F32))
            row += rows
    for (first, count, columns), out in zip(spans, outs):
        if len(out.shape) == 3:
            for index in range(out.shape[0]):
                out[index] = hold[first + index * out.shape[1]:first + (index + 1) * out.shape[1], :]
        else:
            for column in range(columns):
                begin = first + column * count
                out[:, column * hold.shape[1]:(column + 1) * hold.shape[1]] = hold[begin:begin + count, :]


def reduce_end(arrays, rows, spans, shapes):
    width = arrays[0].shape[-1]
    at = lax.axis_index("dp").astype(jnp.int32).reshape(1)
    return local(
        lambda *refs: place_kernel(spans, *refs), "grad_place", shapes, at, *arrays,
        scratch=[pltpu.VMEM((rows, width), F32)], scalars=1,
    )


def small_kernel(me_ref, early, back, late, self_b, cross_b, gain, shift, b_in, b_out):
    me = me_ref[0]
    width, part = early.shape[1], self_b.shape[1]
    turn = lax.rem(width - me * part, width)

    def own(ref, row):
        return pltpu.roll(ref[row // 8 * 8:row // 8 * 8 + 8, :], turn, 1)[row % 8:row % 8 + 1, :part]

    for ref, index in ((gain, 0), (shift, 1)):
        ref[0:1, :] = own(back, index)
        ref[1:2, :] = own(early, 3 + index)
        ref[2:3, :] = own(early, 1 + index)
    b_out[...] = own(early, 0)
    cross_b[0:1, :] = own(back, 8)
    cross_b[1:2, :] = own(back, 9)
    cross_b[2:3, :] = own(early, 5)
    self_b[0:1, :] = own(late, 0)
    self_b[1:2, :] = own(late, 1)
    self_b[2:3, :] = own(back, 2)
    wide = b_in.shape[1]
    row = early[pl.ds(6 + me * wide // width, 1), :]
    b_in[...] = jnp.where(lax.rem(me, 2) == 0, row[:, :wide], row[:, wide:])


def reduce_plain(sizes, blocks):
    value = lax.psum_scatter(blocks.astype(F32), "fsdp", scatter_dimension=0, tiled=False)
    return lax.psum(value.astype(BF), "dp").astype(F32)


def first_hops(shard):
    return swap(shard, 2), swap(shard, 4)


def pieces_of(shard, core, x, y, x_core, y_core, far, offsets=(0,)):
    rows = shard.shape[0]
    found = [((0, 0, rows), shard), ((1, 0, rows), core), ((2, 0, rows), x), ((4, 0, rows), y)]
    found += [((3, 0, rows), x_core), ((5, 0, rows), y_core)]
    for offset, piece in zip(offsets, far):
        found += [((6, offset, piece.shape[0]), piece), ((7, offset, piece.shape[0]), swap(piece, 1))]
    return found


def shards(sizes, target, memory, target_lengths, memory_lengths, self_qkv, self_bias, self_out, cross_qkv, cross_bias,
           cross_out, ffn_in, ffn_in_bias, ffn_out, ffn_out_bias, norm_gain, norm_bias, cotangent):
    n = sizes[0]
    fast = n == 8 and sizes[1] == 4
    width, hidden = target.shape[-1], ffn_in.shape[1]
    part, wide = width // n, hidden // n
    ratio = hidden // width
    x, mem, cot = target[0], memory[0], cotangent[0]
    place = lax.axis_index("fsdp").astype(jnp.int32)
    me = place.reshape(1)
    vectors = [self_bias, cross_bias, norm_gain, norm_bias, ffn_in_bias.reshape(ratio, part), ffn_out_bias.reshape(1, part)]

    if fast:
        owners = 8
        own = self_qkv.reshape(3 * part, width)
        half = halves(own.shape[0])
        s_x, s_y = first_hops(own)
        s_core = swap(own, 1)
        slabs = lax.all_to_all(pack(vectors, owners, width), "fsdp", 0, 0)
        c_one = cross_qkv.reshape(3 * part, width)
        c_two = jnp.concatenate([self_out, cross_out])
        c_one_core, c_two_core, f_in_core, f_out_core = [swap(member, 1) for member in (c_one, c_two, ffn_in, ffn_out)]
        s_x, s_y, s_core, c_one, c_two, c_one_core, c_two_core, f_in_core, f_out_core = tie(
            s_x, s_y, s_core, c_one, c_two, c_one_core, c_two_core, f_in_core, f_out_core
        )
        s_low, s_high = swap(s_y[:half], 2), swap(s_x[half:], 4)
        s_x_core, s_y_core = swap(s_x, 1), swap(s_y, 1)
        c_one_x, c_one_y = first_hops(c_one)
        c_two_x, c_two_y = first_hops(c_two)
        self_pieces = pieces_of(own, s_core, s_x, s_y, s_x_core, s_y_core, (s_low, s_high), (0, half))
    else:
        owners, me = 1, jnp.zeros((1,), jnp.int32)

        def gathered(member, axis):
            return lax.all_gather(member, "fsdp", axis=axis, tiled=True)

        def single(value):
            return [((0, 0, value.shape[0]), value)]

        fulls = [gathered(member, 1) for member in vectors[:4]]
        fulls += [gathered(ffn_in_bias, 0).reshape(ratio, width), gathered(ffn_out_bias, 0).reshape(1, width)]
        fulls = jnp.concatenate(fulls)
        slabs = jnp.pad(fulls, ((0, SLAB - fulls.shape[0]), (0, 0)))[None]
        self_pieces = single(gathered(self_qkv, 1).reshape(3 * width, width))
        ones = single(gathered(cross_qkv, 1).reshape(3 * width, width))
        twos = single(jnp.concatenate([gathered(self_out, 0), gathered(cross_out, 0)]))
        in_pieces, out_pieces = single(gathered(ffn_in, 0)), single(gathered(ffn_out, 0))

    pairs = width // PAIR
    early_pairs, late_pairs = (0, pairs // 2), (pairs // 2, pairs)
    self_w, vec, q, k, v = project(me, x, slabs, self_pieces, owners)
    if fast:
        q, c_one_x, c_one_y, c_two_x, c_two_y = tie(q, c_one_x, c_one_y, c_two_x, c_two_y)
        c_one_far, c_two_far = swap(c_one_y, 2), swap(c_two_x, 4)
        c_cores = [swap(member, 1) for member in (c_one_x, c_one_y, c_two_x)]
    o, lse = attend_forward(q, k, v, target_lengths, True)
    if fast:
        o, c_one_far, c_two_far, f_in, f_out, *c_cores = tie(o, c_one_far, c_two_far, ffn_in, ffn_out, *c_cores)
        ones = pieces_of(c_one, c_one_core, c_one_x, c_one_y, c_cores[0], c_cores[1], (c_one_far,))
        twos = pieces_of(c_two, c_two_core, c_two_x, c_two_y, c_cores[2], swap(c_two_y, 1), (c_two_far,))
        f_in_x, f_in_y = first_hops(f_in)
        f_out_x, f_out_y = first_hops(f_out)
    cross_w, out_w, z_one, r_one, h_one, q2, k2, v2 = between(me, vec, o, x, mem, ones, twos, owners)
    half_one = attend_forward(q2, k2, v2, memory_lengths, False, early_pairs)
    if fast:
        q2, f_in_x, f_in_y, *half_one = tie(q2, f_in_x, f_in_y, *half_one)
        f_in_far = swap(f_in_y, 2)
        f_in_x_core, f_in_y_core = swap(f_in_x, 1), swap(f_in_y, 1)
    o2, lse2 = attend_forward(q2, k2, v2, memory_lengths, False, late_pairs, half_one)
    if fast:
        o2, f_in_far, f_out_x, f_out_y, f_in_x_core, f_in_y_core = tie(
            o2, f_in_far, f_out_x, f_out_y, f_in_x_core, f_in_y_core
        )
        f_half = halves(f_out.shape[0])
        f_out_low, f_out_high = swap(f_out_y[:f_half], 2), swap(f_out_x[f_half:], 4)
        in_pieces = pieces_of(f_in, f_in_core, f_in_x, f_in_y, f_in_x_core, f_in_y_core, (f_in_far,))
        out_pieces = pieces_of(
            f_out, f_out_core, f_out_x, f_out_y, swap(f_out_x, 1), swap(f_out_y, 1), (f_out_low, f_out_high), (0, f_half)
        )
    mixed, act, da, df, h_two, dy, db2, do2, ffn_sums = ffn(
        me, vec, o2, z_one, cot, out_w, in_pieces, out_pieces, hidden
    )
    if fast:
        out_state = reduce_core(*tall_grad(me, act, df, "ffn_out_grad"))
        h_two, out_state[0] = tie(h_two, out_state[0])
        operands, chunks = [h_two, da, o2, db2], [(0, 0)] + [(1, c) for c in range(ratio)] + [(2, 0), (3, 0)]
        items = [(0, 1 + c, 1.0) for c in range(ratio)] + [(1 + ratio, 2 + ratio, 1.0)]
        in_state = reduce_core(*weight_grad(me, operands, chunks, items, "ffn_in_grad", (ffn_sums,), SLAB // 2))
        do2, *out_state = tie(do2, *out_state)
        out_state = reduce_first(out_state)
        do2, in_state[0], out_state[0] = tie(do2, in_state[0], out_state[0])
    grads = attend_backward(q2, k2, v2, o2, do2, lse2, memory_lengths, False, early_pairs)
    if fast:
        do2, *states = tie(do2, *grads, *out_state, *in_state)
        grads, out_state, in_state = states[:4], reduce_second(states[4:9]), reduce_first(states[9:])
        do2, out_state[0], in_state[0] = tie(do2, out_state[0], in_state[0])
    dq2, dk2, dv2, cross_sums = attend_backward(q2, k2, v2, o2, do2, lse2, memory_lengths, False, late_pairs, grads)
    if fast:
        dq2, *states = tie(dq2, *out_state, *in_state)
        (out_state,), in_state = reduce_inward(states[:3]), reduce_second(states[3:])
        dq2, out_state[0], in_state[0] = tie(dq2, out_state[0], in_state[0])
    dy_one, db, do, back_sums = cross_back(vec, dq2, dy, z_one, r_one, cross_w, out_w)
    if fast:
        operands = [h_one, dq2, mem, dk2, dv2, o, db]
        chunks = [(at, 0) for at in range(7)]
        items = [(0, 1, FACTOR), (2, 3, 1.0), (2, 4, 1.0), (5, 6, 1.0)]
        cross_state = reduce_core(
            *weight_grad(me, operands, chunks, items, "cross_grad", (back_sums, cross_sums), SLAB // 2)
        )
        do, *states = tie(do, *out_state, *in_state, cross_state[0])
        out_state, (in_state,), cross_state[0] = reduce_across(states[:2]), reduce_inward(states[2:5]), states[5]
        do, out_state[0], in_state[0] = tie(do, out_state[0], in_state[0])
    grads = attend_backward(q, k, v, o, do, lse, target_lengths, True, early_pairs)
    if fast:
        do, *states = tie(do, *grads, *out_state, *in_state, *cross_state)
        grads, out_state, in_state = states[:4], reduce_outward(states[4:6]), reduce_across(states[6:8])
        cross_state = reduce_first(states[8:])
        do, out_state[0], in_state[0], cross_state[0] = tie(do, out_state[0], in_state[0], cross_state[0])
    dq, dk, dv, self_sums = attend_backward(q, k, v, o, do, lse, target_lengths, True, late_pairs, grads)
    if fast:
        chunks = [(at, 0) for at in range(4)]
        items = [(0, 1, FACTOR), (0, 2, 1.0), (0, 3, 1.0)]
        self_state = reduce_core(*weight_grad(me, [x, dq, dk, dv], chunks, items, "self_grad", (self_sums,), SLAB))
        dq, *states = tie(dq, *out_state, *in_state, *cross_state, self_state[0])
        out_state, in_state, cross_state = states[:2], reduce_outward(states[2:4]), reduce_second(states[4:9])
        dq, in_state[0], cross_state[0], self_state[0] = tie(dq, in_state[0], cross_state[0], states[9])
    d_target = self_back(dq, dk, dv, dy_one, self_w)
    if fast:
        d_target, dk2, *states = tie(d_target, dk2, *self_state, *cross_state)
        self_state, cross_chunks = reduce_first(states[:2]), reduce_inward(states[2:], 2)
        dk2, self_state[0], cross_chunks[0][0] = tie(dk2, self_state[0], cross_chunks[0][0])
    d_memory = memory_back(dk2, dv2, cross_w)

    if fast:
        f32 = dict(dtype=F32)
        states = tie(d_memory, *self_state, *cross_chunks[0], *cross_chunks[1])
        d_memory, self_state = states[0], reduce_second(states[1:6])
        cross_chunks = [reduce_across(states[6:8]), reduce_across(states[8:10])]
        states = tie(*self_state, *cross_chunks[0], *cross_chunks[1], *out_state, *in_state)
        self_parts = reduce_quarters(states[:3])
        cross_chunks = [reduce_outward(states[3:5]), reduce_outward(states[5:7])]
        out_state, in_state = states[7:9], states[9:11]
        (out_sum,) = reduce_end(out_state, wide, [(0, wide, 1)], [of(wide, width, **f32)])
        in_sum, cross_o_sum, early = reduce_end(
            in_state, in_state[0].shape[0], [(0, part, ratio), (wide, part, 1), (wide + part, SLAB // 2, 1)],
            [of(part, hidden, **f32), of(part, width, **f32), of(SLAB // 2, width, **f32)],
        )
        states = tie(self_parts, out_sum, in_sum, *cross_chunks[0], *cross_chunks[1])
        self_parts, out_sum, in_sum = reduce_return(states[0]), states[1], states[2]
        rows = sum(chunk[0].shape[0] for chunk in cross_chunks)
        cross_w_sum, self_o_sum, back = reduce_end(
            states[3:], rows, [(0, 0, 0), (3 * part, part, 1), (4 * part, SLAB // 2, 1)],
            [of(3, part, width, **f32), of(part, width, **f32), of(SLAB // 2, width, **f32)],
        )
        self_w_sum, late = reduce_end(
            [self_parts], 3 * part + SLAB, [(0, 0, 0), (3 * part, SLAB, 1)],
            [of(3, part, width, **f32), of(SLAB, width, **f32)],
        )
        shapes = [of(3, part, **f32)] * 4 + [of(1, wide, **f32), of(1, part, **f32)]
        self_b, cross_b, gain, shift, b_in, b_out = local(small_kernel, "small_grads", shapes, me, early, back, late, scalars=1)
        b_in, b_out = b_in[0], b_out[0]
    else:
        def whole(left, right, scale=1.0):
            return reduce_plain(sizes, (dot_tn(left, right) * scale).reshape(n, left.shape[1] // n, right.shape[1]))

        def mine(rows, size):
            rows = rows.reshape(-1, n * size)
            return lax.dynamic_slice(rows, (0, place * size), (rows.shape[0], size))

        self_w_sum = jnp.stack([whole(x, dq, FACTOR), whole(x, dk), whole(x, dv)])
        cross_w_sum = jnp.stack([whole(h_one, dq2, FACTOR), whole(mem, dk2), whole(mem, dv2)])
        cross_o_sum, self_o_sum = whole(o2, db2), whole(o, db)
        in_sum, out_sum = whole(h_two, da), whole(act, df)
        sums = lax.psum(jnp.concatenate([ffn_sums, back_sums, cross_sums, self_sums]), ("fsdp", "dp"))
        narrow = mine(sums, part)
        self_b = jnp.stack([narrow[32], narrow[33], narrow[18]])
        cross_b = jnp.stack([narrow[24], narrow[25], narrow[5]])
        gain = jnp.stack([narrow[16], narrow[3], narrow[1]])
        shift = jnp.stack([narrow[17], narrow[4], narrow[2]])
        b_in, b_out = mine(sums[6:10], wide)[0], narrow[0]
    return (
        mixed[None], d_target[None], d_memory[None], self_w_sum, self_b, self_o_sum, cross_w_sum, cross_b, cross_o_sum,
        in_sum, b_in, out_sum, b_out, gain, shift,
    )


def solution(mesh):
    rows = P(("fsdp", "dp"), None, None)
    row = P(("fsdp", "dp"))
    stacked, vectors, matrix, vector = P(None, "fsdp", None), P(None, "fsdp"), P("fsdp", None), P("fsdp")
    weights = (stacked, vectors, matrix, stacked, vectors, matrix, matrix, vector, matrix, vector, vectors, vectors)
    sizes = (mesh.shape["fsdp"], mesh.shape["dp"])
    return jax.shard_map(
        lambda *args: shards(sizes, *args),
        mesh=mesh,
        in_specs=(rows, rows, row, row) + weights + (rows,),
        out_specs=(rows, rows, rows) + weights,
        check_vma=False,
    )
```

```python
import jax
import jax.numpy as jnp
from jax import lax
from jax.experimental import pallas as pl
from jax.experimental.pallas import tpu as pltpu
from jax.sharding import PartitionSpec as P

HDIM = 64
PAIR = 2 * HDIM
BLOCK = 256
ROWS = 256
ATTEND_VMEM = 20
MASKED = -1e30
FACTOR = HDIM ** (-0.5)
BF = jnp.bfloat16
F32 = jnp.float32


def dot_nn(a, b):
    return lax.dot_general(a, b, (((1,), (0,)), ((), ())), preferred_element_type=F32)


def dot_nt(a, b):
    return lax.dot_general(a, b, (((1,), (1,)), ((), ())), preferred_element_type=F32)


def dot_tn(a, b):
    return lax.dot_general(a, b, (((0,), (0,)), ((), ())), preferred_element_type=F32)


def column_sum(values):
    return jnp.sum(values.astype(F32), axis=0, keepdims=True)


def head_lanes(head):
    lane = lax.broadcasted_iota(jnp.int32, (1, PAIR), 1)
    return (lane // HDIM) == head, lane == (HDIM if head == 0 else 0)


def pick(mask, yes, no, shape):
    return jnp.where(jnp.broadcast_to(mask, shape), yes, no)


def length_bias(count, limit):
    positions = lax.broadcasted_iota(jnp.int32, (count, PAIR), 0)
    return jnp.where(positions < limit, 0.0, MASKED).astype(F32)


def causal_edge(values, fill):
    key_at = lax.broadcasted_iota(jnp.int32, values.shape, 0)
    query_at = lax.broadcasted_iota(jnp.int32, values.shape, 1)
    return jnp.where(key_at <= query_at, values, fill)


def attend_forward_kernel(causal, limit_ref, q_ref, k_ref, v_ref, o_ref, lse_ref):
    count, sources = q_ref.shape[0], k_ref.shape[0]
    k_all, v_all = k_ref[...].astype(F32), v_ref[...].astype(F32)
    bias = length_bias(sources, limit_ref[0])
    keys, values = [], []
    for head in range(2):
        own, spare = head_lanes(head)
        keys.append(pick(spare, bias, k_all, k_all.shape).astype(BF))
        ones = pick(spare, 1.0, 0.0, v_all.shape)
        values.append(pick(own, v_all, ones, v_all.shape).T.astype(BF))

    def scores_of(unit):
        block, head = unit
        rows = slice(block * BLOCK, (block + 1) * BLOCK)
        extent = (block + 1) * BLOCK if causal else sources
        own, spare = head_lanes(head)
        q_block = q_ref[rows, :].astype(F32)
        ones = pick(spare, 1.0, 0.0, q_block.shape)
        scores = dot_nt(keys[head][:extent], pick(own, q_block, ones, q_block.shape).astype(BF))
        if causal:
            edge = causal_edge(scores[extent - BLOCK:], MASKED)
            scores = edge if extent == BLOCK else jnp.concatenate([scores[: extent - BLOCK], edge], axis=0)
        return scores

    parts = {}

    def finish(unit, expo, highest):
        block, head = unit
        rows = slice(block * BLOCK, (block + 1) * BLOCK)
        mixed = dot_nn(values[head][:, : expo.shape[0]], expo)
        at = HDIM if head == 0 else 0
        total = mixed[at:at + 1]
        lse_ref[0, head:head + 1, rows] = highest + jnp.log(total)
        parts[unit] = mixed[head * HDIM:(head + 1) * HDIM] * (1.0 / total)
        if head == 1:
            o_ref[rows, :] = jnp.concatenate([parts[(block, 0)], parts[unit]], axis=0).T.astype(BF)

    units = [(block, head) for block in range(count // BLOCK) for head in range(2)]
    ahead = [scores_of(unit) for unit in units[:2]]
    before = None
    for at, unit in enumerate(units):
        if at + 2 < len(units):
            ahead.append(scores_of(units[at + 2]))
        highest = jnp.max(ahead[at], axis=0, keepdims=True)
        expo = jnp.exp(ahead[at] - highest).astype(BF)
        if before is not None:
            finish(*before)
        before = (unit, expo, highest)
    finish(*before)


def attend_backward_kernel(
    causal, limit_ref, q_ref, k_ref, v_ref, o_ref, do_ref, lse_ref, dq_ref, dk_ref, dv_ref, sums_ref, dq_acc
):
    count, sources = q_ref.shape[0], k_ref.shape[0]
    q_all, k_all = q_ref[...].astype(F32), k_ref[...].astype(F32)
    do_all = do_ref[...].astype(F32)
    bias = length_bias(sources, limit_ref[0])
    product = (do_all * o_ref[...].astype(F32)).T
    q_aug, q_own, k_aug, kt_own, do_own, delta, lse = [], [], [], [], [], [], []
    for head in range(2):
        own, spare = head_lanes(head)
        q_aug.append(pick(own, q_all, pick(spare, 1.0, 0.0, q_all.shape), q_all.shape).astype(BF))
        q_own.append(pick(own, q_all, 0.0, q_all.shape).astype(BF))
        k_aug.append(pick(spare, bias, k_all, k_all.shape).astype(BF))
        kt_own.append(pick(own, k_all, 0.0, k_all.shape).T.astype(BF))
        do_own.append(pick(own, do_all, 0.0, do_all.shape).astype(BF))
        delta.append(jnp.sum(product[head * HDIM:(head + 1) * HDIM], axis=0, keepdims=True))
        lse.append(lse_ref[0, head:head + 1, :])

    def products(unit):
        block, head = unit
        rows = slice(block * BLOCK, (block + 1) * BLOCK)
        first = block * BLOCK if causal else 0
        return (
            dot_nt(k_aug[head][rows], q_aug[head][first:]),
            dot_nt(v_ref[rows, :], do_own[head][first:]),
        )

    def gradients(unit, scores, d_probs):
        block, head = unit
        first = block * BLOCK if causal else 0
        probs = jnp.exp(scores - lse[head][:, first:])
        if causal:
            edge = causal_edge(probs[:, :BLOCK], 0.0)
            probs = edge if first + BLOCK == count else jnp.concatenate([edge, probs[:, BLOCK:]], axis=1)
        d_scores = (probs * (d_probs - delta[head][:, first:])).astype(BF)
        return probs.astype(BF), d_scores

    held = {}

    def finish(unit, probs, d_scores):
        block, head = unit
        rows = slice(block * BLOCK, (block + 1) * BLOCK)
        first = block * BLOCK if causal else 0
        dv = dot_nn(probs, do_own[head][first:])
        dk = dot_nn(d_scores, q_own[head][first:])
        dq = dot_nn(kt_own[head][:, rows], d_scores)
        if head == 0:
            held[block] = (dv, dk, dq)
            return
        dv = (held[block][0] + dv).astype(BF)
        dv_ref[rows, :] = dv
        held["dv"] = held.get("dv", 0.0) + column_sum(dv)
        dk_ref[rows, :] = (held[block][1] + dk).astype(BF)
        if block == 0:
            dq_acc[...] = held[block][2] + dq
        else:
            dq_acc[:, first:] += held[block][2] + dq

    units = [(block, head) for block in range(sources // BLOCK) for head in range(2)]
    ahead = [products(units[0])]
    before = None
    for at, unit in enumerate(units):
        if at + 1 < len(units):
            ahead.append(products(units[at + 1]))
        current = (unit,) + gradients(unit, *ahead[at])
        if before is not None:
            finish(*before)
        before = current
    finish(*before)
    dq = dq_acc[...].T.astype(BF)
    dq_ref[...] = dq
    sums_ref[...] = jnp.concatenate([column_sum(dq) * FACTOR, held["dv"], jnp.zeros((6, PAIR), F32)], axis=0)


def attend_call(kernel, name, causal, work, specs, arrays, out_specs, outs, scratch, limit, pairs, held):
    first, last = pairs
    held = list(held)

    def shifted(spec):
        if spec is None:
            return pl.BlockSpec(memory_space=pltpu.SMEM)
        shape, index = spec
        return pl.BlockSpec(shape, lambda i: index(i + first))

    def body(*refs):
        kernel(causal, *refs[: len(specs)], *refs[len(specs) + len(held):])

    return pl.pallas_call(
        body,
        grid=(last - first,),
        in_specs=[shifted(spec) for spec in specs] + [pl.BlockSpec(memory_space=pl.ANY)] * len(held),
        out_specs=[shifted(spec) for spec in out_specs],
        out_shape=outs,
        scratch_shapes=scratch,
        input_output_aliases={len(specs) + at: at for at in range(len(held))},
        compiler_params=pltpu.CompilerParams(vmem_limit_bytes=limit << 20),
        cost_estimate=pl.CostEstimate(flops=8 * work * (last - first) * PAIR, bytes_accessed=1 << 20, transcendentals=0),
        name=name,
    )(*arrays, *held)


def attend_forward(q, k, v, limit, causal, pairs=None, held=()):
    count, width = q.shape
    sources = k.shape[0]
    total = width // PAIR
    of_q = ((count, PAIR), lambda i: (0, i))
    of_k = ((sources, PAIR), lambda i: (0, i))
    stats = ((1, 2, count), lambda i: (i, 0, 0))
    outs = [jax.ShapeDtypeStruct((count, width), BF), jax.ShapeDtypeStruct((total, 2, count), F32)]
    return attend_call(
        attend_forward_kernel, "attend_forward", causal, 16 * count * sources * (5 if causal else 8) // 8,
        [None, of_q, of_k, of_k], [limit, q, k, v], [of_q, stats], outs, [], ATTEND_VMEM, pairs or (0, total), held,
    )


def attend_backward(q, k, v, o, do, lse, limit, causal, pairs=None, held=(), memory=ATTEND_VMEM):
    count, width = q.shape
    sources = k.shape[0]
    total = width // PAIR
    of_q = ((count, PAIR), lambda i: (0, i))
    of_k = ((sources, PAIR), lambda i: (0, i))
    stats = ((1, 2, count), lambda i: (i, 0, 0))
    outs = [
        jax.ShapeDtypeStruct((count, width), BF),
        jax.ShapeDtypeStruct((sources, width), BF),
        jax.ShapeDtypeStruct((sources, width), BF),
        jax.ShapeDtypeStruct((8, width), F32),
    ]
    return attend_call(
        attend_backward_kernel, "attend_backward", causal, 40 * count * sources * (5 if causal else 8) // 8,
        [None, of_q, of_k, of_k, of_q, of_q, stats], [limit, q, k, v, o, do, lse],
        [of_q, of_k, of_k, ((8, PAIR), lambda i: (0, i))], outs, [pltpu.VMEM((PAIR, count), F32)], memory,
        pairs or (0, total), held,
    )


WHOLE = pl.BlockSpec(memory_space=pltpu.VMEM)
DENSE_VMEM = 32
FFN_VMEM = 48
GRAD_VMEM = 56
SMALL_VMEM = 16
LARGE_VMEM = 58
ANYWHERE = pl.BlockSpec(memory_space=pl.ANY)
SCALAR = pl.BlockSpec(memory_space=pltpu.SMEM)
SLAB = 32


def params(limit):
    return pltpu.CompilerParams(vmem_limit_bytes=limit << 20)


def full(value):
    shape = tuple(value.shape)
    return pl.BlockSpec(shape, lambda *_: (0,) * len(shape), pipeline_mode=pl.Buffered(1))


def cost(flops, *arrays):
    size = sum(a.size * a.dtype.itemsize for a in arrays)
    return pl.CostEstimate(flops=8 * flops, bytes_accessed=size, transcendentals=0)


def of(*shape, dtype=BF):
    return jax.ShapeDtypeStruct(shape, dtype)


def matrix(bundle, index):
    owners, width = bundle.shape[0], bundle.shape[2]
    part = width // owners
    return bundle[:, index * part:(index + 1) * part, :].reshape(width, width)


def bring(refs, holds, sem):
    copies = [pltpu.make_async_copy(ref, hold, sem.at[at]) for at, (ref, hold) in enumerate(zip(refs, holds))]
    for copy in copies:
        copy.start()
    return copies


def one_matrix(bundle, index):
    owners, width = bundle.shape[0], bundle.shape[2]
    return pl.BlockSpec((owners, width // owners, width), lambda *_: (0, index, 0), pipeline_mode=pl.Buffered(1))


def fetch(me, pieces, bundle, sem, first):
    copies = []
    shard = max(offset + rows for (_, offset, rows), _ in pieces)
    for at, ((relative, offset, rows), piece) in enumerate(pieces):
        owner = jnp.bitwise_xor(me, relative)
        if len(bundle.shape) == 3:
            target = bundle.at[owner, pl.ds(offset, rows)]
        else:
            target = bundle.at[pl.ds(pl.multiple_of(owner * shard + offset, 16), rows)]
        copies.append(pltpu.make_async_copy(piece, target, sem.at[first + at]))
        copies[-1].start()
    return copies


def wait_all(copies):
    for copy in copies:
        copy.wait()


def leave(inside, outside, sem, at):
    return pltpu.make_async_copy(inside, outside, sem.at[at])


def at_first(action):
    pl.when(pl.program_id(0) == 0)(action)


def at_last(action):
    pl.when(pl.program_id(0) == pl.num_programs(0) - 1)(action)


def normalise(summed):
    centred = summed - jnp.mean(summed, axis=-1, keepdims=True)
    inverse = lax.rsqrt(jnp.mean(centred * centred, axis=-1, keepdims=True) + 1e-05)
    return centred * inverse, inverse


def norm_backward(d_out, normed, inverse, gain):
    d_normed = d_out * gain
    return inverse * (
        d_normed
        - jnp.mean(d_normed, axis=-1, keepdims=True)
        - normed * jnp.mean(d_normed * normed, axis=-1, keepdims=True)
    )


def gelu_parts(a):
    bell = jnp.exp(-0.5 * a * a)
    t = 1.0 / (1.0 + 0.23164189 * jnp.abs(a))
    tail = t * (0.127414796 + t * (-0.142248368 + t * (0.7107068705 + t * (-0.7265760135 + t * 0.5307027145)))) * bell
    phi = jnp.where(a >= 0.0, 1.0 - tail, tail)
    return a * phi, phi + a * bell * 0.3989422804014327


def add_rows(ref, rows):
    block = jnp.concatenate(rows + [jnp.zeros((ref.shape[0] - len(rows), ref.shape[1]), F32)], axis=0)

    @pl.when(pl.program_id(0) == 0)
    def _():
        ref[...] = block

    @pl.when(pl.program_id(0) > 0)
    def _():
        ref[...] += block


def pack_kernel(matrix_ref, *refs):
    count = (len(refs) - 3) // 2
    vectors, out, holds, slab, sem = refs[:count], refs[count], refs[count + 1:-2], refs[-2], refs[-1]
    rows = matrix_ref.shape[0]
    whole = pltpu.make_async_copy(matrix_ref, out.at[pl.ds(0, rows)], sem.at[count])
    whole.start()
    copies = bring(vectors, holds, sem)
    slab[...] = jnp.zeros(slab.shape, F32)
    row = 0
    for copy, hold in zip(copies, holds):
        copy.wait()
        slab[row:row + hold.shape[0], : hold.shape[1]] = hold[...].astype(F32)
        row += hold.shape[0]
    out[rows:, :] = slab[...].astype(BF)
    whole.wait()


def pack(value, vectors):
    rows, width = value.shape
    total = rows + SLAB // 2
    return pl.pallas_call(
        pack_kernel,
        grid=(1,),
        in_specs=[ANYWHERE] * (1 + len(vectors)),
        out_specs=full(of(total, width)),
        out_shape=of(total, width),
        scratch_shapes=[pltpu.VMEM(vector.shape, BF) for vector in vectors] + [
            pltpu.VMEM((SLAB // 2, width), F32), pltpu.SemaphoreType.DMA((len(vectors) + 1,)),
        ],
        compiler_params=params(LARGE_VMEM),
        name="pack_self",
    )(value, *vectors)


def project_kernel(layout, me_ref, x, *refs):
    pieces, (w_out, vec, q_ref, k_ref, v_ref, w, sem) = refs[: len(layout)], refs[len(layout):]
    owners, width = w.shape[0], w.shape[2]
    part = width // owners

    @at_first
    def _():
        wait_all(fetch(me_ref[0], list(zip(layout, pieces)), w, sem, 0))
        leave(w, w_out, sem, len(layout)).start()
        vec[...] = jnp.zeros(vec.shape, F32)
        if owners == 1:
            vec[:17, :] = w[0, 3 * part:, :].astype(F32)[:17, :]
        else:
            wide = 4 * width // owners
            for owner in range(owners):
                slab = w[owner, 3 * part:, :].astype(F32)
                vec[:12, owner * part:(owner + 1) * part] = slab[:12, :part]
                vec[16:17, owner * part:(owner + 1) * part] = slab[13:14, :part]
                at = owner * wide
                vec[12 + at // width:13 + at // width, at % width:at % width + wide] = slab[12:13, :wide]

    values = x[...]
    q_ref[...] = ((dot_nn(values, matrix(w, 0)) + vec[0:1, :]) * FACTOR).astype(BF)
    k_ref[...] = dot_nn(values, matrix(w, 1)).astype(BF)
    v_ref[...] = (dot_nn(values, matrix(w, 2)) + vec[1:2, :]).astype(BF)
    at_last(lambda: leave(w, w_out, sem, len(layout)).wait())


def project(me, x, pieces, owners):
    count, width = x.shape
    rows = pl.BlockSpec((ROWS, width), lambda i: (i, 0))
    layout = [key for key, _ in pieces]
    bundle = (owners, max(offset + size for _, offset, size in layout), width)
    return pl.pallas_call(
        lambda *refs: project_kernel(layout, *refs),
        grid=(count // ROWS,),
        in_specs=[SCALAR, rows] + [ANYWHERE] * len(pieces),
        out_specs=[ANYWHERE, full(of(24, width)), rows, rows, rows],
        out_shape=[of(*bundle), of(24, width, dtype=F32)] + [of(count, width)] * 3,
        scratch_shapes=[
            pltpu.VMEM(bundle, BF),
            pltpu.SemaphoreType.DMA((len(pieces) + 1,)),
        ],
        compiler_params=params(DENSE_VMEM),
        cost_estimate=cost(6 * count * width * width, x, x, x, x, x),
        name="self_project",
    )(me, x, *[piece for _, piece in pieces])


def between_kernel(layout, me_ref, vec, o, x, mem, *refs):
    pieces, (w_out, z_ref, r_ref, h_ref, q_ref, k_ref, v_ref, w, sem) = refs[: len(layout)], refs[len(layout):]

    @at_first
    def _():
        wait_all(fetch(me_ref[0], list(zip(layout, pieces)), w, sem, 0))
        leave(w, w_out, sem, len(layout)).start()

    summed = x[...].astype(F32) + dot_nn(o[...], matrix(w, 3)) + vec[2:3, :]
    source = mem[...]
    k_ref[...] = dot_nn(source, matrix(w, 1)).astype(BF)
    v_ref[...] = (dot_nn(source, matrix(w, 2)) + vec[4:5, :]).astype(BF)
    z, r = normalise(summed)
    z_ref[...] = z
    r_ref[...] = jnp.broadcast_to(r, r_ref.shape)
    hidden = (z * vec[6:7, :] + vec[9:10, :]).astype(BF)
    h_ref[...] = hidden
    q_ref[...] = ((dot_nn(hidden, matrix(w, 0)) + vec[3:4, :]) * FACTOR).astype(BF)
    at_last(lambda: leave(w, w_out, sem, len(layout)).wait())


def between(me, vec, o, x, mem, pieces, owners):
    count, width = x.shape
    rows = pl.BlockSpec((ROWS, width), lambda i: (i, 0))
    layout = [key for key, _ in pieces]
    bundle = (owners, 5 * width // owners, width)
    return pl.pallas_call(
        lambda *refs: between_kernel(layout, *refs),
        grid=(count // ROWS,),
        in_specs=[SCALAR, full(vec), rows, rows, rows] + [ANYWHERE] * len(pieces),
        out_specs=[ANYWHERE, rows, pl.BlockSpec((ROWS, 128), lambda i: (i, 0))] + [rows] * 4,
        out_shape=[of(*bundle), of(count, width, dtype=F32), of(count, 128, dtype=F32)] + [of(count, width)] * 4,
        scratch_shapes=[pltpu.VMEM(bundle, BF), pltpu.SemaphoreType.DMA((len(pieces) + 1,))],
        compiler_params=params(DENSE_VMEM),
        cost_estimate=cost(8 * count * width * width, x, x, x, x, x, x, x, x, x),
        name="self_out_cross_project",
    )(me, vec, o, x, mem, *[piece for _, piece in pieces])


def ffn_kernel(layouts, me_ref, vec, o, z_in, cot, wo, *refs):
    count = len(layouts[0])
    ins, outs = refs[:count], refs[count:count + len(layouts[1])]
    (mixed, act_ref, da_ref, df_ref, h_ref, dy_ref, db_ref, do_ref, sums_ref, w_in, w_out, slope, sem) = (
        refs[count + len(layouts[1]):]
    )
    width = o.shape[1]
    chunks = w_in.shape[1] // width
    in_copies = list(zip(layouts[0], ins)), list(zip(layouts[1], outs))

    @at_first
    def _():
        copies = fetch(me_ref[0], in_copies[0], w_in, sem, 0) + fetch(me_ref[0], in_copies[1], w_out, sem, count)
        wait_all(copies)

    gains = [vec[6 + i:7 + i, :] for i in range(3)]
    shifts = [vec[9 + i:10 + i, :] for i in range(3)]
    first = z_in[...] * gains[0] + shifts[0]
    z_two, r_two = normalise(first + dot_nn(o[...], matrix(wo, 0)) + vec[5:6, :])
    second = z_two * gains[1] + shifts[1]
    hidden = second.astype(BF)
    h_ref[...] = hidden

    def columns(c):
        return slice(c * width, (c + 1) * width)

    total = second + vec[16:17, :]
    ahead = dot_nn(hidden, w_in[:, columns(0)])
    before = None
    for c in range(chunks):
        pre = ahead + vec[12 + c:13 + c, :]
        if c + 1 < chunks:
            ahead = dot_nn(hidden, w_in[:, columns(c + 1)])
        act, grad = gelu_parts(pre)
        act = act.astype(BF)
        act_ref[:, columns(c)] = act
        slope[:, columns(c)] = grad
        if before is not None:
            total = total + dot_nn(before, w_out[columns(c - 1), :])
        before = act
    total = total + dot_nn(before, w_out[columns(chunks - 1), :])
    z, r = normalise(total)
    mixed[...] = (z * gains[2] + shifts[2]).astype(BF)
    incoming = cot[...].astype(F32)
    dy_three = norm_backward(incoming, z, r, gains[2])
    df = dy_three.astype(BF)
    df_ref[...] = df
    rows = [column_sum(df), column_sum(incoming * z), column_sum(incoming)]

    da_sums = []
    d_two = dy_three
    ahead = dot_nt(df, w_out[columns(0), :])
    before = None
    for c in range(chunks):
        d_act = ahead
        if c + 1 < chunks:
            ahead = dot_nt(df, w_out[columns(c + 1), :])
        da = (d_act * slope[:, columns(c)]).astype(BF)
        da_ref[:, columns(c)] = da
        da_sums.append(column_sum(da))
        if before is not None:
            d_two = d_two + dot_nt(before, w_in[:, columns(c - 1)])
        before = da
    d_two = d_two + dot_nt(before, w_in[:, columns(chunks - 1)])
    dy_two = norm_backward(d_two, z_two, r_two, gains[1])
    dy_ref[...] = dy_two
    db = dy_two.astype(BF)
    db_ref[...] = db
    do_ref[...] = dot_nt(db, matrix(wo, 0)).astype(BF)
    rows += [column_sum(d_two * z_two), column_sum(d_two), column_sum(db)]
    add_rows(sums_ref, rows + da_sums)


def ffn(me, vec, o, z, cot, wo, ins, outs, hidden):
    count, width = o.shape
    rows = pl.BlockSpec((ROWS, width), lambda i: (i, 0))
    wide = pl.BlockSpec((ROWS, hidden), lambda i: (i, 0))
    layouts = [key for key, _ in ins], [key for key, _ in outs]
    return pl.pallas_call(
        lambda *refs: ffn_kernel(layouts, *refs),
        grid=(count // ROWS,),
        in_specs=[SCALAR, full(vec), rows, rows, rows, one_matrix(wo, 4)] + [ANYWHERE] * (len(ins) + len(outs)),
        out_specs=[rows, wide, wide, rows, rows, rows, rows, rows, pl.BlockSpec((16, width), lambda i: (0, 0))],
        out_shape=[
            of(count, width), of(count, hidden), of(count, hidden), of(count, width), of(count, width),
            of(count, width, dtype=F32), of(count, width), of(count, width), of(16, width, dtype=F32),
        ],
        scratch_shapes=[
            pltpu.VMEM((width, hidden), BF),
            pltpu.VMEM((hidden, width), BF),
            pltpu.VMEM((ROWS, hidden), F32),
            pltpu.SemaphoreType.DMA((len(ins) + len(outs),)),
        ],
        compiler_params=params(FFN_VMEM),
        cost_estimate=cost(8 * count * width * hidden + 4 * count * width * width, o, z, z, cot, o, o, o, o),
        name="ffn",
    )(me, vec, o, z, cot, wo, *[piece for _, piece in ins + outs])


def cross_back_kernel(vec, dq, dy, z, r, w, wo, dy_ref, db_ref, do_ref, sums_ref):
    d_one = dy[...] + dot_nt(dq[...], matrix(w, 0)) * FACTOR
    normed = z[...]
    dy_one = norm_backward(d_one, normed, r[:, :1], vec[6:7, :])
    dy_ref[...] = dy_one
    db = dy_one.astype(BF)
    db_ref[...] = db
    do_ref[...] = dot_nt(db, matrix(wo, 0)).astype(BF)
    add_rows(sums_ref, [column_sum(d_one * normed), column_sum(d_one), column_sum(db)])


def cross_back(vec, dq, dy, z, r, w):
    count, width = dq.shape
    rows = pl.BlockSpec((ROWS, width), lambda i: (i, 0))
    return pl.pallas_call(
        cross_back_kernel,
        grid=(count // ROWS,),
        in_specs=[full(vec)] + [rows] * 3 + [pl.BlockSpec((ROWS, 128), lambda i: (i, 0)), one_matrix(w, 0), one_matrix(w, 3)],
        out_specs=[rows] * 3 + [pl.BlockSpec((8, width), lambda i: (0, 0))],
        out_shape=[of(count, width, dtype=F32), of(count, width), of(count, width), of(8, width, dtype=F32)],
        compiler_params=params(DENSE_VMEM),
        cost_estimate=cost(4 * count * width * width, dq, dy, z, dy, dq, dq, dq, dq),
        name="cross_query_back",
    )(vec, dq, dy, z, r, w, w)


def memory_back_kernel(dk, dv, wk, wv, out):
    out[...] = dot_nt(dk[...], matrix(wk, 0)) + dot_nt(dv[...], matrix(wv, 0))


def memory_back(dk, dv, w):
    count, width = dk.shape
    rows = pl.BlockSpec((ROWS, width), lambda i: (i, 0))
    return pl.pallas_call(
        memory_back_kernel,
        grid=(count // ROWS,),
        in_specs=[rows, rows, one_matrix(w, 1), one_matrix(w, 2)],
        out_specs=rows,
        out_shape=of(count, width, dtype=F32),
        compiler_params=params(DENSE_VMEM),
        cost_estimate=cost(4 * count * width * width, dk, dv, dk, dk, dk, dk),
        name="memory_back",
    )(dk, dv, w, w)


def self_back_kernel(dq, dk, dv, dy, w, out):
    total = dy[...] + dot_nt(dq[...], matrix(w, 0)) * FACTOR
    out[...] = total + dot_nt(dk[...], matrix(w, 1)) + dot_nt(dv[...], matrix(w, 2))


def self_back(dq, dk, dv, dy, w):
    count, width = dq.shape
    rows = pl.BlockSpec((ROWS, width), lambda i: (i, 0))
    return pl.pallas_call(
        self_back_kernel,
        grid=(count // ROWS,),
        in_specs=[rows] * 4 + [full(w)],
        out_specs=rows,
        out_shape=of(count, width, dtype=F32),
        compiler_params=params(DENSE_VMEM),
        cost_estimate=cost(6 * count * width * width, dq, dk, dv, dy, dy, w),
        name="self_project_back",
    )(dq, dk, dv, dy, w)


def hand_out(me, hold, keep, send, sem, rows, first):
    copies = []
    for relative in range(8):
        source = hold.at[jnp.bitwise_xor(me, relative), rows]
        target = (send if relative % 2 else keep).at[relative // 2, rows]
        copies.append(pltpu.make_async_copy(source, target, sem.at[first + relative]))
        copies[-1].start()
    return copies


def weight_grad_kernel(items, parts, count, me_ref, *refs):
    held = len(parts)
    outside, slabs = refs[:count], refs[count:-(held + 5)]
    keep, send = refs[-(held + 5):-(held + 3)]
    holds, hold, extra, sem = refs[-(held + 3):-3], refs[-3], refs[-2], refs[-1]
    width = hold.shape[2]
    part = width // 8
    coming = bring([outside[at].at[:, pl.ds(chunk * width, width)] for at, chunk in parts], holds, sem)
    waited = set()
    leaving, done = [], 0
    for at, (left, right, scale) in enumerate(items):
        for index in (left, right):
            if index not in waited:
                coming[index].wait()
                waited.add(index)
        product = dot_tn(holds[left][...], holds[right][...])
        product = product if scale == 1.0 else product * scale
        hold[:, at * part:(at + 1) * part, :] = product.astype(BF).reshape(8, part, width)
        if at == len(items) - 2:
            done = (at + 1) * part
            leaving += hand_out(me_ref[0], hold, keep, send, sem, pl.ds(0, done), held)
    if slabs:
        row = 0
        extra[...] = jnp.zeros(extra.shape, F32)
        for ref in slabs:
            extra[row:row + ref.shape[0], :] = ref[...]
            row += ref.shape[0]
        block = extra[...].astype(BF)
        for owner in range(8):
            hold[owner, part * len(items):, :] = block
    leaving += hand_out(me_ref[0], hold, keep, send, sem, pl.ds(done, hold.shape[1] - done), held + 8)
    wait_all(leaving)


def weight_grad(me, operands, parts, items, name, slabs=(), slab_rows=0):
    count, width = operands[0].shape
    rows = width // 8 * len(items) + slab_rows
    return pl.pallas_call(
        lambda *refs: weight_grad_kernel(items, parts, len(operands), *refs),
        grid=(1,),
        in_specs=[SCALAR] + [ANYWHERE] * len(operands) + [full(slab) for slab in slabs],
        out_specs=[ANYWHERE, ANYWHERE],
        out_shape=[of(4, rows, width)] * 2,
        scratch_shapes=[pltpu.VMEM((count, width), BF) for _ in parts] + [
            pltpu.VMEM((8, rows, width), BF),
            pltpu.VMEM((max(slab_rows, 8), width), F32),
            pltpu.SemaphoreType.DMA((len(parts) + 16,)),
        ],
        compiler_params=params(GRAD_VMEM),
        cost_estimate=cost(2 * count * width * width * len(items), *operands),
        name=name,
    )(me, *operands, *slabs)


def tall_grad_kernel(me_ref, left, right, keep, send, left_hold, right_hold, hold, sem):
    width = right.shape[1]
    chunks = left.shape[1] // width
    chip, core = me_ref[0] // 2, lax.rem(me_ref[0], 2)
    coming = [pltpu.make_async_copy(right, right_hold, sem.at[0])]
    for c in range(chunks):
        span = pl.ds(pl.multiple_of(jnp.bitwise_xor(chip, c) * width, width), width)
        coming.append(pltpu.make_async_copy(left.at[:, span], left_hold.at[c], sem.at[1 + c]))
    for copy in coming:
        copy.start()
    coming[0].wait()
    leaving = []
    for c in range(chunks):
        coming[1 + c].wait()
        product = dot_tn(left_hold[c], right_hold[...])
        hold[c] = product.astype(BF).reshape(hold.shape[1:])
        for at, (index, out) in enumerate(((core, keep), (1 - core, send))):
            leaving.append(pltpu.make_async_copy(hold.at[c, index], out.at[c], sem.at[1 + chunks + 2 * c + at]))
            leaving[-1].start()
    wait_all(leaving)


def tall_grad(me, left, right, name):
    (count, tall), width = left.shape, right.shape[1]
    chunks = tall // width
    return pl.pallas_call(
        tall_grad_kernel,
        grid=(1,),
        in_specs=[SCALAR, ANYWHERE, ANYWHERE],
        out_specs=[ANYWHERE, ANYWHERE],
        out_shape=[of(4, tall // 8, width)] * 2,
        scratch_shapes=[
            pltpu.VMEM((chunks, count, width), BF),
            pltpu.VMEM(right.shape, BF),
            pltpu.VMEM((chunks, 2, tall // 8, width), BF),
            pltpu.SemaphoreType.DMA((1 + 3 * chunks,)),
        ],
        compiler_params=params(GRAD_VMEM),
        cost_estimate=cost(2 * count * tall * width, left, left, right),
        name=name,
    )(me, left, right)


def swap(value, bit, axis="fsdp", size=8):
    return lax.ppermute(value, axis, [(i, i ^ bit) for i in range(size)])


def tie(*values):
    return lax.optimization_barrier(values)


def local(kernel, name, out_shape, *args, scratch=(), scalars=0):
    return pl.pallas_call(
        kernel,
        in_specs=[SCALAR] * scalars + [WHOLE] * (len(args) - scalars),
        out_specs=[WHOLE] * len(out_shape),
        out_shape=out_shape,
        scratch_shapes=scratch,
        compiler_params=params(SMALL_VMEM),
        cost_estimate=cost(0, *args, *out_shape),
        name=name,
    )(*args)


def halves(rows):
    return rows // 32 * 16


def split_kernel(keep, came, own, to_x, to_y, rest_y, rest_x):
    half = rest_y.shape[0]

    def total(index, rows):
        return keep[index, rows, :].astype(F32) + came[index, rows, :].astype(F32)

    low, high = slice(None, half), slice(half, None)
    own[...] = total(0, slice(None))
    to_x[0], to_x[1] = total(1, low).astype(BF), total(3, low).astype(BF)
    to_y[0], to_y[1] = total(2, high).astype(BF), total(3, high).astype(BF)
    rest_y[...] = total(2, low).astype(BF)
    rest_x[...] = total(1, high).astype(BF)


def reduce_core(keep, send):
    return [keep, swap(send, 1)]


def reduce_first(state):
    keep, came = state
    rows, width = keep.shape[1:]
    low, high = halves(rows), rows - halves(rows)
    shapes = [of(rows, width, dtype=F32), of(2, low, width), of(2, high, width), of(low, width), of(high, width)]
    own, to_x, to_y, rest_y, rest_x = local(split_kernel, "grad_split", shapes, keep, came)
    return [own, rest_y, rest_x, swap(to_x, 2), swap(to_y, 4)]


def second_kernel(own, rest_y, rest_x, from_x, from_y, out, last_y, last_x):
    half = rest_y.shape[0]
    out[:half, :] = own[:half, :] + from_x[0].astype(F32)
    out[half:, :] = own[half:, :] + from_y[0].astype(F32)
    last_y[...] = (rest_y[...].astype(F32) + from_x[1].astype(F32)).astype(BF)
    last_x[...] = (rest_x[...].astype(F32) + from_y[1].astype(F32)).astype(BF)


def reduce_second(state):
    own, rest_y, rest_x = state[:3]
    shapes = [of(*own.shape, dtype=F32), of(*rest_y.shape), of(*rest_x.shape)]
    out, last_y, last_x = local(second_kernel, "grad_second", shapes, *state)
    return [out, swap(last_y, 4), swap(last_x, 2)]


def joined_kernel(own, got_y, got_x, *outs):
    half = got_y.shape[0]
    at = 0
    for out in outs:
        rows = out.shape[-2] * (out.shape[0] if len(out.shape) == 3 else 1)
        value = own[at:at + rows, :]
        parts = []
        if at < half:
            parts.append(got_y[at:min(half, at + rows), :].astype(F32))
        if at + rows > half:
            parts.append(got_x[max(at, half) - half:at + rows - half, :].astype(F32))
        value = value + (parts[0] if len(parts) == 1 else jnp.concatenate(parts, axis=0))
        out[...] = value.astype(BF).reshape(out.shape)
        at += rows


def inward(value):
    return [value, lax.ppermute(value, "dp", [(0, 1), (3, 2)])]


def reduce_inward(state, chunks=1):
    rows, width = state[0].shape
    step = rows // chunks // 16 * 16
    sizes = [step] * (chunks - 1) + [rows - step * (chunks - 1)]
    values = local(joined_kernel, "grad_join", [of(size, width) for size in sizes], *state)
    return [inward(value) for value in values]


def pair_kernel(one, two, out):
    out[...] = (one[...].astype(F32) + two[...].astype(F32)).astype(BF)


def reduce_across(state):
    (side,) = local(pair_kernel, "grad_add", [of(*state[0].shape)], *state)
    return [side, lax.ppermute(side, "dp", [(1, 2), (2, 1)])]


def reduce_outward(state):
    (total,) = local(pair_kernel, "grad_add", [of(*state[0].shape)], *state)
    return [total, lax.ppermute(total, "dp", [(1, 0), (2, 3)])]


def exchange(value):
    return lax.all_to_all(value, "dp", 0, 0)


def reduce_joined(state):
    rows, width = state[0].shape
    return local(joined_kernel, "grad_join", [of(4, rows // 4, width)], *state)[0]


def four_kernel(parts, out):
    total = parts[0].astype(F32) + parts[1].astype(F32) + parts[2].astype(F32) + parts[3].astype(F32)
    for index in range(4):
        out[index] = total.astype(BF)


def reduce_added(parts):
    return local(four_kernel, "grad_add", [of(*parts.shape)], parts)[0]


def place_kernel(spans, at_ref, *refs):
    count = len(refs) - 1 - len(spans)
    ins, outs, hold = refs[:count], refs[count:-1], refs[-1]
    at = at_ref[0]
    middle = (at == 1) | (at == 2)
    if count == 1:
        rows = ins[0].shape[1]
        for index in range(4):
            hold[index * rows:(index + 1) * rows, :] = ins[0][index].astype(F32)
    else:
        row = 0
        for total, came in zip(ins[::2], ins[1::2]):
            rows = total.shape[0]
            hold[row:row + rows, :] = jnp.where(middle, total[...].astype(F32), came[...].astype(F32))
            row += rows
    for (first, count, columns), out in zip(spans, outs):
        if len(out.shape) == 3:
            for index in range(out.shape[0]):
                out[index] = hold[first + index * out.shape[1]:first + (index + 1) * out.shape[1], :]
        else:
            for column in range(columns):
                begin = first + column * count
                out[:, column * hold.shape[1]:(column + 1) * hold.shape[1]] = hold[begin:begin + count, :]


def reduce_end(arrays, rows, spans, shapes):
    width = arrays[0].shape[-1]
    at = lax.axis_index("dp").astype(jnp.int32).reshape(1)
    return local(
        lambda *refs: place_kernel(spans, *refs), "grad_place", shapes, at, *arrays,
        scratch=[pltpu.VMEM((rows, width), F32)], scalars=1,
    )


def small_kernel(me_ref, early, back, late, self_b, cross_b, gain, shift, b_in, b_out):
    me = me_ref[0]
    width, part = early.shape[1], self_b.shape[1]
    turn = lax.rem(width - me * part, width)

    def own(ref, row):
        return pltpu.roll(ref[row // 8 * 8:row // 8 * 8 + 8, :], turn, 1)[row % 8:row % 8 + 1, :part]

    for ref, index in ((gain, 0), (shift, 1)):
        ref[0:1, :] = own(back, index)
        ref[1:2, :] = own(early, 3 + index)
        ref[2:3, :] = own(early, 1 + index)
    b_out[...] = own(early, 0)
    cross_b[0:1, :] = own(back, 8)
    cross_b[1:2, :] = own(back, 9)
    cross_b[2:3, :] = own(early, 5)
    self_b[0:1, :] = own(late, 0)
    self_b[1:2, :] = own(late, 1)
    self_b[2:3, :] = own(back, 2)
    wide = b_in.shape[1]
    row = early[pl.ds(6 + me * wide // width, 1), :]
    b_in[...] = jnp.where(lax.rem(me, 2) == 0, row[:, :wide], row[:, wide:])


def reduce_plain(sizes, blocks):
    value = lax.psum_scatter(blocks.astype(F32), "fsdp", scatter_dimension=0, tiled=False)
    return lax.psum(value.astype(BF), "dp").astype(F32)


def first_hops(shard):
    return swap(shard, 2), swap(shard, 4)


def pieces_of(shard, core, x, y, x_core, y_core, far, offsets=(0,)):
    rows = shard.shape[0]
    found = [((0, 0, rows), shard), ((1, 0, rows), core), ((2, 0, rows), x), ((4, 0, rows), y)]
    found += [((3, 0, rows), x_core), ((5, 0, rows), y_core)]
    for offset, piece in zip(offsets, far):
        found += [((6, offset, piece.shape[0]), piece), ((7, offset, piece.shape[0]), swap(piece, 1))]
    return found


def shards(sizes, target, memory, target_lengths, memory_lengths, self_qkv, self_bias, self_out, cross_qkv, cross_bias,
           cross_out, ffn_in, ffn_in_bias, ffn_out, ffn_out_bias, norm_gain, norm_bias, cotangent):
    n = sizes[0]
    fast = n == 8 and sizes[1] == 4
    width, hidden = target.shape[-1], ffn_in.shape[1]
    part, wide = width // n, hidden // n
    ratio = hidden // width
    x, mem, cot = target[0], memory[0], cotangent[0]
    place = lax.axis_index("fsdp").astype(jnp.int32)
    me = place.reshape(1)
    vectors = [self_bias, cross_bias, norm_gain, norm_bias, ffn_in_bias.reshape(1, wide), ffn_out_bias.reshape(1, part)]

    if fast:
        owners = 8
        own = pack(self_qkv.reshape(3 * part, width), vectors)
        s_x, s_y = first_hops(own)
        s_core = swap(own, 1)
        half = halves(own.shape[0])
        s_core, c_own, c_self, c_cross, f_in, f_out = tie(s_core, cross_qkv, self_out, cross_out, ffn_in, ffn_out)
        c_own = jnp.concatenate([c_own.reshape(3 * part, width), c_self, c_cross])
        c_core, f_in_core, f_out_core = [swap(member, 1) for member in (c_own, f_in, f_out)]
        s_x, s_y, s_core, c_own, c_core, f_in_core, f_out_core = tie(
            s_x, s_y, s_core, c_own, c_core, f_in_core, f_out_core
        )
        s_low, s_high = swap(s_y[:half], 2), swap(s_x[half:], 4)
        s_x_core, s_y_core = swap(s_x, 1), swap(s_y, 1)
        c_x, c_y = first_hops(c_own)
        self_pieces = pieces_of(own, s_core, s_x, s_y, s_x_core, s_y_core, (s_low, s_high), (0, half))
    else:
        owners, me = 1, jnp.zeros((1,), jnp.int32)

        def gathered(member, axis):
            return lax.all_gather(member, "fsdp", axis=axis, tiled=True)

        def single(value):
            return [((0, 0, value.shape[0]), value)]

        fulls = [gathered(member, 1) for member in vectors[:4]]
        fulls += [gathered(ffn_in_bias, 0).reshape(ratio, width), gathered(ffn_out_bias, 0).reshape(1, width)]
        fulls = jnp.concatenate(fulls)
        fulls = jnp.pad(fulls, ((0, SLAB - fulls.shape[0]), (0, 0)))
        self_pieces = single(jnp.concatenate([gathered(self_qkv, 1).reshape(3 * width, width), fulls]))
        fulls = [gathered(cross_qkv, 1).reshape(3 * width, width), gathered(self_out, 0), gathered(cross_out, 0)]
        cross_pieces = single(jnp.concatenate(fulls))
        in_pieces, out_pieces = single(gathered(ffn_in, 0)), single(gathered(ffn_out, 0))

    pairs = width // PAIR
    early_pairs, late_pairs = (0, pairs // 2), (pairs // 2, pairs)
    self_w, vec, q, k, v = project(me, x, self_pieces, owners)
    if fast:
        q, c_x, c_y, f_in, f_out = tie(q, c_x, c_y, f_in, f_out)
        c_half = halves(c_own.shape[0])
        c_low, c_high = swap(c_y[:c_half], 2), swap(c_x[c_half:], 4)
        f_in_x, f_in_y = first_hops(f_in)
    o, lse = attend_forward(q, k, v, target_lengths, True)
    if fast:
        o, c_low, c_high, c_x, c_y, f_out = tie(o, c_low, c_high, c_x, c_y, f_out)
        cross_pieces = pieces_of(c_own, c_core, c_x, c_y, swap(c_x, 1), swap(c_y, 1), (c_low, c_high), (0, c_half))
        f_out_x, f_out_y = first_hops(f_out)
    cross_w, z_one, r_one, h_one, q2, k2, v2 = between(me, vec, o, x, mem, cross_pieces, owners)
    if fast:
        q2, f_in_x, f_in_y = tie(q2, f_in_x, f_in_y)
        f_in_far = swap(f_in_y, 2)
        f_in_x_core, f_in_y_core = swap(f_in_x, 1), swap(f_in_y, 1)
    half_one = attend_forward(q2, k2, v2, memory_lengths, False, early_pairs)
    if fast:
        q2, f_out_x, f_out_y, f_in_x_core, f_in_y_core, *half_one = tie(
            q2, f_out_x, f_out_y, f_in_x_core, f_in_y_core, *half_one
        )
        f_out_far = swap(f_out_x, 4)
        f_out_x_core, f_out_y_core = swap(f_out_x, 1), swap(f_out_y, 1)
    o2, lse2 = attend_forward(q2, k2, v2, memory_lengths, False, late_pairs, half_one)
    if fast:
        o2, f_in_far, f_out_far, f_out_x_core, f_out_y_core = tie(o2, f_in_far, f_out_far, f_out_x_core, f_out_y_core)
        in_pieces = pieces_of(f_in, f_in_core, f_in_x, f_in_y, f_in_x_core, f_in_y_core, (f_in_far,))
        out_pieces = pieces_of(f_out, f_out_core, f_out_x, f_out_y, f_out_x_core, f_out_y_core, (f_out_far,))
    mixed, act, da, df, h_two, dy, db2, do2, ffn_sums = ffn(
        me, vec, o2, z_one, cot, cross_w, in_pieces, out_pieces, hidden
    )
    if fast:
        out_state = reduce_core(*tall_grad(me, act, df, "ffn_out_grad"))
        h_two, out_state[0] = tie(h_two, out_state[0])
        operands, chunks = [h_two, da, o2, db2], [(0, 0)] + [(1, c) for c in range(ratio)] + [(2, 0), (3, 0)]
        items = [(0, 1 + c, 1.0) for c in range(ratio)] + [(1 + ratio, 2 + ratio, 1.0)]
        in_state = reduce_core(*weight_grad(me, operands, chunks, items, "ffn_in_grad", (ffn_sums,), SLAB // 2))
        do2, *out_state = tie(do2, *out_state)
        out_state = reduce_first(out_state)
        do2, in_state[0], out_state[0] = tie(do2, in_state[0], out_state[0])
    grads = attend_backward(q2, k2, v2, o2, do2, lse2, memory_lengths, False, early_pairs)
    if fast:
        do2, *states = tie(do2, *grads, *out_state, *in_state)
        grads, out_state, in_state = states[:4], reduce_second(states[4:9]), reduce_first(states[9:])
        do2, out_state[0], in_state[0] = tie(do2, out_state[0], in_state[0])
    dq2, dk2, dv2, cross_sums = attend_backward(q2, k2, v2, o2, do2, lse2, memory_lengths, False, late_pairs, grads)
    if fast:
        dq2, *states = tie(dq2, *out_state, *in_state)
        (out_state,), in_state = reduce_inward(states[:3]), reduce_second(states[3:])
        dq2, out_state[0], in_state[0] = tie(dq2, out_state[0], in_state[0])
    dy_one, db, do, back_sums = cross_back(vec, dq2, dy, z_one, r_one, cross_w)
    if fast:
        operands = [h_one, dq2, mem, dk2, dv2, o, db]
        chunks = [(at, 0) for at in range(7)]
        items = [(0, 1, FACTOR), (2, 3, 1.0), (2, 4, 1.0), (5, 6, 1.0)]
        cross_state = reduce_core(
            *weight_grad(me, operands, chunks, items, "cross_grad", (back_sums, cross_sums), SLAB // 2)
        )
        do, *states = tie(do, *out_state, *in_state, cross_state[0])
        out_state, (in_state,), cross_state[0] = reduce_across(states[:2]), reduce_inward(states[2:5]), states[5]
        do, out_state[0], in_state[0] = tie(do, out_state[0], in_state[0])
    grads = attend_backward(q, k, v, o, do, lse, target_lengths, True, early_pairs)
    if fast:
        do, *states = tie(do, *grads, *out_state, *in_state, *cross_state)
        grads, out_state, in_state = states[:4], reduce_outward(states[4:6]), reduce_across(states[6:8])
        cross_state = reduce_first(states[8:])
        do, out_state[0], in_state[0], cross_state[0] = tie(do, out_state[0], in_state[0], cross_state[0])
    dq, dk, dv, self_sums = attend_backward(q, k, v, o, do, lse, target_lengths, True, late_pairs, grads)
    if fast:
        dq, *states = tie(dq, *in_state, *cross_state, *out_state)
        in_state, cross_state, out_state = reduce_outward(states[:2]), reduce_second(states[2:7]), states[7:]
        dq, in_state[0], cross_state[0] = tie(dq, in_state[0], cross_state[0])
        chunks = [(at, 0) for at in range(4)]
        items = [(0, 1, FACTOR), (0, 2, 1.0), (0, 3, 1.0)]
        keep, send = weight_grad(me, [x, dq, dk, dv], chunks, items, "self_grad", (self_sums,), SLAB)
        send, *cross_state = tie(send, *cross_state)
        self_state = reduce_core(keep, send)
        first, second = reduce_inward(cross_state, 2)
        *self_state, first[0], second[0] = tie(*self_state, first[0], second[0])
        self_state = reduce_first(self_state)
        dq, self_state[0] = tie(dq, self_state[0])
    d_target = self_back(dq, dk, dv, dy_one, self_w)
    if fast:
        d_target, *states = tie(d_target, *self_state, *in_state)
        self_state, in_state = states[:5], states[5:]
        self_state = reduce_second(self_state)
        self_state[0], *states = tie(self_state[0], *first, *second)
        first, second = reduce_across(states[:2]), reduce_across(states[2:])
        *self_state, first[0], second[0] = tie(*self_state, first[0], second[0])
        one, two = reduce_inward(self_state, 2)
        one[0], two[0], *states = tie(one[0], two[0], *first, *second)
        first, second = reduce_outward(states[:2]), reduce_outward(states[2:])
        *one, first[0], second[0] = tie(*one, first[0], second[0])
        one = reduce_across(one)
        *two, one[0] = tie(*two, one[0])
        two = reduce_across(two)
        dk2, one[0], two[0] = tie(dk2, one[0], two[0])
    d_memory = memory_back(dk2, dv2, cross_w)

    if fast:
        f32 = dict(dtype=F32)
        d_memory, *one = tie(d_memory, *one)
        one = reduce_outward(one)
        *two, one[0] = tie(*two, one[0])
        two = reduce_outward(two)
        two[0], *states = tie(two[0], *out_state, *in_state, *first, *second)
        out_state, in_state, first, second = states[:2], states[2:4], states[4:6], states[6:]
        (out_sum,) = reduce_end(out_state, wide, [(0, wide, 1)], [of(wide, width, **f32)])
        in_sum, cross_o_sum, early = reduce_end(
            in_state, in_state[0].shape[0], [(0, part, ratio), (wide, part, 1), (wide + part, SLAB // 2, 1)],
            [of(part, hidden, **f32), of(part, width, **f32), of(SLAB // 2, width, **f32)],
        )
        cross_w_sum, self_o_sum, back = reduce_end(
            first + second, first[0].shape[0] + second[0].shape[0],
            [(0, 0, 0), (3 * part, part, 1), (4 * part, SLAB // 2, 1)],
            [of(3, part, width, **f32), of(part, width, **f32), of(SLAB // 2, width, **f32)],
        )
        self_w_sum, late = reduce_end(
            one + two, one[0].shape[0] + two[0].shape[0], [(0, 0, 0), (3 * part, SLAB, 1)],
            [of(3, part, width, **f32), of(SLAB, width, **f32)],
        )
        shapes = [of(3, part, **f32)] * 4 + [of(1, wide, **f32), of(1, part, **f32)]
        self_b, cross_b, gain, shift, b_in, b_out = local(small_kernel, "small_grads", shapes, me, early, back, late, scalars=1)
        b_in, b_out = b_in[0], b_out[0]
    else:
        def whole(left, right, scale=1.0):
            return reduce_plain(sizes, (dot_tn(left, right) * scale).reshape(n, left.shape[1] // n, right.shape[1]))

        def mine(rows, size):
            rows = rows.reshape(-1, n * size)
            return lax.dynamic_slice(rows, (0, place * size), (rows.shape[0], size))

        self_w_sum = jnp.stack([whole(x, dq, FACTOR), whole(x, dk), whole(x, dv)])
        cross_w_sum = jnp.stack([whole(h_one, dq2, FACTOR), whole(mem, dk2), whole(mem, dv2)])
        cross_o_sum, self_o_sum = whole(o2, db2), whole(o, db)
        in_sum, out_sum = whole(h_two, da), whole(act, df)
        sums = lax.psum(jnp.concatenate([ffn_sums, back_sums, cross_sums, self_sums]), ("fsdp", "dp"))
        narrow = mine(sums, part)
        self_b = jnp.stack([narrow[32], narrow[33], narrow[18]])
        cross_b = jnp.stack([narrow[24], narrow[25], narrow[5]])
        gain = jnp.stack([narrow[16], narrow[3], narrow[1]])
        shift = jnp.stack([narrow[17], narrow[4], narrow[2]])
        b_in, b_out = mine(sums[6:10], wide)[0], narrow[0]
    return (
        mixed[None], d_target[None], d_memory[None], self_w_sum, self_b, self_o_sum, cross_w_sum, cross_b, cross_o_sum,
        in_sum, b_in, out_sum, b_out, gain, shift,
    )


def solution(mesh):
    rows = P(("fsdp", "dp"), None, None)
    row = P(("fsdp", "dp"))
    stacked, vectors, matrix, vector = P(None, "fsdp", None), P(None, "fsdp"), P("fsdp", None), P("fsdp")
    weights = (stacked, vectors, matrix, stacked, vectors, matrix, matrix, vector, matrix, vector, vectors, vectors)
    sizes = (mesh.shape["fsdp"], mesh.shape["dp"])
    return jax.shard_map(
        lambda *args: shards(sizes, *args),
        mesh=mesh,
        in_specs=(rows, rows, row, row) + weights + (rows,),
        out_specs=(rows, rows, rows) + weights,
        check_vma=False,
    )
```

```python
import jax
import jax.numpy as jnp
from jax import lax
from jax.experimental import pallas as pl
from jax.experimental.pallas import tpu as pltpu
from jax.sharding import PartitionSpec as P

HDIM = 64
PAIR = 2 * HDIM
BLOCK = 256
ROWS = 256
ATTEND_VMEM = 20
MASKED = -1e30
FACTOR = HDIM ** (-0.5)
BF = jnp.bfloat16
F32 = jnp.float32


def dot_nn(a, b):
    return lax.dot_general(a, b, (((1,), (0,)), ((), ())), preferred_element_type=F32)


def dot_nt(a, b):
    return lax.dot_general(a, b, (((1,), (1,)), ((), ())), preferred_element_type=F32)


def dot_tn(a, b):
    return lax.dot_general(a, b, (((0,), (0,)), ((), ())), preferred_element_type=F32)


def column_sum(values):
    return jnp.sum(values.astype(F32), axis=0, keepdims=True)


def head_lanes(head):
    lane = lax.broadcasted_iota(jnp.int32, (1, PAIR), 1)
    return (lane // HDIM) == head, lane == (HDIM if head == 0 else 0)


def pick(mask, yes, no, shape):
    return jnp.where(jnp.broadcast_to(mask, shape), yes, no)


def length_bias(count, limit):
    positions = lax.broadcasted_iota(jnp.int32, (count, PAIR), 0)
    return jnp.where(positions < limit, 0.0, MASKED).astype(F32)


def causal_edge(values, fill):
    key_at = lax.broadcasted_iota(jnp.int32, values.shape, 0)
    query_at = lax.broadcasted_iota(jnp.int32, values.shape, 1)
    return jnp.where(key_at <= query_at, values, fill)


def attend_forward_kernel(causal, limit_ref, q_ref, k_ref, v_ref, o_ref, lse_ref):
    count, sources = q_ref.shape[0], k_ref.shape[0]
    k_all, v_all = k_ref[...].astype(F32), v_ref[...].astype(F32)
    bias = length_bias(sources, limit_ref[0])
    keys, values = [], []
    for head in range(2):
        own, spare = head_lanes(head)
        keys.append(pick(spare, bias, k_all, k_all.shape).astype(BF))
        ones = pick(spare, 1.0, 0.0, v_all.shape)
        values.append(pick(own, v_all, ones, v_all.shape).T.astype(BF))

    def scores_of(unit):
        block, head = unit
        rows = slice(block * BLOCK, (block + 1) * BLOCK)
        extent = (block + 1) * BLOCK if causal else sources
        own, spare = head_lanes(head)
        q_block = q_ref[rows, :].astype(F32)
        ones = pick(spare, 1.0, 0.0, q_block.shape)
        scores = dot_nt(keys[head][:extent], pick(own, q_block, ones, q_block.shape).astype(BF))
        if causal:
            edge = causal_edge(scores[extent - BLOCK:], MASKED)
            scores = edge if extent == BLOCK else jnp.concatenate([scores[: extent - BLOCK], edge], axis=0)
        return scores

    parts = {}

    def finish(unit, expo, highest):
        block, head = unit
        rows = slice(block * BLOCK, (block + 1) * BLOCK)
        mixed = dot_nn(values[head][:, : expo.shape[0]], expo)
        at = HDIM if head == 0 else 0
        total = mixed[at:at + 1]
        lse_ref[0, head:head + 1, rows] = highest + jnp.log(total)
        parts[unit] = mixed[head * HDIM:(head + 1) * HDIM] * (1.0 / total)
        if head == 1:
            o_ref[rows, :] = jnp.concatenate([parts[(block, 0)], parts[unit]], axis=0).T.astype(BF)

    units = [(block, head) for block in range(count // BLOCK) for head in range(2)]
    ahead = [scores_of(unit) for unit in units[:2]]
    before = None
    for at, unit in enumerate(units):
        if at + 2 < len(units):
            ahead.append(scores_of(units[at + 2]))
        highest = jnp.max(ahead[at], axis=0, keepdims=True)
        expo = jnp.exp(ahead[at] - highest).astype(BF)
        if before is not None:
            finish(*before)
        before = (unit, expo, highest)
    finish(*before)


def attend_backward_kernel(
    causal, limit_ref, q_ref, k_ref, v_ref, o_ref, do_ref, lse_ref, dq_ref, dk_ref, dv_ref, sums_ref, dq_acc
):
    count, sources = q_ref.shape[0], k_ref.shape[0]
    q_all, k_all = q_ref[...].astype(F32), k_ref[...].astype(F32)
    do_all = do_ref[...].astype(F32)
    bias = length_bias(sources, limit_ref[0])
    product = (do_all * o_ref[...].astype(F32)).T
    q_aug, q_own, k_aug, kt_own, do_own, delta, lse = [], [], [], [], [], [], []
    for head in range(2):
        own, spare = head_lanes(head)
        q_aug.append(pick(own, q_all, pick(spare, 1.0, 0.0, q_all.shape), q_all.shape).astype(BF))
        q_own.append(pick(own, q_all, 0.0, q_all.shape).astype(BF))
        k_aug.append(pick(spare, bias, k_all, k_all.shape).astype(BF))
        kt_own.append(pick(own, k_all, 0.0, k_all.shape).T.astype(BF))
        do_own.append(pick(own, do_all, 0.0, do_all.shape).astype(BF))
        delta.append(jnp.sum(product[head * HDIM:(head + 1) * HDIM], axis=0, keepdims=True))
        lse.append(lse_ref[0, head:head + 1, :])

    def products(unit):
        block, head = unit
        rows = slice(block * BLOCK, (block + 1) * BLOCK)
        first = block * BLOCK if causal else 0
        return (
            dot_nt(k_aug[head][rows], q_aug[head][first:]),
            dot_nt(v_ref[rows, :], do_own[head][first:]),
        )

    def gradients(unit, scores, d_probs):
        block, head = unit
        first = block * BLOCK if causal else 0
        probs = jnp.exp(scores - lse[head][:, first:])
        if causal:
            edge = causal_edge(probs[:, :BLOCK], 0.0)
            probs = edge if first + BLOCK == count else jnp.concatenate([edge, probs[:, BLOCK:]], axis=1)
        d_scores = (probs * (d_probs - delta[head][:, first:])).astype(BF)
        return probs.astype(BF), d_scores

    held = {}

    def finish(unit, probs, d_scores):
        block, head = unit
        rows = slice(block * BLOCK, (block + 1) * BLOCK)
        first = block * BLOCK if causal else 0
        dv = dot_nn(probs, do_own[head][first:])
        dk = dot_nn(d_scores, q_own[head][first:])
        dq = dot_nn(kt_own[head][:, rows], d_scores)
        if head == 0:
            held[block] = (dv, dk, dq)
            return
        dv = (held[block][0] + dv).astype(BF)
        dv_ref[rows, :] = dv
        held["dv"] = held.get("dv", 0.0) + column_sum(dv)
        dk_ref[rows, :] = (held[block][1] + dk).astype(BF)
        if block == 0:
            dq_acc[...] = held[block][2] + dq
        else:
            dq_acc[:, first:] += held[block][2] + dq

    units = [(block, head) for block in range(sources // BLOCK) for head in range(2)]
    ahead = [products(units[0])]
    before = None
    for at, unit in enumerate(units):
        if at + 1 < len(units):
            ahead.append(products(units[at + 1]))
        current = (unit,) + gradients(unit, *ahead[at])
        if before is not None:
            finish(*before)
        before = current
    finish(*before)
    dq = dq_acc[...].T.astype(BF)
    dq_ref[...] = dq
    sums_ref[...] = jnp.concatenate([column_sum(dq) * FACTOR, held["dv"], jnp.zeros((6, PAIR), F32)], axis=0)


def attend_call(kernel, name, causal, work, specs, arrays, out_specs, outs, scratch, limit, pairs, held):
    first, last = pairs
    held = list(held)

    def shifted(spec):
        if spec is None:
            return pl.BlockSpec(memory_space=pltpu.SMEM)
        shape, index = spec
        return pl.BlockSpec(shape, lambda i: index(i + first))

    def body(*refs):
        kernel(causal, *refs[: len(specs)], *refs[len(specs) + len(held):])

    return pl.pallas_call(
        body,
        grid=(last - first,),
        in_specs=[shifted(spec) for spec in specs] + [pl.BlockSpec(memory_space=pl.ANY)] * len(held),
        out_specs=[shifted(spec) for spec in out_specs],
        out_shape=outs,
        scratch_shapes=scratch,
        input_output_aliases={len(specs) + at: at for at in range(len(held))},
        compiler_params=pltpu.CompilerParams(vmem_limit_bytes=limit << 20),
        cost_estimate=pl.CostEstimate(flops=8 * work * (last - first) * PAIR, bytes_accessed=1 << 20, transcendentals=0),
        name=name,
    )(*arrays, *held)


def attend_forward(q, k, v, limit, causal, pairs=None, held=()):
    count, width = q.shape
    sources = k.shape[0]
    total = width // PAIR
    of_q = ((count, PAIR), lambda i: (0, i))
    of_k = ((sources, PAIR), lambda i: (0, i))
    stats = ((1, 2, count), lambda i: (i, 0, 0))
    outs = [jax.ShapeDtypeStruct((count, width), BF), jax.ShapeDtypeStruct((total, 2, count), F32)]
    return attend_call(
        attend_forward_kernel, "attend_forward", causal, 16 * count * sources * (5 if causal else 8) // 8,
        [None, of_q, of_k, of_k], [limit, q, k, v], [of_q, stats], outs, [], ATTEND_VMEM, pairs or (0, total), held,
    )


def attend_backward(q, k, v, o, do, lse, limit, causal, pairs=None, held=(), memory=ATTEND_VMEM):
    count, width = q.shape
    sources = k.shape[0]
    total = width // PAIR
    of_q = ((count, PAIR), lambda i: (0, i))
    of_k = ((sources, PAIR), lambda i: (0, i))
    stats = ((1, 2, count), lambda i: (i, 0, 0))
    outs = [
        jax.ShapeDtypeStruct((count, width), BF),
        jax.ShapeDtypeStruct((sources, width), BF),
        jax.ShapeDtypeStruct((sources, width), BF),
        jax.ShapeDtypeStruct((8, width), F32),
    ]
    return attend_call(
        attend_backward_kernel, "attend_backward", causal, 40 * count * sources * (5 if causal else 8) // 8,
        [None, of_q, of_k, of_k, of_q, of_q, stats], [limit, q, k, v, o, do, lse],
        [of_q, of_k, of_k, ((8, PAIR), lambda i: (0, i))], outs, [pltpu.VMEM((PAIR, count), F32)], memory,
        pairs or (0, total), held,
    )


WHOLE = pl.BlockSpec(memory_space=pltpu.VMEM)
DENSE_VMEM = 32
FFN_VMEM = 48
FFN_ROWS = 256
GRAD_VMEM = 56
SMALL_VMEM = 16
LARGE_VMEM = 58
ANYWHERE = pl.BlockSpec(memory_space=pl.ANY)
SCALAR = pl.BlockSpec(memory_space=pltpu.SMEM)
SLAB = 32


def params(limit):
    return pltpu.CompilerParams(vmem_limit_bytes=limit << 20)


def full(value):
    shape = tuple(value.shape)
    return pl.BlockSpec(shape, lambda *_: (0,) * len(shape), pipeline_mode=pl.Buffered(1))


def cost(flops, *arrays):
    size = sum(a.size * a.dtype.itemsize for a in arrays)
    return pl.CostEstimate(flops=8 * flops, bytes_accessed=size, transcendentals=0)


def of(*shape, dtype=BF):
    return jax.ShapeDtypeStruct(shape, dtype)


def matrix(bundle, index):
    owners, width = bundle.shape[0], bundle.shape[2]
    part = width // owners
    return bundle[:, index * part:(index + 1) * part, :].reshape(width, width)


def bring(refs, holds, sem):
    copies = [pltpu.make_async_copy(ref, hold, sem.at[at]) for at, (ref, hold) in enumerate(zip(refs, holds))]
    for copy in copies:
        copy.start()
    return copies


def one_matrix(bundle, index):
    owners, width = bundle.shape[0], bundle.shape[2]
    return pl.BlockSpec((owners, width // owners, width), lambda *_: (0, index, 0), pipeline_mode=pl.Buffered(1))


def fetch(me, pieces, bundle, sem, first):
    copies = []
    shard = max(offset + rows for (_, offset, rows), _ in pieces)
    for at, ((relative, offset, rows), piece) in enumerate(pieces):
        owner = jnp.bitwise_xor(me, relative)
        if len(bundle.shape) == 3:
            target = bundle.at[owner, pl.ds(offset, rows)]
        else:
            target = bundle.at[pl.ds(pl.multiple_of(owner * shard + offset, 16), rows)]
        copies.append(pltpu.make_async_copy(piece, target, sem.at[first + at]))
        copies[-1].start()
    return copies


def wait_all(copies):
    for copy in copies:
        copy.wait()


def leave(inside, outside, sem, at):
    return pltpu.make_async_copy(inside, outside, sem.at[at])


def at_first(action):
    pl.when(pl.program_id(0) == 0)(action)


def at_last(action):
    pl.when(pl.program_id(0) == pl.num_programs(0) - 1)(action)


def normalise(summed):
    centred = summed - jnp.mean(summed, axis=-1, keepdims=True)
    inverse = lax.rsqrt(jnp.mean(centred * centred, axis=-1, keepdims=True) + 1e-05)
    return centred * inverse, inverse


def norm_backward(d_out, normed, inverse, gain):
    d_normed = d_out * gain
    return inverse * (
        d_normed
        - jnp.mean(d_normed, axis=-1, keepdims=True)
        - normed * jnp.mean(d_normed * normed, axis=-1, keepdims=True)
    )


def gelu_parts(a):
    bell = jnp.exp(-0.5 * a * a)
    t = 1.0 / (1.0 + 0.23164189 * jnp.abs(a))
    tail = t * (0.127414796 + t * (-0.142248368 + t * (0.7107068705 + t * (-0.7265760135 + t * 0.5307027145)))) * bell
    phi = jnp.where(a >= 0.0, 1.0 - tail, tail)
    return a * phi, phi + a * bell * 0.3989422804014327


def add_rows(ref, rows):
    block = jnp.concatenate(rows + [jnp.zeros((ref.shape[0] - len(rows), ref.shape[1]), F32)], axis=0)

    @pl.when(pl.program_id(0) == 0)
    def _():
        ref[...] = block

    @pl.when(pl.program_id(0) > 0)
    def _():
        ref[...] += block


def pack_kernel(matrix_ref, *refs):
    count = (len(refs) - 3) // 2
    vectors, out, holds, slab, sem = refs[:count], refs[count], refs[count + 1:-2], refs[-2], refs[-1]
    rows = matrix_ref.shape[0]
    whole = pltpu.make_async_copy(matrix_ref, out.at[pl.ds(0, rows)], sem.at[count])
    whole.start()
    copies = bring(vectors, holds, sem)
    slab[...] = jnp.zeros(slab.shape, F32)
    row = 0
    for copy, hold in zip(copies, holds):
        copy.wait()
        slab[row:row + hold.shape[0], : hold.shape[1]] = hold[...].astype(F32)
        row += hold.shape[0]
    out[rows:, :] = slab[...].astype(BF)
    whole.wait()


def pack(value, vectors):
    rows, width = value.shape
    total = rows + SLAB // 2
    return pl.pallas_call(
        pack_kernel,
        grid=(1,),
        in_specs=[ANYWHERE] * (1 + len(vectors)),
        out_specs=full(of(total, width)),
        out_shape=of(total, width),
        scratch_shapes=[pltpu.VMEM(vector.shape, BF) for vector in vectors] + [
            pltpu.VMEM((SLAB // 2, width), F32), pltpu.SemaphoreType.DMA((len(vectors) + 1,)),
        ],
        compiler_params=params(LARGE_VMEM),
        name="pack_self",
    )(value, *vectors)


def project_kernel(layout, me_ref, x, *refs):
    pieces, (w_out, vec, q_ref, k_ref, v_ref, w, sem) = refs[: len(layout)], refs[len(layout):]
    owners, width = w.shape[0], w.shape[2]
    part = width // owners

    @at_first
    def _():
        wait_all(fetch(me_ref[0], list(zip(layout, pieces)), w, sem, 0))
        leave(w, w_out, sem, len(layout)).start()
        vec[...] = jnp.zeros(vec.shape, F32)
        if owners == 1:
            vec[:17, :] = w[0, 3 * part:, :].astype(F32)[:17, :]
        else:
            wide = 4 * width // owners
            for owner in range(owners):
                slab = w[owner, 3 * part:, :].astype(F32)
                vec[:12, owner * part:(owner + 1) * part] = slab[:12, :part]
                vec[16:17, owner * part:(owner + 1) * part] = slab[13:14, :part]
                at = owner * wide
                vec[12 + at // width:13 + at // width, at % width:at % width + wide] = slab[12:13, :wide]

    values = x[...]
    q_ref[...] = ((dot_nn(values, matrix(w, 0)) + vec[0:1, :]) * FACTOR).astype(BF)
    k_ref[...] = dot_nn(values, matrix(w, 1)).astype(BF)
    v_ref[...] = (dot_nn(values, matrix(w, 2)) + vec[1:2, :]).astype(BF)
    at_last(lambda: leave(w, w_out, sem, len(layout)).wait())


def project(me, x, pieces, owners):
    count, width = x.shape
    rows = pl.BlockSpec((ROWS, width), lambda i: (i, 0))
    layout = [key for key, _ in pieces]
    bundle = (owners, max(offset + size for _, offset, size in layout), width)
    return pl.pallas_call(
        lambda *refs: project_kernel(layout, *refs),
        grid=(count // ROWS,),
        in_specs=[SCALAR, rows] + [ANYWHERE] * len(pieces),
        out_specs=[ANYWHERE, full(of(24, width)), rows, rows, rows],
        out_shape=[of(*bundle), of(24, width, dtype=F32)] + [of(count, width)] * 3,
        scratch_shapes=[
            pltpu.VMEM(bundle, BF),
            pltpu.SemaphoreType.DMA((len(pieces) + 1,)),
        ],
        compiler_params=params(DENSE_VMEM),
        cost_estimate=cost(6 * count * width * width, x, x, x, x, x),
        name="self_project",
    )(me, x, *[piece for _, piece in pieces])


def between_kernel(layout, me_ref, vec, o, x, mem, *refs):
    pieces, (w_out, z_ref, r_ref, h_ref, q_ref, k_ref, v_ref, w, sem) = refs[: len(layout)], refs[len(layout):]

    @at_first
    def _():
        wait_all(fetch(me_ref[0], list(zip(layout, pieces)), w, sem, 0))
        leave(w, w_out, sem, len(layout)).start()

    summed = x[...].astype(F32) + dot_nn(o[...], matrix(w, 3)) + vec[2:3, :]
    source = mem[...]
    k_ref[...] = dot_nn(source, matrix(w, 1)).astype(BF)
    v_ref[...] = (dot_nn(source, matrix(w, 2)) + vec[4:5, :]).astype(BF)
    z, r = normalise(summed)
    z_ref[...] = z
    r_ref[...] = jnp.broadcast_to(r, r_ref.shape)
    hidden = (z * vec[6:7, :] + vec[9:10, :]).astype(BF)
    h_ref[...] = hidden
    q_ref[...] = ((dot_nn(hidden, matrix(w, 0)) + vec[3:4, :]) * FACTOR).astype(BF)
    at_last(lambda: leave(w, w_out, sem, len(layout)).wait())


def between(me, vec, o, x, mem, pieces, owners):
    count, width = x.shape
    rows = pl.BlockSpec((ROWS, width), lambda i: (i, 0))
    layout = [key for key, _ in pieces]
    bundle = (owners, 5 * width // owners, width)
    return pl.pallas_call(
        lambda *refs: between_kernel(layout, *refs),
        grid=(count // ROWS,),
        in_specs=[SCALAR, full(vec), rows, rows, rows] + [ANYWHERE] * len(pieces),
        out_specs=[ANYWHERE, rows, pl.BlockSpec((ROWS, 128), lambda i: (i, 0))] + [rows] * 4,
        out_shape=[of(*bundle), of(count, width, dtype=F32), of(count, 128, dtype=F32)] + [of(count, width)] * 4,
        scratch_shapes=[pltpu.VMEM(bundle, BF), pltpu.SemaphoreType.DMA((len(pieces) + 1,))],
        compiler_params=params(DENSE_VMEM),
        cost_estimate=cost(8 * count * width * width, x, x, x, x, x, x, x, x, x),
        name="self_out_cross_project",
    )(me, vec, o, x, mem, *[piece for _, piece in pieces])


def ffn_kernel(layouts, me_ref, vec, o, z_in, cot, wo, *refs):
    count = len(layouts[0])
    ins, outs = refs[:count], refs[count:count + len(layouts[1])]
    (mixed, act_ref, da_ref, df_ref, h_ref, dy_ref, db_ref, do_ref, sums_ref, w_in, w_out, slope, sem) = (
        refs[count + len(layouts[1]):]
    )
    width = o.shape[1]
    chunks = w_in.shape[1] // width
    in_copies = list(zip(layouts[0], ins)), list(zip(layouts[1], outs))

    @at_first
    def _():
        copies = fetch(me_ref[0], in_copies[0], w_in, sem, 0) + fetch(me_ref[0], in_copies[1], w_out, sem, count)
        wait_all(copies)

    gains = [vec[6 + i:7 + i, :] for i in range(3)]
    shifts = [vec[9 + i:10 + i, :] for i in range(3)]
    first = z_in[...] * gains[0] + shifts[0]
    z_two, r_two = normalise(first + dot_nn(o[...], matrix(wo, 0)) + vec[5:6, :])
    second = z_two * gains[1] + shifts[1]
    hidden = second.astype(BF)
    h_ref[...] = hidden

    def columns(c):
        return slice(c * width, (c + 1) * width)

    total = second + vec[16:17, :]
    ahead = dot_nn(hidden, w_in[:, columns(0)])
    before = None
    for c in range(chunks):
        pre = ahead + vec[12 + c:13 + c, :]
        if c + 1 < chunks:
            ahead = dot_nn(hidden, w_in[:, columns(c + 1)])
        act, grad = gelu_parts(pre)
        act = act.astype(BF)
        act_ref[:, columns(c)] = act
        slope[:, columns(c)] = grad
        if before is not None:
            total = total + dot_nn(before, w_out[columns(c - 1), :])
        before = act
    total = total + dot_nn(before, w_out[columns(chunks - 1), :])
    z, r = normalise(total)
    mixed[...] = (z * gains[2] + shifts[2]).astype(BF)
    incoming = cot[...].astype(F32)
    dy_three = norm_backward(incoming, z, r, gains[2])
    df = dy_three.astype(BF)
    df_ref[...] = df
    rows = [column_sum(df), column_sum(incoming * z), column_sum(incoming)]

    da_sums = []
    d_two = dy_three
    ahead = dot_nt(df, w_out[columns(0), :])
    before = None
    for c in range(chunks):
        d_act = ahead
        if c + 1 < chunks:
            ahead = dot_nt(df, w_out[columns(c + 1), :])
        da = (d_act * slope[:, columns(c)]).astype(BF)
        da_ref[:, columns(c)] = da
        da_sums.append(column_sum(da))
        if before is not None:
            d_two = d_two + dot_nt(before, w_in[:, columns(c - 1)])
        before = da
    d_two = d_two + dot_nt(before, w_in[:, columns(chunks - 1)])
    dy_two = norm_backward(d_two, z_two, r_two, gains[1])
    dy_ref[...] = dy_two
    db = dy_two.astype(BF)
    db_ref[...] = db
    do_ref[...] = dot_nt(db, matrix(wo, 0)).astype(BF)
    rows += [column_sum(d_two * z_two), column_sum(d_two), column_sum(db)]
    add_rows(sums_ref, rows + da_sums)


def ffn(me, vec, o, z, cot, wo, ins, outs, hidden):
    count, width = o.shape
    rows = pl.BlockSpec((FFN_ROWS, width), lambda i: (i, 0))
    wide = pl.BlockSpec((FFN_ROWS, hidden), lambda i: (i, 0))
    layouts = [key for key, _ in ins], [key for key, _ in outs]
    return pl.pallas_call(
        lambda *refs: ffn_kernel(layouts, *refs),
        grid=(count // FFN_ROWS,),
        in_specs=[SCALAR, full(vec), rows, rows, rows, one_matrix(wo, 4)] + [ANYWHERE] * (len(ins) + len(outs)),
        out_specs=[rows, wide, wide, rows, rows, rows, rows, rows, pl.BlockSpec((16, width), lambda i: (0, 0))],
        out_shape=[
            of(count, width), of(count, hidden), of(count, hidden), of(count, width), of(count, width),
            of(count, width, dtype=F32), of(count, width), of(count, width), of(16, width, dtype=F32),
        ],
        scratch_shapes=[
            pltpu.VMEM((width, hidden), BF),
            pltpu.VMEM((hidden, width), BF),
            pltpu.VMEM((FFN_ROWS, hidden), F32),
            pltpu.SemaphoreType.DMA((len(ins) + len(outs),)),
        ],
        compiler_params=params(FFN_VMEM),
        cost_estimate=cost(8 * count * width * hidden + 4 * count * width * width, o, z, z, cot, o, o, o, o),
        name="ffn",
    )(me, vec, o, z, cot, wo, *[piece for _, piece in ins + outs])


def cross_back_kernel(vec, dq, dy, z, r, w, wo, dy_ref, db_ref, do_ref, sums_ref):
    d_one = dy[...] + dot_nt(dq[...], matrix(w, 0)) * FACTOR
    normed = z[...]
    dy_one = norm_backward(d_one, normed, r[:, :1], vec[6:7, :])
    dy_ref[...] = dy_one
    db = dy_one.astype(BF)
    db_ref[...] = db
    do_ref[...] = dot_nt(db, matrix(wo, 0)).astype(BF)
    add_rows(sums_ref, [column_sum(d_one * normed), column_sum(d_one), column_sum(db)])


def cross_back(vec, dq, dy, z, r, w):
    count, width = dq.shape
    rows = pl.BlockSpec((ROWS, width), lambda i: (i, 0))
    return pl.pallas_call(
        cross_back_kernel,
        grid=(count // ROWS,),
        in_specs=[full(vec)] + [rows] * 3 + [pl.BlockSpec((ROWS, 128), lambda i: (i, 0)), one_matrix(w, 0), one_matrix(w, 3)],
        out_specs=[rows] * 3 + [pl.BlockSpec((8, width), lambda i: (0, 0))],
        out_shape=[of(count, width, dtype=F32), of(count, width), of(count, width), of(8, width, dtype=F32)],
        compiler_params=params(DENSE_VMEM),
        cost_estimate=cost(4 * count * width * width, dq, dy, z, dy, dq, dq, dq, dq),
        name="cross_query_back",
    )(vec, dq, dy, z, r, w, w)


def memory_back_kernel(dk, dv, wk, wv, out):
    out[...] = dot_nt(dk[...], matrix(wk, 0)) + dot_nt(dv[...], matrix(wv, 0))


def memory_back(dk, dv, w):
    count, width = dk.shape
    rows = pl.BlockSpec((ROWS, width), lambda i: (i, 0))
    return pl.pallas_call(
        memory_back_kernel,
        grid=(count // ROWS,),
        in_specs=[rows, rows, one_matrix(w, 1), one_matrix(w, 2)],
        out_specs=rows,
        out_shape=of(count, width, dtype=F32),
        compiler_params=params(DENSE_VMEM),
        cost_estimate=cost(4 * count * width * width, dk, dv, dk, dk, dk, dk),
        name="memory_back",
    )(dk, dv, w, w)


def self_back_kernel(dq, dk, dv, dy, w, out):
    total = dy[...] + dot_nt(dq[...], matrix(w, 0)) * FACTOR
    out[...] = total + dot_nt(dk[...], matrix(w, 1)) + dot_nt(dv[...], matrix(w, 2))


def self_back(dq, dk, dv, dy, w):
    count, width = dq.shape
    rows = pl.BlockSpec((ROWS, width), lambda i: (i, 0))
    return pl.pallas_call(
        self_back_kernel,
        grid=(count // ROWS,),
        in_specs=[rows] * 4 + [full(w)],
        out_specs=rows,
        out_shape=of(count, width, dtype=F32),
        compiler_params=params(DENSE_VMEM),
        cost_estimate=cost(6 * count * width * width, dq, dk, dv, dy, dy, w),
        name="self_project_back",
    )(dq, dk, dv, dy, w)


def hand_out(me, hold, keep, send, sem, rows, first):
    copies = []
    for relative in range(8):
        source = hold.at[jnp.bitwise_xor(me, relative), rows]
        target = (send if relative % 2 else keep).at[relative // 2, rows]
        copies.append(pltpu.make_async_copy(source, target, sem.at[first + relative]))
        copies[-1].start()
    return copies


def weight_grad_kernel(items, parts, count, me_ref, *refs):
    held = len(parts)
    outside, slabs = refs[:count], refs[count:-(held + 5)]
    keep, send = refs[-(held + 5):-(held + 3)]
    holds, hold, extra, sem = refs[-(held + 3):-3], refs[-3], refs[-2], refs[-1]
    width = hold.shape[2]
    part = width // 8
    coming = bring([outside[at].at[:, pl.ds(chunk * width, width)] for at, chunk in parts], holds, sem)
    waited = set()
    leaving, done = [], 0
    for at, (left, right, scale) in enumerate(items):
        for index in (left, right):
            if index not in waited:
                coming[index].wait()
                waited.add(index)
        product = dot_tn(holds[left][...], holds[right][...])
        product = product if scale == 1.0 else product * scale
        hold[:, at * part:(at + 1) * part, :] = product.astype(BF).reshape(8, part, width)
        if at == len(items) - 2:
            done = (at + 1) * part
            leaving += hand_out(me_ref[0], hold, keep, send, sem, pl.ds(0, done), held)
    if slabs:
        row = 0
        extra[...] = jnp.zeros(extra.shape, F32)
        for ref in slabs:
            extra[row:row + ref.shape[0], :] = ref[...]
            row += ref.shape[0]
        block = extra[...].astype(BF)
        for owner in range(8):
            hold[owner, part * len(items):, :] = block
    leaving += hand_out(me_ref[0], hold, keep, send, sem, pl.ds(done, hold.shape[1] - done), held + 8)
    wait_all(leaving)


def weight_grad(me, operands, parts, items, name, slabs=(), slab_rows=0):
    count, width = operands[0].shape
    rows = width // 8 * len(items) + slab_rows
    return pl.pallas_call(
        lambda *refs: weight_grad_kernel(items, parts, len(operands), *refs),
        grid=(1,),
        in_specs=[SCALAR] + [ANYWHERE] * len(operands) + [full(slab) for slab in slabs],
        out_specs=[ANYWHERE, ANYWHERE],
        out_shape=[of(4, rows, width)] * 2,
        scratch_shapes=[pltpu.VMEM((count, width), BF) for _ in parts] + [
            pltpu.VMEM((8, rows, width), BF),
            pltpu.VMEM((max(slab_rows, 8), width), F32),
            pltpu.SemaphoreType.DMA((len(parts) + 16,)),
        ],
        compiler_params=params(GRAD_VMEM),
        cost_estimate=cost(2 * count * width * width * len(items), *operands),
        name=name,
    )(me, *operands, *slabs)


def tall_grad_kernel(me_ref, left, right, keep, send, left_hold, right_hold, hold, sem):
    width = right.shape[1]
    chunks = left.shape[1] // width
    chip, core = me_ref[0] // 2, lax.rem(me_ref[0], 2)
    coming = [pltpu.make_async_copy(right, right_hold, sem.at[0])]
    for c in range(chunks):
        span = pl.ds(pl.multiple_of(jnp.bitwise_xor(chip, c) * width, width), width)
        coming.append(pltpu.make_async_copy(left.at[:, span], left_hold.at[c], sem.at[1 + c]))
    for copy in coming:
        copy.start()
    coming[0].wait()
    leaving = []
    for c in range(chunks):
        coming[1 + c].wait()
        product = dot_tn(left_hold[c], right_hold[...])
        hold[c] = product.astype(BF).reshape(hold.shape[1:])
        for at, (index, out) in enumerate(((core, keep), (1 - core, send))):
            leaving.append(pltpu.make_async_copy(hold.at[c, index], out.at[c], sem.at[1 + chunks + 2 * c + at]))
            leaving[-1].start()
    wait_all(leaving)


def tall_grad(me, left, right, name):
    (count, tall), width = left.shape, right.shape[1]
    chunks = tall // width
    return pl.pallas_call(
        tall_grad_kernel,
        grid=(1,),
        in_specs=[SCALAR, ANYWHERE, ANYWHERE],
        out_specs=[ANYWHERE, ANYWHERE],
        out_shape=[of(4, tall // 8, width)] * 2,
        scratch_shapes=[
            pltpu.VMEM((chunks, count, width), BF),
            pltpu.VMEM(right.shape, BF),
            pltpu.VMEM((chunks, 2, tall // 8, width), BF),
            pltpu.SemaphoreType.DMA((1 + 3 * chunks,)),
        ],
        compiler_params=params(GRAD_VMEM),
        cost_estimate=cost(2 * count * tall * width, left, left, right),
        name=name,
    )(me, left, right)


def swap(value, bit, axis="fsdp", size=8):
    return lax.ppermute(value, axis, [(i, i ^ bit) for i in range(size)])


def tie(*values):
    return lax.optimization_barrier(values)


def local(kernel, name, out_shape, *args, scratch=(), scalars=0):
    return pl.pallas_call(
        kernel,
        in_specs=[SCALAR] * scalars + [WHOLE] * (len(args) - scalars),
        out_specs=[WHOLE] * len(out_shape),
        out_shape=out_shape,
        scratch_shapes=scratch,
        compiler_params=params(SMALL_VMEM),
        cost_estimate=cost(0, *args, *out_shape),
        name=name,
    )(*args)


def halves(rows):
    return rows // 32 * 16


def split_kernel(keep, came, own, to_x, to_y, rest_y, rest_x):
    half = rest_y.shape[0]

    def total(index, rows):
        return keep[index, rows, :].astype(F32) + came[index, rows, :].astype(F32)

    low, high = slice(None, half), slice(half, None)
    own[...] = total(0, slice(None))
    to_x[0], to_x[1] = total(1, low).astype(BF), total(3, low).astype(BF)
    to_y[0], to_y[1] = total(2, high).astype(BF), total(3, high).astype(BF)
    rest_y[...] = total(2, low).astype(BF)
    rest_x[...] = total(1, high).astype(BF)


def reduce_core(keep, send):
    return [keep, swap(send, 1)]


def reduce_first(state):
    keep, came = state
    rows, width = keep.shape[1:]
    low, high = halves(rows), rows - halves(rows)
    shapes = [of(rows, width, dtype=F32), of(2, low, width), of(2, high, width), of(low, width), of(high, width)]
    own, to_x, to_y, rest_y, rest_x = local(split_kernel, "grad_split", shapes, keep, came)
    return [own, rest_y, rest_x, swap(to_x, 2), swap(to_y, 4)]


def second_kernel(own, rest_y, rest_x, from_x, from_y, out, last_y, last_x):
    half = rest_y.shape[0]
    out[:half, :] = own[:half, :] + from_x[0].astype(F32)
    out[half:, :] = own[half:, :] + from_y[0].astype(F32)
    last_y[...] = (rest_y[...].astype(F32) + from_x[1].astype(F32)).astype(BF)
    last_x[...] = (rest_x[...].astype(F32) + from_y[1].astype(F32)).astype(BF)


def reduce_second(state):
    own, rest_y, rest_x = state[:3]
    shapes = [of(*own.shape, dtype=F32), of(*rest_y.shape), of(*rest_x.shape)]
    out, last_y, last_x = local(second_kernel, "grad_second", shapes, *state)
    return [out, swap(last_y, 4), swap(last_x, 2)]


def joined_kernel(own, got_y, got_x, *outs):
    half = got_y.shape[0]
    at = 0
    for out in outs:
        rows = out.shape[-2] * (out.shape[0] if len(out.shape) == 3 else 1)
        value = own[at:at + rows, :]
        parts = []
        if at < half:
            parts.append(got_y[at:min(half, at + rows), :].astype(F32))
        if at + rows > half:
            parts.append(got_x[max(at, half) - half:at + rows - half, :].astype(F32))
        value = value + (parts[0] if len(parts) == 1 else jnp.concatenate(parts, axis=0))
        out[...] = value.astype(BF).reshape(out.shape)
        at += rows


def inward(value):
    return [value, lax.ppermute(value, "dp", [(0, 1), (3, 2)])]


def reduce_inward(state, chunks=1):
    rows, width = state[0].shape
    step = rows // chunks // 16 * 16
    sizes = [step] * (chunks - 1) + [rows - step * (chunks - 1)]
    values = local(joined_kernel, "grad_join", [of(size, width) for size in sizes], *state)
    return [inward(value) for value in values]


def pair_kernel(one, two, out):
    out[...] = (one[...].astype(F32) + two[...].astype(F32)).astype(BF)


def reduce_across(state):
    (side,) = local(pair_kernel, "grad_add", [of(*state[0].shape)], *state)
    return [side, lax.ppermute(side, "dp", [(1, 2), (2, 1)])]


def reduce_outward(state):
    (total,) = local(pair_kernel, "grad_add", [of(*state[0].shape)], *state)
    return [total, lax.ppermute(total, "dp", [(1, 0), (2, 3)])]


def exchange(value):
    return lax.all_to_all(value, "dp", 0, 0)


def reduce_joined(state):
    rows, width = state[0].shape
    return local(joined_kernel, "grad_join", [of(4, rows // 4, width)], *state)[0]


def four_kernel(parts, out):
    total = parts[0].astype(F32) + parts[1].astype(F32) + parts[2].astype(F32) + parts[3].astype(F32)
    for index in range(4):
        out[index] = total.astype(BF)


def reduce_added(parts):
    return local(four_kernel, "grad_add", [of(*parts.shape)], parts)[0]


def place_kernel(spans, at_ref, *refs):
    count = len(refs) - 1 - len(spans)
    ins, outs, hold = refs[:count], refs[count:-1], refs[-1]
    at = at_ref[0]
    middle = (at == 1) | (at == 2)
    if count == 1:
        rows = ins[0].shape[1]
        for index in range(4):
            hold[index * rows:(index + 1) * rows, :] = ins[0][index].astype(F32)
    else:
        row = 0
        for total, came in zip(ins[::2], ins[1::2]):
            rows = total.shape[0]
            hold[row:row + rows, :] = jnp.where(middle, total[...].astype(F32), came[...].astype(F32))
            row += rows
    for (first, count, columns), out in zip(spans, outs):
        if len(out.shape) == 3:
            for index in range(out.shape[0]):
                out[index] = hold[first + index * out.shape[1]:first + (index + 1) * out.shape[1], :]
        else:
            for column in range(columns):
                begin = first + column * count
                out[:, column * hold.shape[1]:(column + 1) * hold.shape[1]] = hold[begin:begin + count, :]


def reduce_end(arrays, rows, spans, shapes):
    width = arrays[0].shape[-1]
    at = lax.axis_index("dp").astype(jnp.int32).reshape(1)
    return local(
        lambda *refs: place_kernel(spans, *refs), "grad_place", shapes, at, *arrays,
        scratch=[pltpu.VMEM((rows, width), F32)], scalars=1,
    )


def small_kernel(me_ref, early, back, late, self_b, cross_b, gain, shift, b_in, b_out):
    me = me_ref[0]
    width, part = early.shape[1], self_b.shape[1]
    turn = lax.rem(width - me * part, width)

    def own(ref, row):
        return pltpu.roll(ref[row // 8 * 8:row // 8 * 8 + 8, :], turn, 1)[row % 8:row % 8 + 1, :part]

    for ref, index in ((gain, 0), (shift, 1)):
        ref[0:1, :] = own(back, index)
        ref[1:2, :] = own(early, 3 + index)
        ref[2:3, :] = own(early, 1 + index)
    b_out[...] = own(early, 0)
    cross_b[0:1, :] = own(back, 8)
    cross_b[1:2, :] = own(back, 9)
    cross_b[2:3, :] = own(early, 5)
    self_b[0:1, :] = own(late, 0)
    self_b[1:2, :] = own(late, 1)
    self_b[2:3, :] = own(back, 2)
    wide = b_in.shape[1]
    row = early[pl.ds(6 + me * wide // width, 1), :]
    b_in[...] = jnp.where(lax.rem(me, 2) == 0, row[:, :wide], row[:, wide:])


def reduce_plain(sizes, blocks):
    value = lax.psum_scatter(blocks.astype(F32), "fsdp", scatter_dimension=0, tiled=False)
    return lax.psum(value.astype(BF), "dp").astype(F32)


def first_hops(shard):
    return swap(shard, 2), swap(shard, 4)


def pieces_of(shard, core, x, y, x_core, y_core, far, offsets=(0,)):
    rows = shard.shape[0]
    found = [((0, 0, rows), shard), ((1, 0, rows), core), ((2, 0, rows), x), ((4, 0, rows), y)]
    found += [((3, 0, rows), x_core), ((5, 0, rows), y_core)]
    for offset, piece in zip(offsets, far):
        found += [((6, offset, piece.shape[0]), piece), ((7, offset, piece.shape[0]), swap(piece, 1))]
    return found


def shards(sizes, target, memory, target_lengths, memory_lengths, self_qkv, self_bias, self_out, cross_qkv, cross_bias,
           cross_out, ffn_in, ffn_in_bias, ffn_out, ffn_out_bias, norm_gain, norm_bias, cotangent):
    n = sizes[0]
    fast = n == 8 and sizes[1] == 4
    width, hidden = target.shape[-1], ffn_in.shape[1]
    part, wide = width // n, hidden // n
    ratio = hidden // width
    x, mem, cot = target[0], memory[0], cotangent[0]
    place = lax.axis_index("fsdp").astype(jnp.int32)
    me = place.reshape(1)
    vectors = [self_bias, cross_bias, norm_gain, norm_bias, ffn_in_bias.reshape(1, wide), ffn_out_bias.reshape(1, part)]

    if fast:
        owners = 8
        own = pack(self_qkv.reshape(3 * part, width), vectors)
        s_x, s_y = first_hops(own)
        s_core = swap(own, 1)
        half = halves(own.shape[0])
        c_own = jnp.concatenate([cross_qkv.reshape(3 * part, width), self_out, cross_out])
        s_x, s_y, s_core, c_own, f_in, f_out = tie(s_x, s_y, s_core, c_own, ffn_in, ffn_out)
        c_core, f_in_core, f_out_core = [swap(member, 1) for member in (c_own, f_in, f_out)]
        s_low, s_high = swap(s_y[:half], 2), swap(s_x[half:], 4)
        s_x_core, s_y_core = swap(s_x, 1), swap(s_y, 1)
        c_x, c_y = first_hops(c_own)
        self_pieces = pieces_of(own, s_core, s_x, s_y, s_x_core, s_y_core, (s_low, s_high), (0, half))
    else:
        owners, me = 1, jnp.zeros((1,), jnp.int32)

        def gathered(member, axis):
            return lax.all_gather(member, "fsdp", axis=axis, tiled=True)

        def single(value):
            return [((0, 0, value.shape[0]), value)]

        fulls = [gathered(member, 1) for member in vectors[:4]]
        fulls += [gathered(ffn_in_bias, 0).reshape(ratio, width), gathered(ffn_out_bias, 0).reshape(1, width)]
        fulls = jnp.concatenate(fulls)
        fulls = jnp.pad(fulls, ((0, SLAB - fulls.shape[0]), (0, 0)))
        self_pieces = single(jnp.concatenate([gathered(self_qkv, 1).reshape(3 * width, width), fulls]))
        fulls = [gathered(cross_qkv, 1).reshape(3 * width, width), gathered(self_out, 0), gathered(cross_out, 0)]
        cross_pieces = single(jnp.concatenate(fulls))
        in_pieces, out_pieces = single(gathered(ffn_in, 0)), single(gathered(ffn_out, 0))

    pairs = width // PAIR
    early_pairs, late_pairs = (0, pairs // 2), (pairs // 2, pairs)
    self_w, vec, q, k, v = project(me, x, self_pieces, owners)
    if fast:
        q, c_x, c_y, f_in, f_out, c_core, f_in_core, f_out_core = tie(
            q, c_x, c_y, f_in, f_out, c_core, f_in_core, f_out_core
        )
        c_half = halves(c_own.shape[0])
        c_low, c_high = swap(c_y[:c_half], 2), swap(c_x[c_half:], 4)
        f_in_x, f_in_y = first_hops(f_in)
    o, lse = attend_forward(q, k, v, target_lengths, True)
    if fast:
        o, c_low, c_high, c_x, c_y, f_out = tie(o, c_low, c_high, c_x, c_y, f_out)
        cross_pieces = pieces_of(c_own, c_core, c_x, c_y, swap(c_x, 1), swap(c_y, 1), (c_low, c_high), (0, c_half))
        f_out_x, f_out_y = first_hops(f_out)
    cross_w, z_one, r_one, h_one, q2, k2, v2 = between(me, vec, o, x, mem, cross_pieces, owners)
    if fast:
        q2, f_in_x, f_in_y = tie(q2, f_in_x, f_in_y)
        f_in_far = swap(f_in_y, 2)
        f_in_x_core, f_in_y_core = swap(f_in_x, 1), swap(f_in_y, 1)
    half_one = attend_forward(q2, k2, v2, memory_lengths, False, early_pairs)
    if fast:
        q2, f_out_x, f_out_y, f_in_x_core, f_in_y_core, *half_one = tie(
            q2, f_out_x, f_out_y, f_in_x_core, f_in_y_core, *half_one
        )
        f_out_far = swap(f_out_x, 4)
        f_out_x_core, f_out_y_core = swap(f_out_x, 1), swap(f_out_y, 1)
    o2, lse2 = attend_forward(q2, k2, v2, memory_lengths, False, late_pairs, half_one)
    if fast:
        o2, f_in_far, f_out_far, f_out_x_core, f_out_y_core = tie(o2, f_in_far, f_out_far, f_out_x_core, f_out_y_core)
        in_pieces = pieces_of(f_in, f_in_core, f_in_x, f_in_y, f_in_x_core, f_in_y_core, (f_in_far,))
        out_pieces = pieces_of(f_out, f_out_core, f_out_x, f_out_y, f_out_x_core, f_out_y_core, (f_out_far,))
    mixed, act, da, df, h_two, dy, db2, do2, ffn_sums = ffn(
        me, vec, o2, z_one, cot, cross_w, in_pieces, out_pieces, hidden
    )
    if fast:
        out_state = reduce_core(*tall_grad(me, act, df, "ffn_out_grad"))
        h_two, out_state[0] = tie(h_two, out_state[0])
        operands, chunks = [h_two, da, o2, db2], [(0, 0)] + [(1, c) for c in range(ratio)] + [(2, 0), (3, 0)]
        items = [(0, 1 + c, 1.0) for c in range(ratio)] + [(1 + ratio, 2 + ratio, 1.0)]
        in_state = reduce_core(*weight_grad(me, operands, chunks, items, "ffn_in_grad", (ffn_sums,), SLAB // 2))
        do2, *out_state = tie(do2, *out_state)
        out_state = reduce_first(out_state)
        do2, in_state[0], out_state[0] = tie(do2, in_state[0], out_state[0])
    grads = attend_backward(q2, k2, v2, o2, do2, lse2, memory_lengths, False, early_pairs)
    if fast:
        do2, *states = tie(do2, *grads, *out_state, *in_state)
        grads, out_state, in_state = states[:4], reduce_second(states[4:9]), reduce_first(states[9:])
        do2, out_state[0], in_state[0] = tie(do2, out_state[0], in_state[0])
    dq2, dk2, dv2, cross_sums = attend_backward(q2, k2, v2, o2, do2, lse2, memory_lengths, False, late_pairs, grads)
    if fast:
        dq2, *states = tie(dq2, *out_state, *in_state)
        (out_state,), in_state = reduce_inward(states[:3]), reduce_second(states[3:])
        dq2, out_state[0], in_state[0] = tie(dq2, out_state[0], in_state[0])
    dy_one, db, do, back_sums = cross_back(vec, dq2, dy, z_one, r_one, cross_w)
    if fast:
        operands = [h_one, dq2, mem, dk2, dv2, o, db]
        chunks = [(at, 0) for at in range(7)]
        items = [(0, 1, FACTOR), (2, 3, 1.0), (2, 4, 1.0), (5, 6, 1.0)]
        cross_state = reduce_core(
            *weight_grad(me, operands, chunks, items, "cross_grad", (back_sums, cross_sums), SLAB // 2)
        )
        do, *states = tie(do, *out_state, *in_state, cross_state[0])
        out_state, (in_state,), cross_state[0] = reduce_across(states[:2]), reduce_inward(states[2:5]), states[5]
        do, out_state[0], in_state[0] = tie(do, out_state[0], in_state[0])
    grads = attend_backward(q, k, v, o, do, lse, target_lengths, True, early_pairs)
    if fast:
        do, *states = tie(do, *grads, *out_state, *in_state, *cross_state)
        grads, out_state, in_state = states[:4], reduce_outward(states[4:6]), reduce_across(states[6:8])
        cross_state = reduce_first(states[8:])
        do, out_state[0], in_state[0], cross_state[0] = tie(do, out_state[0], in_state[0], cross_state[0])
    dq, dk, dv, self_sums = attend_backward(q, k, v, o, do, lse, target_lengths, True, late_pairs, grads)
    if fast:
        dq, *states = tie(dq, *in_state, *cross_state, *out_state)
        in_state, cross_state, out_state = reduce_outward(states[:2]), reduce_second(states[2:7]), states[7:]
        dq, in_state[0], cross_state[0] = tie(dq, in_state[0], cross_state[0])
        chunks = [(at, 0) for at in range(4)]
        items = [(0, 1, FACTOR), (0, 2, 1.0), (0, 3, 1.0)]
        keep, send = weight_grad(me, [x, dq, dk, dv], chunks, items, "self_grad", (self_sums,), SLAB)
        send, *cross_state = tie(send, *cross_state)
        self_state = reduce_core(keep, send)
        first, second = reduce_inward(cross_state, 2)
        *self_state, first[0], second[0] = tie(*self_state, first[0], second[0])
        self_state = reduce_first(self_state)
        dq, self_state[0] = tie(dq, self_state[0])
    d_target = self_back(dq, dk, dv, dy_one, self_w)
    if fast:
        d_target, *states = tie(d_target, *self_state, *in_state)
        self_state, in_state = states[:5], states[5:]
        self_state = reduce_second(self_state)
        self_state[0], *states = tie(self_state[0], *first, *second)
        first, second = reduce_across(states[:2]), reduce_across(states[2:])
        *self_state, first[0], second[0] = tie(*self_state, first[0], second[0])
        one, two = reduce_inward(self_state, 2)
        one[0], two[0], *states = tie(one[0], two[0], *first, *second)
        first, second = reduce_outward(states[:2]), reduce_outward(states[2:])
        *one, first[0], second[0] = tie(*one, first[0], second[0])
        one = reduce_across(one)
        *two, one[0] = tie(*two, one[0])
        two = reduce_across(two)
        dk2, one[0], two[0] = tie(dk2, one[0], two[0])
    d_memory = memory_back(dk2, dv2, cross_w)

    if fast:
        f32 = dict(dtype=F32)
        d_memory, *one = tie(d_memory, *one)
        one = reduce_outward(one)
        *two, one[0] = tie(*two, one[0])
        two = reduce_outward(two)
        two[0], *states = tie(two[0], *out_state, *in_state, *first, *second)
        out_state, in_state, first, second = states[:2], states[2:4], states[4:6], states[6:]
        (out_sum,) = reduce_end(out_state, wide, [(0, wide, 1)], [of(wide, width, **f32)])
        in_sum, cross_o_sum, early = reduce_end(
            in_state, in_state[0].shape[0], [(0, part, ratio), (wide, part, 1), (wide + part, SLAB // 2, 1)],
            [of(part, hidden, **f32), of(part, width, **f32), of(SLAB // 2, width, **f32)],
        )
        cross_w_sum, self_o_sum, back = reduce_end(
            first + second, first[0].shape[0] + second[0].shape[0],
            [(0, 0, 0), (3 * part, part, 1), (4 * part, SLAB // 2, 1)],
            [of(3, part, width, **f32), of(part, width, **f32), of(SLAB // 2, width, **f32)],
        )
        self_w_sum, late = reduce_end(
            one + two, one[0].shape[0] + two[0].shape[0], [(0, 0, 0), (3 * part, SLAB, 1)],
            [of(3, part, width, **f32), of(SLAB, width, **f32)],
        )
        shapes = [of(3, part, **f32)] * 4 + [of(1, wide, **f32), of(1, part, **f32)]
        self_b, cross_b, gain, shift, b_in, b_out = local(small_kernel, "small_grads", shapes, me, early, back, late, scalars=1)
        b_in, b_out = b_in[0], b_out[0]
    else:
        def whole(left, right, scale=1.0):
            return reduce_plain(sizes, (dot_tn(left, right) * scale).reshape(n, left.shape[1] // n, right.shape[1]))

        def mine(rows, size):
            rows = rows.reshape(-1, n * size)
            return lax.dynamic_slice(rows, (0, place * size), (rows.shape[0], size))

        self_w_sum = jnp.stack([whole(x, dq, FACTOR), whole(x, dk), whole(x, dv)])
        cross_w_sum = jnp.stack([whole(h_one, dq2, FACTOR), whole(mem, dk2), whole(mem, dv2)])
        cross_o_sum, self_o_sum = whole(o2, db2), whole(o, db)
        in_sum, out_sum = whole(h_two, da), whole(act, df)
        sums = lax.psum(jnp.concatenate([ffn_sums, back_sums, cross_sums, self_sums]), ("fsdp", "dp"))
        narrow = mine(sums, part)
        self_b = jnp.stack([narrow[32], narrow[33], narrow[18]])
        cross_b = jnp.stack([narrow[24], narrow[25], narrow[5]])
        gain = jnp.stack([narrow[16], narrow[3], narrow[1]])
        shift = jnp.stack([narrow[17], narrow[4], narrow[2]])
        b_in, b_out = mine(sums[6:10], wide)[0], narrow[0]
    return (
        mixed[None], d_target[None], d_memory[None], self_w_sum, self_b, self_o_sum, cross_w_sum, cross_b, cross_o_sum,
        in_sum, b_in, out_sum, b_out, gain, shift,
    )


def solution(mesh):
    rows = P(("fsdp", "dp"), None, None)
    row = P(("fsdp", "dp"))
    stacked, vectors, matrix, vector = P(None, "fsdp", None), P(None, "fsdp"), P("fsdp", None), P("fsdp")
    weights = (stacked, vectors, matrix, stacked, vectors, matrix, matrix, vector, matrix, vector, vectors, vectors)
    sizes = (mesh.shape["fsdp"], mesh.shape["dp"])
    return jax.shard_map(
        lambda *args: shards(sizes, *args),
        mesh=mesh,
        in_specs=(rows, rows, row, row) + weights + (rows,),
        out_specs=(rows, rows, rows) + weights,
        check_vma=False,
    )
```

```python
import jax
import jax.numpy as jnp
from jax import lax
from jax.experimental import pallas as pl
from jax.experimental.pallas import tpu as pltpu
from jax.sharding import PartitionSpec as P

HDIM = 64
PAIR = 2 * HDIM
BLOCK = 256
ROWS = 512
ATTEND_VMEM = 20
MASKED = -1e30
FACTOR = HDIM ** (-0.5)
BF = jnp.bfloat16
F32 = jnp.float32


def dot_nn(a, b):
    return lax.dot_general(a, b, (((1,), (0,)), ((), ())), preferred_element_type=F32)


def dot_nt(a, b):
    return lax.dot_general(a, b, (((1,), (1,)), ((), ())), preferred_element_type=F32)


def dot_tn(a, b):
    return lax.dot_general(a, b, (((0,), (0,)), ((), ())), preferred_element_type=F32)


def column_sum(values):
    return jnp.sum(values.astype(F32), axis=0, keepdims=True)


def head_lanes(head):
    lane = lax.broadcasted_iota(jnp.int32, (1, PAIR), 1)
    return (lane // HDIM) == head, lane == (HDIM if head == 0 else 0)


def pick(mask, yes, no, shape):
    return jnp.where(jnp.broadcast_to(mask, shape), yes, no)


def length_bias(count, limit):
    positions = lax.broadcasted_iota(jnp.int32, (count, PAIR), 0)
    return jnp.where(positions < limit, 0.0, MASKED).astype(F32)


def causal_edge(values, fill):
    key_at = lax.broadcasted_iota(jnp.int32, values.shape, 0)
    query_at = lax.broadcasted_iota(jnp.int32, values.shape, 1)
    return jnp.where(key_at <= query_at, values, fill)


def attend_forward_kernel(causal, limit_ref, q_ref, k_ref, v_ref, o_ref, lse_ref):
    count, sources = q_ref.shape[0], k_ref.shape[0]
    k_all, v_all = k_ref[...].astype(F32), v_ref[...].astype(F32)
    bias = length_bias(sources, limit_ref[0])
    keys, values = [], []
    for head in range(2):
        own, spare = head_lanes(head)
        keys.append(pick(spare, bias, k_all, k_all.shape).astype(BF))
        ones = pick(spare, 1.0, 0.0, v_all.shape)
        values.append(pick(own, v_all, ones, v_all.shape).T.astype(BF))

    def scores_of(unit):
        block, head = unit
        rows = slice(block * BLOCK, (block + 1) * BLOCK)
        extent = (block + 1) * BLOCK if causal else sources
        own, spare = head_lanes(head)
        q_block = q_ref[rows, :].astype(F32)
        ones = pick(spare, 1.0, 0.0, q_block.shape)
        scores = dot_nt(keys[head][:extent], pick(own, q_block, ones, q_block.shape).astype(BF))
        if causal:
            edge = causal_edge(scores[extent - BLOCK:], MASKED)
            scores = edge if extent == BLOCK else jnp.concatenate([scores[: extent - BLOCK], edge], axis=0)
        return scores

    parts = {}

    def finish(unit, expo, highest):
        block, head = unit
        rows = slice(block * BLOCK, (block + 1) * BLOCK)
        mixed = dot_nn(values[head][:, : expo.shape[0]], expo)
        at = HDIM if head == 0 else 0
        total = mixed[at:at + 1]
        lse_ref[0, head:head + 1, rows] = highest + jnp.log(total)
        parts[unit] = mixed[head * HDIM:(head + 1) * HDIM] * (1.0 / total)
        if head == 1:
            o_ref[rows, :] = jnp.concatenate([parts[(block, 0)], parts[unit]], axis=0).T.astype(BF)

    units = [(block, head) for block in range(count // BLOCK) for head in range(2)]
    ahead = [scores_of(unit) for unit in units[:2]]
    before = None
    for at, unit in enumerate(units):
        if at + 2 < len(units):
            ahead.append(scores_of(units[at + 2]))
        highest = jnp.max(ahead[at], axis=0, keepdims=True)
        expo = jnp.exp(ahead[at] - highest).astype(BF)
        if before is not None:
            finish(*before)
        before = (unit, expo, highest)
    finish(*before)


def attend_backward_kernel(
    causal, limit_ref, q_ref, k_ref, v_ref, o_ref, do_ref, lse_ref, dq_ref, dk_ref, dv_ref, sums_ref, dq_acc
):
    count, sources = q_ref.shape[0], k_ref.shape[0]
    q_all, k_all = q_ref[...].astype(F32), k_ref[...].astype(F32)
    do_all = do_ref[...].astype(F32)
    bias = length_bias(sources, limit_ref[0])
    product = (do_all * o_ref[...].astype(F32)).T
    q_aug, q_own, k_aug, kt_own, do_own, delta, lse = [], [], [], [], [], [], []
    for head in range(2):
        own, spare = head_lanes(head)
        q_aug.append(pick(own, q_all, pick(spare, 1.0, 0.0, q_all.shape), q_all.shape).astype(BF))
        q_own.append(pick(own, q_all, 0.0, q_all.shape).astype(BF))
        k_aug.append(pick(spare, bias, k_all, k_all.shape).astype(BF))
        kt_own.append(pick(own, k_all, 0.0, k_all.shape).T.astype(BF))
        do_own.append(pick(own, do_all, 0.0, do_all.shape).astype(BF))
        delta.append(jnp.sum(product[head * HDIM:(head + 1) * HDIM], axis=0, keepdims=True))
        lse.append(lse_ref[0, head:head + 1, :])

    def products(unit):
        block, head = unit
        rows = slice(block * BLOCK, (block + 1) * BLOCK)
        first = block * BLOCK if causal else 0
        return (
            dot_nt(k_aug[head][rows], q_aug[head][first:]),
            dot_nt(v_ref[rows, :], do_own[head][first:]),
        )

    def gradients(unit, scores, d_probs):
        block, head = unit
        first = block * BLOCK if causal else 0
        probs = jnp.exp(scores - lse[head][:, first:])
        if causal:
            edge = causal_edge(probs[:, :BLOCK], 0.0)
            probs = edge if first + BLOCK == count else jnp.concatenate([edge, probs[:, BLOCK:]], axis=1)
        d_scores = (probs * (d_probs - delta[head][:, first:])).astype(BF)
        return probs.astype(BF), d_scores

    held = {}

    def finish(unit, probs, d_scores):
        block, head = unit
        rows = slice(block * BLOCK, (block + 1) * BLOCK)
        first = block * BLOCK if causal else 0
        dv = dot_nn(probs, do_own[head][first:])
        dk = dot_nn(d_scores, q_own[head][first:])
        dq = dot_nn(kt_own[head][:, rows], d_scores)
        if head == 0:
            held[block] = (dv, dk, dq)
            return
        dv = (held[block][0] + dv).astype(BF)
        dv_ref[rows, :] = dv
        held["dv"] = held.get("dv", 0.0) + column_sum(dv)
        dk_ref[rows, :] = (held[block][1] + dk).astype(BF)
        if block == 0:
            dq_acc[...] = held[block][2] + dq
        else:
            dq_acc[:, first:] += held[block][2] + dq

    units = [(block, head) for block in range(sources // BLOCK) for head in range(2)]
    ahead = [products(units[0])]
    before = None
    for at, unit in enumerate(units):
        if at + 1 < len(units):
            ahead.append(products(units[at + 1]))
        current = (unit,) + gradients(unit, *ahead[at])
        if before is not None:
            finish(*before)
        before = current
    finish(*before)
    dq = dq_acc[...].T.astype(BF)
    dq_ref[...] = dq
    sums_ref[...] = jnp.concatenate([column_sum(dq) * FACTOR, held["dv"], jnp.zeros((6, PAIR), F32)], axis=0)


def attend_call(kernel, name, causal, work, specs, arrays, out_specs, outs, scratch, limit, pairs, held):
    first, last = pairs
    held = list(held)

    def shifted(spec):
        if spec is None:
            return pl.BlockSpec(memory_space=pltpu.SMEM)
        shape, index = spec
        return pl.BlockSpec(shape, lambda i: index(i + first))

    def body(*refs):
        kernel(causal, *refs[: len(specs)], *refs[len(specs) + len(held):])

    return pl.pallas_call(
        body,
        grid=(last - first,),
        in_specs=[shifted(spec) for spec in specs] + [pl.BlockSpec(memory_space=pl.ANY)] * len(held),
        out_specs=[shifted(spec) for spec in out_specs],
        out_shape=outs,
        scratch_shapes=scratch,
        input_output_aliases={len(specs) + at: at for at in range(len(held))},
        compiler_params=pltpu.CompilerParams(vmem_limit_bytes=limit << 20),
        cost_estimate=pl.CostEstimate(flops=8 * work * (last - first) * PAIR, bytes_accessed=1 << 20, transcendentals=0),
        name=name,
    )(*arrays, *held)


def attend_forward(q, k, v, limit, causal, pairs=None, held=()):
    count, width = q.shape
    sources = k.shape[0]
    total = width // PAIR
    of_q = ((count, PAIR), lambda i: (0, i))
    of_k = ((sources, PAIR), lambda i: (0, i))
    stats = ((1, 2, count), lambda i: (i, 0, 0))
    outs = [jax.ShapeDtypeStruct((count, width), BF), jax.ShapeDtypeStruct((total, 2, count), F32)]
    return attend_call(
        attend_forward_kernel, "attend_forward", causal, 16 * count * sources * (5 if causal else 8) // 8,
        [None, of_q, of_k, of_k], [limit, q, k, v], [of_q, stats], outs, [], ATTEND_VMEM, pairs or (0, total), held,
    )


def attend_backward(q, k, v, o, do, lse, limit, causal, pairs=None, held=(), memory=ATTEND_VMEM):
    count, width = q.shape
    sources = k.shape[0]
    total = width // PAIR
    of_q = ((count, PAIR), lambda i: (0, i))
    of_k = ((sources, PAIR), lambda i: (0, i))
    stats = ((1, 2, count), lambda i: (i, 0, 0))
    outs = [
        jax.ShapeDtypeStruct((count, width), BF),
        jax.ShapeDtypeStruct((sources, width), BF),
        jax.ShapeDtypeStruct((sources, width), BF),
        jax.ShapeDtypeStruct((8, width), F32),
    ]
    return attend_call(
        attend_backward_kernel, "attend_backward", causal, 40 * count * sources * (5 if causal else 8) // 8,
        [None, of_q, of_k, of_k, of_q, of_q, stats], [limit, q, k, v, o, do, lse],
        [of_q, of_k, of_k, ((8, PAIR), lambda i: (0, i))], outs, [pltpu.VMEM((PAIR, count), F32)], memory,
        pairs or (0, total), held,
    )


WHOLE = pl.BlockSpec(memory_space=pltpu.VMEM)
DENSE_VMEM = 32
FFN_VMEM = 48
FFN_ROWS = 256
GRAD_VMEM = 56
SMALL_VMEM = 16
LARGE_VMEM = 58
ANYWHERE = pl.BlockSpec(memory_space=pl.ANY)
SCALAR = pl.BlockSpec(memory_space=pltpu.SMEM)
SLAB = 32


def params(limit):
    return pltpu.CompilerParams(vmem_limit_bytes=limit << 20)


def full(value):
    shape = tuple(value.shape)
    return pl.BlockSpec(shape, lambda *_: (0,) * len(shape), pipeline_mode=pl.Buffered(1))


def cost(flops, *arrays):
    size = sum(a.size * a.dtype.itemsize for a in arrays)
    return pl.CostEstimate(flops=8 * flops, bytes_accessed=size, transcendentals=0)


def of(*shape, dtype=BF):
    return jax.ShapeDtypeStruct(shape, dtype)


def matrix(bundle, index):
    owners, width = bundle.shape[0], bundle.shape[2]
    part = width // owners
    return bundle[:, index * part:(index + 1) * part, :].reshape(width, width)


def bring(refs, holds, sem):
    copies = [pltpu.make_async_copy(ref, hold, sem.at[at]) for at, (ref, hold) in enumerate(zip(refs, holds))]
    for copy in copies:
        copy.start()
    return copies


def one_matrix(bundle, index):
    owners, width = bundle.shape[0], bundle.shape[2]
    return pl.BlockSpec((owners, width // owners, width), lambda *_: (0, index, 0), pipeline_mode=pl.Buffered(1))


def fetch(me, pieces, bundle, sem, first):
    copies = []
    shard = max(offset + rows for (_, offset, rows), _ in pieces)
    for at, ((relative, offset, rows), piece) in enumerate(pieces):
        owner = jnp.bitwise_xor(me, relative)
        if len(bundle.shape) == 3:
            target = bundle.at[owner, pl.ds(offset, rows)]
        else:
            target = bundle.at[pl.ds(pl.multiple_of(owner * shard + offset, 16), rows)]
        copies.append(pltpu.make_async_copy(piece, target, sem.at[first + at]))
        copies[-1].start()
    return copies


def wait_all(copies):
    for copy in copies:
        copy.wait()


def leave(inside, outside, sem, at):
    return pltpu.make_async_copy(inside, outside, sem.at[at])


def at_first(action):
    pl.when(pl.program_id(0) == 0)(action)


def at_last(action):
    pl.when(pl.program_id(0) == pl.num_programs(0) - 1)(action)


def normalise(summed):
    centred = summed - jnp.mean(summed, axis=-1, keepdims=True)
    inverse = lax.rsqrt(jnp.mean(centred * centred, axis=-1, keepdims=True) + 1e-05)
    return centred * inverse, inverse


def norm_backward(d_out, normed, inverse, gain):
    d_normed = d_out * gain
    return inverse * (
        d_normed
        - jnp.mean(d_normed, axis=-1, keepdims=True)
        - normed * jnp.mean(d_normed * normed, axis=-1, keepdims=True)
    )


def gelu_parts(a):
    bell = jnp.exp(-0.5 * a * a)
    t = 1.0 / (1.0 + 0.23164189 * jnp.abs(a))
    tail = t * (0.127414796 + t * (-0.142248368 + t * (0.7107068705 + t * (-0.7265760135 + t * 0.5307027145)))) * bell
    phi = jnp.where(a >= 0.0, 1.0 - tail, tail)
    return a * phi, phi + a * bell * 0.3989422804014327


def add_rows(ref, rows):
    block = jnp.concatenate(rows + [jnp.zeros((ref.shape[0] - len(rows), ref.shape[1]), F32)], axis=0)

    @pl.when(pl.program_id(0) == 0)
    def _():
        ref[...] = block

    @pl.when(pl.program_id(0) > 0)
    def _():
        ref[...] += block


def pack_kernel(matrix_ref, *refs):
    count = (len(refs) - 3) // 2
    vectors, out, holds, slab, sem = refs[:count], refs[count], refs[count + 1:-2], refs[-2], refs[-1]
    rows = matrix_ref.shape[0]
    whole = pltpu.make_async_copy(matrix_ref, out.at[pl.ds(0, rows)], sem.at[count])
    whole.start()
    copies = bring(vectors, holds, sem)
    slab[...] = jnp.zeros(slab.shape, F32)
    row = 0
    for copy, hold in zip(copies, holds):
        copy.wait()
        slab[row:row + hold.shape[0], : hold.shape[1]] = hold[...].astype(F32)
        row += hold.shape[0]
    out[rows:, :] = slab[...].astype(BF)
    whole.wait()


def pack(value, vectors):
    rows, width = value.shape
    total = rows + SLAB // 2
    return pl.pallas_call(
        pack_kernel,
        grid=(1,),
        in_specs=[ANYWHERE] * (1 + len(vectors)),
        out_specs=full(of(total, width)),
        out_shape=of(total, width),
        scratch_shapes=[pltpu.VMEM(vector.shape, BF) for vector in vectors] + [
            pltpu.VMEM((SLAB // 2, width), F32), pltpu.SemaphoreType.DMA((len(vectors) + 1,)),
        ],
        compiler_params=params(LARGE_VMEM),
        name="pack_self",
    )(value, *vectors)


def project_kernel(layout, me_ref, x, *refs):
    pieces, (w_out, vec, q_ref, k_ref, v_ref, w, sem) = refs[: len(layout)], refs[len(layout):]
    owners, width = w.shape[0], w.shape[2]
    part = width // owners

    @at_first
    def _():
        wait_all(fetch(me_ref[0], list(zip(layout, pieces)), w, sem, 0))
        leave(w, w_out, sem, len(layout)).start()
        vec[...] = jnp.zeros(vec.shape, F32)
        if owners == 1:
            vec[:17, :] = w[0, 3 * part:, :].astype(F32)[:17, :]
        else:
            wide = 4 * width // owners
            for owner in range(owners):
                slab = w[owner, 3 * part:, :].astype(F32)
                vec[:12, owner * part:(owner + 1) * part] = slab[:12, :part]
                vec[16:17, owner * part:(owner + 1) * part] = slab[13:14, :part]
                at = owner * wide
                vec[12 + at // width:13 + at // width, at % width:at % width + wide] = slab[12:13, :wide]

    values = x[...]
    q_ref[...] = ((dot_nn(values, matrix(w, 0)) + vec[0:1, :]) * FACTOR).astype(BF)
    k_ref[...] = dot_nn(values, matrix(w, 1)).astype(BF)
    v_ref[...] = (dot_nn(values, matrix(w, 2)) + vec[1:2, :]).astype(BF)
    at_last(lambda: leave(w, w_out, sem, len(layout)).wait())


def project(me, x, pieces, owners):
    count, width = x.shape
    rows = pl.BlockSpec((ROWS, width), lambda i: (i, 0))
    layout = [key for key, _ in pieces]
    bundle = (owners, max(offset + size for _, offset, size in layout), width)
    return pl.pallas_call(
        lambda *refs: project_kernel(layout, *refs),
        grid=(count // ROWS,),
        in_specs=[SCALAR, rows] + [ANYWHERE] * len(pieces),
        out_specs=[ANYWHERE, full(of(24, width)), rows, rows, rows],
        out_shape=[of(*bundle), of(24, width, dtype=F32)] + [of(count, width)] * 3,
        scratch_shapes=[
            pltpu.VMEM(bundle, BF),
            pltpu.SemaphoreType.DMA((len(pieces) + 1,)),
        ],
        compiler_params=params(DENSE_VMEM),
        cost_estimate=cost(6 * count * width * width, x, x, x, x, x),
        name="self_project",
    )(me, x, *[piece for _, piece in pieces])


def between_kernel(layout, me_ref, vec, o, x, mem, *refs):
    pieces, (w_out, z_ref, r_ref, h_ref, q_ref, k_ref, v_ref, w, sem) = refs[: len(layout)], refs[len(layout):]

    @at_first
    def _():
        wait_all(fetch(me_ref[0], list(zip(layout, pieces)), w, sem, 0))
        leave(w, w_out, sem, len(layout)).start()

    summed = x[...].astype(F32) + dot_nn(o[...], matrix(w, 3)) + vec[2:3, :]
    source = mem[...]
    k_ref[...] = dot_nn(source, matrix(w, 1)).astype(BF)
    v_ref[...] = (dot_nn(source, matrix(w, 2)) + vec[4:5, :]).astype(BF)
    z, r = normalise(summed)
    z_ref[...] = z
    r_ref[...] = jnp.broadcast_to(r, r_ref.shape)
    hidden = (z * vec[6:7, :] + vec[9:10, :]).astype(BF)
    h_ref[...] = hidden
    q_ref[...] = ((dot_nn(hidden, matrix(w, 0)) + vec[3:4, :]) * FACTOR).astype(BF)
    at_last(lambda: leave(w, w_out, sem, len(layout)).wait())


def between(me, vec, o, x, mem, pieces, owners):
    count, width = x.shape
    rows = pl.BlockSpec((ROWS, width), lambda i: (i, 0))
    layout = [key for key, _ in pieces]
    bundle = (owners, 5 * width // owners, width)
    return pl.pallas_call(
        lambda *refs: between_kernel(layout, *refs),
        grid=(count // ROWS,),
        in_specs=[SCALAR, full(vec), rows, rows, rows] + [ANYWHERE] * len(pieces),
        out_specs=[ANYWHERE, rows, pl.BlockSpec((ROWS, 128), lambda i: (i, 0))] + [rows] * 4,
        out_shape=[of(*bundle), of(count, width, dtype=F32), of(count, 128, dtype=F32)] + [of(count, width)] * 4,
        scratch_shapes=[pltpu.VMEM(bundle, BF), pltpu.SemaphoreType.DMA((len(pieces) + 1,))],
        compiler_params=params(DENSE_VMEM),
        cost_estimate=cost(8 * count * width * width, x, x, x, x, x, x, x, x, x),
        name="self_out_cross_project",
    )(me, vec, o, x, mem, *[piece for _, piece in pieces])


def ffn_kernel(layouts, me_ref, vec, o, z_in, cot, wo, *refs):
    count = len(layouts[0])
    ins, outs = refs[:count], refs[count:count + len(layouts[1])]
    (mixed, act_ref, da_ref, df_ref, h_ref, dy_ref, db_ref, do_ref, sums_ref, w_in, w_out, slope, sem) = (
        refs[count + len(layouts[1]):]
    )
    width = o.shape[1]
    chunks = w_in.shape[1] // width
    in_copies = list(zip(layouts[0], ins)), list(zip(layouts[1], outs))

    @at_first
    def _():
        copies = fetch(me_ref[0], in_copies[0], w_in, sem, 0) + fetch(me_ref[0], in_copies[1], w_out, sem, count)
        wait_all(copies)

    gains = [vec[6 + i:7 + i, :] for i in range(3)]
    shifts = [vec[9 + i:10 + i, :] for i in range(3)]
    first = z_in[...] * gains[0] + shifts[0]
    z_two, r_two = normalise(first + dot_nn(o[...], matrix(wo, 0)) + vec[5:6, :])
    second = z_two * gains[1] + shifts[1]
    hidden = second.astype(BF)
    h_ref[...] = hidden

    def columns(c):
        return slice(c * width, (c + 1) * width)

    total = second + vec[16:17, :]
    ahead = dot_nn(hidden, w_in[:, columns(0)])
    before = None
    for c in range(chunks):
        pre = ahead + vec[12 + c:13 + c, :]
        if c + 1 < chunks:
            ahead = dot_nn(hidden, w_in[:, columns(c + 1)])
        act, grad = gelu_parts(pre)
        act = act.astype(BF)
        act_ref[:, columns(c)] = act
        slope[:, columns(c)] = grad
        if before is not None:
            total = total + dot_nn(before, w_out[columns(c - 1), :])
        before = act
    total = total + dot_nn(before, w_out[columns(chunks - 1), :])
    z, r = normalise(total)
    mixed[...] = (z * gains[2] + shifts[2]).astype(BF)
    incoming = cot[...].astype(F32)
    dy_three = norm_backward(incoming, z, r, gains[2])
    df = dy_three.astype(BF)
    df_ref[...] = df
    rows = [column_sum(df), column_sum(incoming * z), column_sum(incoming)]

    da_sums = []
    d_two = dy_three
    ahead = dot_nt(df, w_out[columns(0), :])
    before = None
    for c in range(chunks):
        d_act = ahead
        if c + 1 < chunks:
            ahead = dot_nt(df, w_out[columns(c + 1), :])
        da = (d_act * slope[:, columns(c)]).astype(BF)
        da_ref[:, columns(c)] = da
        da_sums.append(column_sum(da))
        if before is not None:
            d_two = d_two + dot_nt(before, w_in[:, columns(c - 1)])
        before = da
    d_two = d_two + dot_nt(before, w_in[:, columns(chunks - 1)])
    dy_two = norm_backward(d_two, z_two, r_two, gains[1])
    dy_ref[...] = dy_two
    db = dy_two.astype(BF)
    db_ref[...] = db
    do_ref[...] = dot_nt(db, matrix(wo, 0)).astype(BF)
    rows += [column_sum(d_two * z_two), column_sum(d_two), column_sum(db)]
    add_rows(sums_ref, rows + da_sums)


def ffn(me, vec, o, z, cot, wo, ins, outs, hidden):
    count, width = o.shape
    rows = pl.BlockSpec((FFN_ROWS, width), lambda i: (i, 0))
    wide = pl.BlockSpec((FFN_ROWS, hidden), lambda i: (i, 0))
    layouts = [key for key, _ in ins], [key for key, _ in outs]
    return pl.pallas_call(
        lambda *refs: ffn_kernel(layouts, *refs),
        grid=(count // FFN_ROWS,),
        in_specs=[SCALAR, full(vec), rows, rows, rows, one_matrix(wo, 4)] + [ANYWHERE] * (len(ins) + len(outs)),
        out_specs=[rows, wide, wide, rows, rows, rows, rows, rows, pl.BlockSpec((16, width), lambda i: (0, 0))],
        out_shape=[
            of(count, width), of(count, hidden), of(count, hidden), of(count, width), of(count, width),
            of(count, width, dtype=F32), of(count, width), of(count, width), of(16, width, dtype=F32),
        ],
        scratch_shapes=[
            pltpu.VMEM((width, hidden), BF),
            pltpu.VMEM((hidden, width), BF),
            pltpu.VMEM((FFN_ROWS, hidden), F32),
            pltpu.SemaphoreType.DMA((len(ins) + len(outs),)),
        ],
        compiler_params=params(FFN_VMEM),
        cost_estimate=cost(8 * count * width * hidden + 4 * count * width * width, o, z, z, cot, o, o, o, o),
        name="ffn",
    )(me, vec, o, z, cot, wo, *[piece for _, piece in ins + outs])


def cross_back_kernel(vec, dq, dy, z, r, w, wo, dy_ref, db_ref, do_ref, sums_ref):
    d_one = dy[...] + dot_nt(dq[...], matrix(w, 0)) * FACTOR
    normed = z[...]
    dy_one = norm_backward(d_one, normed, r[:, :1], vec[6:7, :])
    dy_ref[...] = dy_one
    db = dy_one.astype(BF)
    db_ref[...] = db
    do_ref[...] = dot_nt(db, matrix(wo, 0)).astype(BF)
    add_rows(sums_ref, [column_sum(d_one * normed), column_sum(d_one), column_sum(db)])


def cross_back(vec, dq, dy, z, r, w):
    count, width = dq.shape
    rows = pl.BlockSpec((ROWS, width), lambda i: (i, 0))
    return pl.pallas_call(
        cross_back_kernel,
        grid=(count // ROWS,),
        in_specs=[full(vec)] + [rows] * 3 + [pl.BlockSpec((ROWS, 128), lambda i: (i, 0)), one_matrix(w, 0), one_matrix(w, 3)],
        out_specs=[rows] * 3 + [pl.BlockSpec((8, width), lambda i: (0, 0))],
        out_shape=[of(count, width, dtype=F32), of(count, width), of(count, width), of(8, width, dtype=F32)],
        compiler_params=params(DENSE_VMEM),
        cost_estimate=cost(4 * count * width * width, dq, dy, z, dy, dq, dq, dq, dq),
        name="cross_query_back",
    )(vec, dq, dy, z, r, w, w)


def memory_back_kernel(dk, dv, wk, wv, out):
    out[...] = dot_nt(dk[...], matrix(wk, 0)) + dot_nt(dv[...], matrix(wv, 0))


def memory_back(dk, dv, w):
    count, width = dk.shape
    rows = pl.BlockSpec((ROWS, width), lambda i: (i, 0))
    return pl.pallas_call(
        memory_back_kernel,
        grid=(count // ROWS,),
        in_specs=[rows, rows, one_matrix(w, 1), one_matrix(w, 2)],
        out_specs=rows,
        out_shape=of(count, width, dtype=F32),
        compiler_params=params(DENSE_VMEM),
        cost_estimate=cost(4 * count * width * width, dk, dv, dk, dk, dk, dk),
        name="memory_back",
    )(dk, dv, w, w)


def self_back_kernel(dq, dk, dv, dy, w, out):
    total = dy[...] + dot_nt(dq[...], matrix(w, 0)) * FACTOR
    out[...] = total + dot_nt(dk[...], matrix(w, 1)) + dot_nt(dv[...], matrix(w, 2))


def self_back(dq, dk, dv, dy, w):
    count, width = dq.shape
    rows = pl.BlockSpec((ROWS, width), lambda i: (i, 0))
    return pl.pallas_call(
        self_back_kernel,
        grid=(count // ROWS,),
        in_specs=[rows] * 4 + [full(w)],
        out_specs=rows,
        out_shape=of(count, width, dtype=F32),
        compiler_params=params(DENSE_VMEM),
        cost_estimate=cost(6 * count * width * width, dq, dk, dv, dy, dy, w),
        name="self_project_back",
    )(dq, dk, dv, dy, w)


def hand_out(me, hold, keep, send, sem, rows, first):
    copies = []
    for relative in range(8):
        source = hold.at[jnp.bitwise_xor(me, relative), rows]
        target = (send if relative % 2 else keep).at[relative // 2, rows]
        copies.append(pltpu.make_async_copy(source, target, sem.at[first + relative]))
        copies[-1].start()
    return copies


def weight_grad_kernel(items, parts, count, me_ref, *refs):
    held = len(parts)
    outside, slabs = refs[:count], refs[count:-(held + 5)]
    keep, send = refs[-(held + 5):-(held + 3)]
    holds, hold, extra, sem = refs[-(held + 3):-3], refs[-3], refs[-2], refs[-1]
    width = hold.shape[2]
    part = width // 8
    coming = bring([outside[at].at[:, pl.ds(chunk * width, width)] for at, chunk in parts], holds, sem)
    waited = set()
    leaving, done = [], 0
    for at, (left, right, scale) in enumerate(items):
        for index in (left, right):
            if index not in waited:
                coming[index].wait()
                waited.add(index)
        product = dot_tn(holds[left][...], holds[right][...])
        product = product if scale == 1.0 else product * scale
        hold[:, at * part:(at + 1) * part, :] = product.astype(BF).reshape(8, part, width)
        if at == len(items) - 2:
            done = (at + 1) * part
            leaving += hand_out(me_ref[0], hold, keep, send, sem, pl.ds(0, done), held)
    if slabs:
        row = 0
        extra[...] = jnp.zeros(extra.shape, F32)
        for ref in slabs:
            extra[row:row + ref.shape[0], :] = ref[...]
            row += ref.shape[0]
        block = extra[...].astype(BF)
        for owner in range(8):
            hold[owner, part * len(items):, :] = block
    leaving += hand_out(me_ref[0], hold, keep, send, sem, pl.ds(done, hold.shape[1] - done), held + 8)
    wait_all(leaving)


def weight_grad(me, operands, parts, items, name, slabs=(), slab_rows=0):
    count, width = operands[0].shape
    rows = width // 8 * len(items) + slab_rows
    return pl.pallas_call(
        lambda *refs: weight_grad_kernel(items, parts, len(operands), *refs),
        grid=(1,),
        in_specs=[SCALAR] + [ANYWHERE] * len(operands) + [full(slab) for slab in slabs],
        out_specs=[ANYWHERE, ANYWHERE],
        out_shape=[of(4, rows, width)] * 2,
        scratch_shapes=[pltpu.VMEM((count, width), BF) for _ in parts] + [
            pltpu.VMEM((8, rows, width), BF),
            pltpu.VMEM((max(slab_rows, 8), width), F32),
            pltpu.SemaphoreType.DMA((len(parts) + 16,)),
        ],
        compiler_params=params(GRAD_VMEM),
        cost_estimate=cost(2 * count * width * width * len(items), *operands),
        name=name,
    )(me, *operands, *slabs)


def tall_grad_kernel(me_ref, left, right, keep, send, left_hold, right_hold, hold, sem):
    width = right.shape[1]
    chunks = left.shape[1] // width
    chip, core = me_ref[0] // 2, lax.rem(me_ref[0], 2)
    coming = [pltpu.make_async_copy(right, right_hold, sem.at[0])]
    for c in range(chunks):
        span = pl.ds(pl.multiple_of(jnp.bitwise_xor(chip, c) * width, width), width)
        coming.append(pltpu.make_async_copy(left.at[:, span], left_hold.at[c], sem.at[1 + c]))
    for copy in coming:
        copy.start()
    coming[0].wait()
    leaving = []
    for c in range(chunks):
        coming[1 + c].wait()
        product = dot_tn(left_hold[c], right_hold[...])
        hold[c] = product.astype(BF).reshape(hold.shape[1:])
        for at, (index, out) in enumerate(((core, keep), (1 - core, send))):
            leaving.append(pltpu.make_async_copy(hold.at[c, index], out.at[c], sem.at[1 + chunks + 2 * c + at]))
            leaving[-1].start()
    wait_all(leaving)


def tall_grad(me, left, right, name):
    (count, tall), width = left.shape, right.shape[1]
    chunks = tall // width
    return pl.pallas_call(
        tall_grad_kernel,
        grid=(1,),
        in_specs=[SCALAR, ANYWHERE, ANYWHERE],
        out_specs=[ANYWHERE, ANYWHERE],
        out_shape=[of(4, tall // 8, width)] * 2,
        scratch_shapes=[
            pltpu.VMEM((chunks, count, width), BF),
            pltpu.VMEM(right.shape, BF),
            pltpu.VMEM((chunks, 2, tall // 8, width), BF),
            pltpu.SemaphoreType.DMA((1 + 3 * chunks,)),
        ],
        compiler_params=params(GRAD_VMEM),
        cost_estimate=cost(2 * count * tall * width, left, left, right),
        name=name,
    )(me, left, right)


def swap(value, bit, axis="fsdp", size=8):
    return lax.ppermute(value, axis, [(i, i ^ bit) for i in range(size)])


def tie(*values):
    return lax.optimization_barrier(values)


def local(kernel, name, out_shape, *args, scratch=(), scalars=0):
    return pl.pallas_call(
        kernel,
        in_specs=[SCALAR] * scalars + [WHOLE] * (len(args) - scalars),
        out_specs=[WHOLE] * len(out_shape),
        out_shape=out_shape,
        scratch_shapes=scratch,
        compiler_params=params(SMALL_VMEM),
        cost_estimate=cost(0, *args, *out_shape),
        name=name,
    )(*args)


def halves(rows):
    return rows // 32 * 16


def split_kernel(keep, came, own, to_x, to_y, rest_y, rest_x):
    half = rest_y.shape[0]

    def total(index, rows):
        return keep[index, rows, :].astype(F32) + came[index, rows, :].astype(F32)

    low, high = slice(None, half), slice(half, None)
    own[...] = total(0, slice(None))
    to_x[0], to_x[1] = total(1, low).astype(BF), total(3, low).astype(BF)
    to_y[0], to_y[1] = total(2, high).astype(BF), total(3, high).astype(BF)
    rest_y[...] = total(2, low).astype(BF)
    rest_x[...] = total(1, high).astype(BF)


def reduce_core(keep, send):
    return [keep, swap(send, 1)]


def reduce_first(state):
    keep, came = state
    rows, width = keep.shape[1:]
    low, high = halves(rows), rows - halves(rows)
    shapes = [of(rows, width, dtype=F32), of(2, low, width), of(2, high, width), of(low, width), of(high, width)]
    own, to_x, to_y, rest_y, rest_x = local(split_kernel, "grad_split", shapes, keep, came)
    return [own, rest_y, rest_x, swap(to_x, 2), swap(to_y, 4)]


def second_kernel(own, rest_y, rest_x, from_x, from_y, out, last_y, last_x):
    half = rest_y.shape[0]
    out[:half, :] = own[:half, :] + from_x[0].astype(F32)
    out[half:, :] = own[half:, :] + from_y[0].astype(F32)
    last_y[...] = (rest_y[...].astype(F32) + from_x[1].astype(F32)).astype(BF)
    last_x[...] = (rest_x[...].astype(F32) + from_y[1].astype(F32)).astype(BF)


def reduce_second(state):
    own, rest_y, rest_x = state[:3]
    shapes = [of(*own.shape, dtype=F32), of(*rest_y.shape), of(*rest_x.shape)]
    out, last_y, last_x = local(second_kernel, "grad_second", shapes, *state)
    return [out, swap(last_y, 4), swap(last_x, 2)]


def joined_kernel(own, got_y, got_x, *outs):
    half = got_y.shape[0]
    at = 0
    for out in outs:
        rows = out.shape[-2] * (out.shape[0] if len(out.shape) == 3 else 1)
        value = own[at:at + rows, :]
        parts = []
        if at < half:
            parts.append(got_y[at:min(half, at + rows), :].astype(F32))
        if at + rows > half:
            parts.append(got_x[max(at, half) - half:at + rows - half, :].astype(F32))
        value = value + (parts[0] if len(parts) == 1 else jnp.concatenate(parts, axis=0))
        out[...] = value.astype(BF).reshape(out.shape)
        at += rows


def inward(value):
    return [value, lax.ppermute(value, "dp", [(0, 1), (3, 2)])]


def reduce_inward(state, chunks=1):
    rows, width = state[0].shape
    step = rows // chunks // 16 * 16
    sizes = [step] * (chunks - 1) + [rows - step * (chunks - 1)]
    values = local(joined_kernel, "grad_join", [of(size, width) for size in sizes], *state)
    return [inward(value) for value in values]


def pair_kernel(one, two, out):
    out[...] = (one[...].astype(F32) + two[...].astype(F32)).astype(BF)


def reduce_across(state):
    (side,) = local(pair_kernel, "grad_add", [of(*state[0].shape)], *state)
    return [side, lax.ppermute(side, "dp", [(1, 2), (2, 1)])]


def reduce_outward(state):
    (total,) = local(pair_kernel, "grad_add", [of(*state[0].shape)], *state)
    return [total, lax.ppermute(total, "dp", [(1, 0), (2, 3)])]


def exchange(value):
    return lax.all_to_all(value, "dp", 0, 0)


def reduce_joined(state):
    rows, width = state[0].shape
    return local(joined_kernel, "grad_join", [of(4, rows // 4, width)], *state)[0]


def four_kernel(parts, out):
    total = parts[0].astype(F32) + parts[1].astype(F32) + parts[2].astype(F32) + parts[3].astype(F32)
    for index in range(4):
        out[index] = total.astype(BF)


def reduce_added(parts):
    return local(four_kernel, "grad_add", [of(*parts.shape)], parts)[0]


def place_kernel(spans, at_ref, *refs):
    count = len(refs) - 1 - len(spans)
    ins, outs, hold = refs[:count], refs[count:-1], refs[-1]
    at = at_ref[0]
    middle = (at == 1) | (at == 2)
    if count == 1:
        rows = ins[0].shape[1]
        for index in range(4):
            hold[index * rows:(index + 1) * rows, :] = ins[0][index].astype(F32)
    else:
        row = 0
        for total, came in zip(ins[::2], ins[1::2]):
            rows = total.shape[0]
            hold[row:row + rows, :] = jnp.where(middle, total[...].astype(F32), came[...].astype(F32))
            row += rows
    for (first, count, columns), out in zip(spans, outs):
        if len(out.shape) == 3:
            for index in range(out.shape[0]):
                out[index] = hold[first + index * out.shape[1]:first + (index + 1) * out.shape[1], :]
        else:
            for column in range(columns):
                begin = first + column * count
                out[:, column * hold.shape[1]:(column + 1) * hold.shape[1]] = hold[begin:begin + count, :]


def reduce_end(arrays, rows, spans, shapes):
    width = arrays[0].shape[-1]
    at = lax.axis_index("dp").astype(jnp.int32).reshape(1)
    return local(
        lambda *refs: place_kernel(spans, *refs), "grad_place", shapes, at, *arrays,
        scratch=[pltpu.VMEM((rows, width), F32)], scalars=1,
    )


def small_kernel(me_ref, early, back, late, self_b, cross_b, gain, shift, b_in, b_out):
    me = me_ref[0]
    width, part = early.shape[1], self_b.shape[1]
    turn = lax.rem(width - me * part, width)

    def own(ref, row):
        return pltpu.roll(ref[row // 8 * 8:row // 8 * 8 + 8, :], turn, 1)[row % 8:row % 8 + 1, :part]

    for ref, index in ((gain, 0), (shift, 1)):
        ref[0:1, :] = own(back, index)
        ref[1:2, :] = own(early, 3 + index)
        ref[2:3, :] = own(early, 1 + index)
    b_out[...] = own(early, 0)
    cross_b[0:1, :] = own(back, 8)
    cross_b[1:2, :] = own(back, 9)
    cross_b[2:3, :] = own(early, 5)
    self_b[0:1, :] = own(late, 0)
    self_b[1:2, :] = own(late, 1)
    self_b[2:3, :] = own(back, 2)
    wide = b_in.shape[1]
    row = early[pl.ds(6 + me * wide // width, 1), :]
    b_in[...] = jnp.where(lax.rem(me, 2) == 0, row[:, :wide], row[:, wide:])


def reduce_plain(sizes, blocks):
    value = lax.psum_scatter(blocks.astype(F32), "fsdp", scatter_dimension=0, tiled=False)
    return lax.psum(value.astype(BF), "dp").astype(F32)


def first_hops(shard):
    return swap(shard, 2), swap(shard, 4)


def pieces_of(shard, core, x, y, x_core, y_core, far, offsets=(0,)):
    rows = shard.shape[0]
    found = [((0, 0, rows), shard), ((1, 0, rows), core), ((2, 0, rows), x), ((4, 0, rows), y)]
    found += [((3, 0, rows), x_core), ((5, 0, rows), y_core)]
    for offset, piece in zip(offsets, far):
        found += [((6, offset, piece.shape[0]), piece), ((7, offset, piece.shape[0]), swap(piece, 1))]
    return found


def shards(sizes, target, memory, target_lengths, memory_lengths, self_qkv, self_bias, self_out, cross_qkv, cross_bias,
           cross_out, ffn_in, ffn_in_bias, ffn_out, ffn_out_bias, norm_gain, norm_bias, cotangent):
    n = sizes[0]
    fast = n == 8 and sizes[1] == 4
    width, hidden = target.shape[-1], ffn_in.shape[1]
    part, wide = width // n, hidden // n
    ratio = hidden // width
    x, mem, cot = target[0], memory[0], cotangent[0]
    place = lax.axis_index("fsdp").astype(jnp.int32)
    me = place.reshape(1)
    vectors = [self_bias, cross_bias, norm_gain, norm_bias, ffn_in_bias.reshape(1, wide), ffn_out_bias.reshape(1, part)]

    if fast:
        owners = 8
        own = pack(self_qkv.reshape(3 * part, width), vectors)
        s_x, s_y = first_hops(own)
        s_core = swap(own, 1)
        half = halves(own.shape[0])
        c_own = jnp.concatenate([cross_qkv.reshape(3 * part, width), self_out, cross_out])
        s_x, s_y, s_core, c_own, f_in, f_out = tie(s_x, s_y, s_core, c_own, ffn_in, ffn_out)
        c_core, f_in_core, f_out_core = [swap(member, 1) for member in (c_own, f_in, f_out)]
        s_low, s_high = swap(s_y[:half], 2), swap(s_x[half:], 4)
        s_x_core, s_y_core = swap(s_x, 1), swap(s_y, 1)
        c_x, c_y = first_hops(c_own)
        self_pieces = pieces_of(own, s_core, s_x, s_y, s_x_core, s_y_core, (s_low, s_high), (0, half))
    else:
        owners, me = 1, jnp.zeros((1,), jnp.int32)

        def gathered(member, axis):
            return lax.all_gather(member, "fsdp", axis=axis, tiled=True)

        def single(value):
            return [((0, 0, value.shape[0]), value)]

        fulls = [gathered(member, 1) for member in vectors[:4]]
        fulls += [gathered(ffn_in_bias, 0).reshape(ratio, width), gathered(ffn_out_bias, 0).reshape(1, width)]
        fulls = jnp.concatenate(fulls)
        fulls = jnp.pad(fulls, ((0, SLAB - fulls.shape[0]), (0, 0)))
        self_pieces = single(jnp.concatenate([gathered(self_qkv, 1).reshape(3 * width, width), fulls]))
        fulls = [gathered(cross_qkv, 1).reshape(3 * width, width), gathered(self_out, 0), gathered(cross_out, 0)]
        cross_pieces = single(jnp.concatenate(fulls))
        in_pieces, out_pieces = single(gathered(ffn_in, 0)), single(gathered(ffn_out, 0))

    pairs = width // PAIR
    early_pairs, late_pairs = (0, pairs // 2), (pairs // 2, pairs)
    self_w, vec, q, k, v = project(me, x, self_pieces, owners)
    if fast:
        q, c_x, c_y, f_in, f_out, c_core, f_in_core, f_out_core = tie(
            q, c_x, c_y, f_in, f_out, c_core, f_in_core, f_out_core
        )
        c_half = halves(c_own.shape[0])
        c_low, c_high = swap(c_y[:c_half], 2), swap(c_x[c_half:], 4)
        f_in_x, f_in_y = first_hops(f_in)
    o, lse = attend_forward(q, k, v, target_lengths, True)
    if fast:
        o, c_low, c_high, c_x, c_y, f_out = tie(o, c_low, c_high, c_x, c_y, f_out)
        cross_pieces = pieces_of(c_own, c_core, c_x, c_y, swap(c_x, 1), swap(c_y, 1), (c_low, c_high), (0, c_half))
        f_out_x, f_out_y = first_hops(f_out)
    cross_w, z_one, r_one, h_one, q2, k2, v2 = between(me, vec, o, x, mem, cross_pieces, owners)
    if fast:
        q2, f_in_x, f_in_y = tie(q2, f_in_x, f_in_y)
        f_in_far = swap(f_in_y, 2)
        f_in_x_core, f_in_y_core = swap(f_in_x, 1), swap(f_in_y, 1)
    half_one = attend_forward(q2, k2, v2, memory_lengths, False, early_pairs)
    if fast:
        q2, f_out_x, f_out_y, f_in_x_core, f_in_y_core, *half_one = tie(
            q2, f_out_x, f_out_y, f_in_x_core, f_in_y_core, *half_one
        )
        f_out_far = swap(f_out_x, 4)
        f_out_x_core, f_out_y_core = swap(f_out_x, 1), swap(f_out_y, 1)
    o2, lse2 = attend_forward(q2, k2, v2, memory_lengths, False, late_pairs, half_one)
    if fast:
        o2, f_in_far, f_out_far, f_out_x_core, f_out_y_core = tie(o2, f_in_far, f_out_far, f_out_x_core, f_out_y_core)
        in_pieces = pieces_of(f_in, f_in_core, f_in_x, f_in_y, f_in_x_core, f_in_y_core, (f_in_far,))
        out_pieces = pieces_of(f_out, f_out_core, f_out_x, f_out_y, f_out_x_core, f_out_y_core, (f_out_far,))
    mixed, act, da, df, h_two, dy, db2, do2, ffn_sums = ffn(
        me, vec, o2, z_one, cot, cross_w, in_pieces, out_pieces, hidden
    )
    if fast:
        out_state = reduce_core(*tall_grad(me, act, df, "ffn_out_grad"))
        h_two, out_state[0] = tie(h_two, out_state[0])
        operands, chunks = [h_two, da, o2, db2], [(0, 0)] + [(1, c) for c in range(ratio)] + [(2, 0), (3, 0)]
        items = [(0, 1 + c, 1.0) for c in range(ratio)] + [(1 + ratio, 2 + ratio, 1.0)]
        in_state = reduce_core(*weight_grad(me, operands, chunks, items, "ffn_in_grad", (ffn_sums,), SLAB // 2))
        do2, *out_state = tie(do2, *out_state)
        out_state = reduce_first(out_state)
        do2, in_state[0], out_state[0] = tie(do2, in_state[0], out_state[0])
    grads = attend_backward(q2, k2, v2, o2, do2, lse2, memory_lengths, False, early_pairs)
    if fast:
        do2, *states = tie(do2, *grads, *out_state, *in_state)
        grads, out_state, in_state = states[:4], reduce_second(states[4:9]), reduce_first(states[9:])
        do2, out_state[0], in_state[0] = tie(do2, out_state[0], in_state[0])
    dq2, dk2, dv2, cross_sums = attend_backward(q2, k2, v2, o2, do2, lse2, memory_lengths, False, late_pairs, grads)
    if fast:
        dq2, *states = tie(dq2, *out_state, *in_state)
        (out_state,), in_state = reduce_inward(states[:3]), reduce_second(states[3:])
        dq2, out_state[0], in_state[0] = tie(dq2, out_state[0], in_state[0])
    dy_one, db, do, back_sums = cross_back(vec, dq2, dy, z_one, r_one, cross_w)
    if fast:
        operands = [h_one, dq2, mem, dk2, dv2, o, db]
        chunks = [(at, 0) for at in range(7)]
        items = [(0, 1, FACTOR), (2, 3, 1.0), (2, 4, 1.0), (5, 6, 1.0)]
        cross_state = reduce_core(
            *weight_grad(me, operands, chunks, items, "cross_grad", (back_sums, cross_sums), SLAB // 2)
        )
        do, *states = tie(do, *out_state, *in_state, cross_state[0])
        out_state, (in_state,), cross_state[0] = reduce_across(states[:2]), reduce_inward(states[2:5]), states[5]
        do, out_state[0], in_state[0] = tie(do, out_state[0], in_state[0])
    grads = attend_backward(q, k, v, o, do, lse, target_lengths, True, early_pairs)
    if fast:
        do, *states = tie(do, *grads, *out_state, *in_state, *cross_state)
        grads, out_state, in_state = states[:4], reduce_outward(states[4:6]), reduce_across(states[6:8])
        cross_state = reduce_first(states[8:])
        do, out_state[0], in_state[0], cross_state[0] = tie(do, out_state[0], in_state[0], cross_state[0])
    dq, dk, dv, self_sums = attend_backward(q, k, v, o, do, lse, target_lengths, True, late_pairs, grads)
    if fast:
        dq, *states = tie(dq, *in_state, *cross_state, *out_state)
        in_state, cross_state, out_state = reduce_outward(states[:2]), reduce_second(states[2:7]), states[7:]
        dq, in_state[0], cross_state[0] = tie(dq, in_state[0], cross_state[0])
        chunks = [(at, 0) for at in range(4)]
        items = [(0, 1, FACTOR), (0, 2, 1.0), (0, 3, 1.0)]
        keep, send = weight_grad(me, [x, dq, dk, dv], chunks, items, "self_grad", (self_sums,), SLAB)
        send, *cross_state = tie(send, *cross_state)
        self_state = reduce_core(keep, send)
        first, second = reduce_inward(cross_state, 2)
        *self_state, first[0], second[0] = tie(*self_state, first[0], second[0])
        self_state = reduce_first(self_state)
        dq, self_state[0] = tie(dq, self_state[0])
    d_target = self_back(dq, dk, dv, dy_one, self_w)
    if fast:
        d_target, *states = tie(d_target, *self_state, *in_state)
        self_state, in_state = states[:5], states[5:]
        self_state = reduce_second(self_state)
        self_state[0], *states = tie(self_state[0], *first, *second)
        first, second = reduce_across(states[:2]), reduce_across(states[2:])
        *self_state, first[0], second[0] = tie(*self_state, first[0], second[0])
        one, two = reduce_inward(self_state, 2)
        one[0], two[0], *states = tie(one[0], two[0], *first, *second)
        first, second = reduce_outward(states[:2]), reduce_outward(states[2:])
        *one, first[0], second[0] = tie(*one, first[0], second[0])
        one = reduce_across(one)
        *two, one[0] = tie(*two, one[0])
        two = reduce_across(two)
        dk2, one[0], two[0] = tie(dk2, one[0], two[0])
    d_memory = memory_back(dk2, dv2, cross_w)

    if fast:
        f32 = dict(dtype=F32)
        d_memory, *one = tie(d_memory, *one)
        one = reduce_outward(one)
        *two, one[0] = tie(*two, one[0])
        two = reduce_outward(two)
        two[0], *states = tie(two[0], *out_state, *in_state, *first, *second)
        out_state, in_state, first, second = states[:2], states[2:4], states[4:6], states[6:]
        (out_sum,) = reduce_end(out_state, wide, [(0, wide, 1)], [of(wide, width, **f32)])
        in_sum, cross_o_sum, early = reduce_end(
            in_state, in_state[0].shape[0], [(0, part, ratio), (wide, part, 1), (wide + part, SLAB // 2, 1)],
            [of(part, hidden, **f32), of(part, width, **f32), of(SLAB // 2, width, **f32)],
        )
        cross_w_sum, self_o_sum, back = reduce_end(
            first + second, first[0].shape[0] + second[0].shape[0],
            [(0, 0, 0), (3 * part, part, 1), (4 * part, SLAB // 2, 1)],
            [of(3, part, width, **f32), of(part, width, **f32), of(SLAB // 2, width, **f32)],
        )
        self_w_sum, late = reduce_end(
            one + two, one[0].shape[0] + two[0].shape[0], [(0, 0, 0), (3 * part, SLAB, 1)],
            [of(3, part, width, **f32), of(SLAB, width, **f32)],
        )
        shapes = [of(3, part, **f32)] * 4 + [of(1, wide, **f32), of(1, part, **f32)]
        self_b, cross_b, gain, shift, b_in, b_out = local(small_kernel, "small_grads", shapes, me, early, back, late, scalars=1)
        b_in, b_out = b_in[0], b_out[0]
    else:
        def whole(left, right, scale=1.0):
            return reduce_plain(sizes, (dot_tn(left, right) * scale).reshape(n, left.shape[1] // n, right.shape[1]))

        def mine(rows, size):
            rows = rows.reshape(-1, n * size)
            return lax.dynamic_slice(rows, (0, place * size), (rows.shape[0], size))

        self_w_sum = jnp.stack([whole(x, dq, FACTOR), whole(x, dk), whole(x, dv)])
        cross_w_sum = jnp.stack([whole(h_one, dq2, FACTOR), whole(mem, dk2), whole(mem, dv2)])
        cross_o_sum, self_o_sum = whole(o2, db2), whole(o, db)
        in_sum, out_sum = whole(h_two, da), whole(act, df)
        sums = lax.psum(jnp.concatenate([ffn_sums, back_sums, cross_sums, self_sums]), ("fsdp", "dp"))
        narrow = mine(sums, part)
        self_b = jnp.stack([narrow[32], narrow[33], narrow[18]])
        cross_b = jnp.stack([narrow[24], narrow[25], narrow[5]])
        gain = jnp.stack([narrow[16], narrow[3], narrow[1]])
        shift = jnp.stack([narrow[17], narrow[4], narrow[2]])
        b_in, b_out = mine(sums[6:10], wide)[0], narrow[0]
    return (
        mixed[None], d_target[None], d_memory[None], self_w_sum, self_b, self_o_sum, cross_w_sum, cross_b, cross_o_sum,
        in_sum, b_in, out_sum, b_out, gain, shift,
    )


def solution(mesh):
    rows = P(("fsdp", "dp"), None, None)
    row = P(("fsdp", "dp"))
    stacked, vectors, matrix, vector = P(None, "fsdp", None), P(None, "fsdp"), P("fsdp", None), P("fsdp")
    weights = (stacked, vectors, matrix, stacked, vectors, matrix, matrix, vector, matrix, vector, vectors, vectors)
    sizes = (mesh.shape["fsdp"], mesh.shape["dp"])
    return jax.shard_map(
        lambda *args: shards(sizes, *args),
        mesh=mesh,
        in_specs=(rows, rows, row, row) + weights + (rows,),
        out_specs=(rows, rows, rows) + weights,
        check_vma=False,
    )
```
